32 devices in a mesh: groups: 2 (over y), dp: 4 (over z), mp: 4 (over x, core).
Axes of the slice: x: 2, y: 2, z: 4, core: 2. Of those that a mesh axis runs over, the one named last changes fastest.
Arguments:
- tokens: bfloat16 [16384, 2048], P(('groups', 'dp'), 'mp'), parts along dimension 0, may hold values from -6 to 6
- x_weight: bfloat16 [2048, 2048], P(None, 'mp'), may hold values from -0.125 to 0.125
- z_weight: bfloat16 [2048, 2048], P(None, 'mp'), may hold values from -0.125 to 0.125
- bc_weight: bfloat16 [2048, 512], P(None, 'mp'), may hold values from -0.125 to 0.125
- dt_weight: bfloat16 [2048, 32], P(None, 'mp'), may hold values from -0.125 to 0.125
- dt_bias: float32 [32], P('mp'), may hold values from -3 to 1
- decay_rate: float32 [32], P('mp'), may hold values from 0.003 to 0.03
- norm_gain: float32 [2048], P('mp'), may hold values from 0.1 to 1.9
- out_weight: bfloat16 [2048, 2048], P('mp'), may hold values from -0.125 to 0.125
- store_states: bfloat16 [128, 131072], P(('groups', 'dp'), 'mp'), parts along dimension 0, may hold values from -6 to 6
- home_rows: int32 [128], P('groups'), parts along dimension 0, may hold values from 0 to 63, as said below
- event_counts: int32 [128], P(('groups', 'dp')), parts along dimension 0, may hold values from 1 to 128, as said below
Outputs:
- out_tokens: bfloat16 [16384, 2048], P(('groups', 'dp', 'mp')), parts along dimension 0
- new_store: bfloat16 [128, 131072], P(('groups', 'dp'), 'mp'), parts along dimension 0
The draws below stay inside these ranges and needn't reach their ends.
There are 2 independent parts, one for each index of `groups`. The reference program is written for one: setup_inputs(seed, part) draws one part's arguments, and reference() takes and returns one part's arrays. A program takes and returns all parts, laid end to end along the dimension named above; an argument that names none is the same for every part. Nothing has to cross between parts.
Inputs may be any that keep to these rules, and one draw needn't show every extreme that they name: A permutation: session r's state is row home_rows[r] of the store. The 16 sessions of one aligned block keep at most 4 states in one aligned block of 16 store rows, and every block of sessions reaches 4 in some block of rows. `event_counts`: event slots at or after a session's count are padding.
All inputs are finite; a program needn't handle non-finite values.
Results may differ from the reference program's by a relative error of at most 0.02.
Values may be sent and summed in bfloat16 or wider, within the bound.
No kernel may reach another device: no remote copies, remote signals or barrier semaphores. Data moves between devices by JAX's collectives and lax.ppermute only.
A program may use at most 128 MiB of HBM per device.

```python
import math
import jax
import jax.numpy as jnp
from jax import lax

D = 2048
HEADS = 32
HEADDIM = 64
NSTATE = 64
GROUPS = 4
SPAN = 128
SES_DEV = 16
SESSIONS = 64
CAP = 4
INNER = 2048
N_DP = 4


def draw_home_rows(key, part):
    key_perm, key_fill, key_servers, key_store, key_place = jax.random.split(key, 5)
    lowest = max(1, (SES_DEV - N_DP + CAP - 2) // (CAP - 1))
    highest = SES_DEV // CAP
    full_pairs = jax.random.randint(key_fill, (), lowest, highest + 1)
    shard_order = jax.random.permutation(key_perm, N_DP)
    position = jnp.arange(SES_DEV, dtype=jnp.int32)
    paired = jnp.minimum(position // CAP, N_DP - 1)
    single = jnp.clip(full_pairs + position - full_pairs * CAP, 0, N_DP - 1)
    offset = shard_order[jnp.where(position < full_pairs * CAP, paired, single)]
    server_shift = jax.random.permutation(key_servers, N_DP)
    store_rotate = jax.random.randint(key_store, (N_DP,), 0, SES_DEV)
    place_rotate = jax.random.randint(key_place, (N_DP,), 0, SES_DEV)
    server = jnp.arange(N_DP, dtype=jnp.int32)[:, None]
    shard = (server_shift[server] + offset[None, :]) % N_DP
    slot = (position[None, :] + store_rotate[shard]) % SES_DEV
    place = (position[None, :] + place_rotate[server]) % SES_DEV
    target = (server * SES_DEV + place).reshape(-1)
    values = (shard * SES_DEV + slot).reshape(-1).astype(jnp.int32)
    return jnp.zeros((N_DP * SES_DEV,), jnp.int32).at[target].set(values)


def draw_event_counts(key, part):
    key_values, key_top, key_low = jax.random.split(key, 3)
    counts = jax.random.randint(key_values, (SESSIONS,), 1, SPAN + 1)
    top_index = jax.random.randint(key_top, (), 0, SESSIONS)
    low_index = (top_index + 1 + jax.random.randint(key_low, (), 0, SESSIONS - 1)) % SESSIONS
    counts = counts.at[top_index].set(SPAN)
    counts = counts.at[low_index].set(1)
    return counts.astype(jnp.int32)


def levels(own_key, dims, cuts, smallest, largest):
    def one(dim, parts):
        heights = jax.random.uniform(jax.random.fold_in(jax.random.fold_in(own_key, 6), dim), (parts,), jnp.float32, smallest / len(cuts), largest / len(cuts))
        return jnp.repeat(jnp.exp(heights), dims[dim] // parts).reshape((-1,) + (1,) * (len(dims) - dim - 1))

    factor_of = one(*cuts[0])
    for cut in cuts[1:]:
        factor_of = factor_of * one(*cut)
    return factor_of


def noise(rng, extent, width, bound, shards=(), kind=jnp.bfloat16):
    gain = levels(rng, extent, shards, -0.22, 0.18) if shards else 1.0
    result = jax.random.normal(rng, extent, jnp.float32) * width * gain
    return jnp.minimum(jnp.maximum(result, -bound), bound).astype(kind)


def setup_inputs(seed: int = 0, part: int = 0) -> dict:
    key_of = jax.random.split(jax.random.key(seed), 13)
    part_splits = jax.random.split(jax.random.fold_in(key_of[12], part), 13)
    tokens = noise(part_splits[0], (SESSIONS * SPAN, D), 1.0, 6.0, ((0, 4), (1, 4)))
    x_weight = noise(key_of[1], (D, INNER), D ** -0.5, 0.125, ((1, 4),))
    z_weight = noise(key_of[2], (D, INNER), D ** -0.5, 0.125, ((1, 4),))
    bc_weight = noise(key_of[3], (D, GROUPS * 2 * NSTATE), D ** -0.5, 0.125, ((1, 4),))
    dt_weight = noise(key_of[4], (D, HEADS), D ** -0.5, 0.125, ((1, 4),))
    dt_bias = jnp.clip(-3.0 + 4.0 * jax.random.uniform(key_of[5], (HEADS,), jnp.float32) ** levels(key_of[5], (HEADS,), ((0, 4),), -0.2, 0.2), -3.0, 1.0)
    decay_rate = jnp.clip(jnp.exp(math.log(0.03) - 2.3025851 * jax.random.uniform(key_of[6], (HEADS,), jnp.float32) ** levels(key_of[6], (HEADS,), ((0, 4),), -0.2, 0.2)), 0.003, 0.03)
    norm_gain = jnp.clip(1.0 + 0.18 * jax.random.normal(key_of[7], (INNER,), jnp.float32), 0.1, 1.9)
    out_weight = noise(key_of[8], (INNER, D), INNER ** -0.5, 0.125, ((0, 4),))
    store_states = noise(part_splits[9], (SESSIONS, HEADS * HEADDIM * NSTATE), 1.0, 6.0, ((0, 4), (1, 4)))
    home_rows = draw_home_rows(jax.random.fold_in(jax.random.fold_in(key_of[12], part), 71), part)
    event_counts = draw_event_counts(jax.random.fold_in(jax.random.fold_in(key_of[12], part), 71), part)
    return dict(tokens=tokens, x_weight=x_weight, z_weight=z_weight, bc_weight=bc_weight, dt_weight=dt_weight, dt_bias=dt_bias, decay_rate=decay_rate, norm_gain=norm_gain, out_weight=out_weight, store_states=store_states, home_rows=home_rows, event_counts=event_counts)


def rounded(values):
    return lax.optimization_barrier(values.astype(jnp.bfloat16)).astype(jnp.float32)

def group_scan(inputs, b_matrix, c_matrix, step_sizes, decay_rates, initial_state):
    decay_sum = jnp.cumsum(step_sizes * decay_rates[None, None, :], axis=1)
    causal_mask = jnp.arange(SPAN)[:, None] >= jnp.arange(SPAN)[None, :]
    lagged = jnp.transpose(decay_sum, (0, 2, 1))
    decay_gaps = jnp.where(causal_mask, lagged[:, :, :, None] - lagged[:, :, None, :], 0.0)
    kernel = jnp.einsum('stn,sun->stu', c_matrix, b_matrix)
    step_rows = jnp.transpose(step_sizes, (0, 2, 1))
    mixing = rounded(jnp.where(causal_mask, jnp.exp(-decay_gaps), 0.0) * step_rows[:, :, None, :] * kernel[:, None, :, :])
    diagonal_part = jnp.einsum('shtu,suhp->sthp', mixing, inputs)
    carried = jnp.einsum('stn,shpn->sthp', c_matrix, initial_state) * jnp.exp(-decay_sum)[:, :, :, None]
    final_decay = decay_sum[:, -1:, :]
    weighted = rounded(b_matrix[:, :, None, :] * (jnp.exp(-(final_decay - decay_sum)) * step_sizes)[:, :, :, None])
    new_state = jnp.exp(-final_decay[:, 0, :])[:, :, None, None] * initial_state + jnp.einsum('suhp,suhn->shpn', inputs, weighted)
    return (diagonal_part + carried, new_state)

def reference(tokens, x_weight, z_weight, bc_weight, dt_weight, dt_bias, decay_rate, norm_gain, out_weight, store_states, home_rows, event_counts):
    group_heads = HEADS // GROUPS
    group_width = group_heads * HEADDIM

    def one_block(block_index):
        first_row = (block_index * SES_DEV).astype(jnp.int32)
        token_rows = lax.dynamic_slice_in_dim(tokens, (first_row * SPAN).astype(jnp.int32), SES_DEV * SPAN, 0)
        wanted = lax.dynamic_slice_in_dim(home_rows, first_row, SES_DEV, 0)
        counts = lax.dynamic_slice_in_dim(event_counts, first_row, SES_DEV, 0)
        initial_all = jnp.take(store_states, wanted, axis=0).astype(jnp.float32).reshape(SES_DEV, HEADS, HEADDIM, NSTATE)
        inputs_all = rounded(jnp.dot(token_rows, x_weight, preferred_element_type=jnp.float32)).reshape(SES_DEV, SPAN, HEADS, HEADDIM)
        gate_values = rounded(jnp.dot(token_rows, z_weight, preferred_element_type=jnp.float32)).reshape(SES_DEV, SPAN, INNER)
        bc_values = rounded(jnp.dot(token_rows, bc_weight, preferred_element_type=jnp.float32)).reshape(SES_DEV, SPAN, GROUPS, 2, NSTATE)
        valid_mask = (jnp.arange(SPAN, dtype=jnp.int32)[None, :] < counts[:, None]).astype(jnp.float32)
        raw_steps = jnp.dot(token_rows, dt_weight, preferred_element_type=jnp.float32).reshape(SES_DEV, SPAN, HEADS)
        step_sizes = jax.nn.softplus(raw_steps + dt_bias[None, None, :]) * valid_mask[:, :, None]
        pieces_out = []
        pieces_state = []
        for group_index in range(GROUPS):
            head_range = slice(group_index * group_heads, (group_index + 1) * group_heads)
            outputs, new_state = group_scan(inputs_all[:, :, head_range], bc_values[:, :, group_index, 0], bc_values[:, :, group_index, 1], step_sizes[:, :, head_range], decay_rate[head_range], initial_all[:, head_range])
            channel_range = slice(group_index * group_width, (group_index + 1) * group_width)
            gated_values = outputs.reshape(SES_DEV, SPAN, group_width) * jax.nn.silu(gate_values[:, :, channel_range])
            inverse_rms = lax.rsqrt(lax.optimization_barrier(jnp.mean(gated_values * gated_values, axis=2, keepdims=True)) + 1e-05)
            pieces_out.append(gated_values * inverse_rms * norm_gain[channel_range][None, None, :] * valid_mask[:, :, None])
            pieces_state.append(new_state)
        normed = jnp.concatenate(pieces_out, axis=2).reshape(SES_DEV * SPAN, INNER).astype(jnp.bfloat16)
        out_block = jnp.dot(normed, out_weight, preferred_element_type=jnp.float32).astype(jnp.bfloat16)
        states_block = jnp.concatenate(pieces_state, axis=1).astype(jnp.bfloat16).reshape(SES_DEV, HEADS * HEADDIM * NSTATE)
        return (out_block, states_block)
    out_blocks, state_blocks = lax.map(one_block, jnp.arange(SESSIONS // SES_DEV, dtype=jnp.int32))
    out_tokens = out_blocks.reshape(SESSIONS * SPAN, D)
    new_store = jnp.zeros_like(store_states).at[home_rows].set(state_blocks.reshape(SESSIONS, HEADS * HEADDIM * NSTATE))
    return (out_tokens, new_store)
```

```python
import functools

import jax
import jax.numpy as jnp
from jax import lax
from jax.experimental import pallas as pl
from jax.experimental.pallas import tpu as pltpu
from jax.sharding import PartitionSpec as P

BF = jnp.bfloat16
F32 = jnp.float32


def pack_rows(values, wanted, slot_count):
    slots = jnp.arange(slot_count, dtype=jnp.int32)
    chosen = wanted[None, :] == slots[:, None]
    places = jnp.arange(wanted.shape[0], dtype=jnp.int32)
    source = jnp.sum(chosen.astype(jnp.int32) * places[None, :], axis=1)
    return jnp.take(values, source, axis=0)


def rank_within(keys, order):
    earlier = (keys[None, :] == keys[:, None]) & (order[None, :] < order[:, None])
    return jnp.sum(earlier.astype(jnp.int32), axis=1)


def layer_kernel(
    heads, span, me_ref, slot_ref, count_ref, t0, t1, t2, t3, xw, zw, bw, bias, rate, gain, states,
    n0, n1, n2, n3, new_states, xs, zs, bcs,
):
    me = me_ref[0]
    pieces = (t0, t1, t2, t3)
    normed_out = (n0, n1, n2, n3)
    depth = t0.shape[1]
    quads = heads // 4

    def project(weight, columns):
        total = None
        for distance in range(4):
            first = pl.multiple_of((me ^ distance) * depth, depth)
            part = jnp.dot(
                pieces[distance][...],
                weight[pl.ds(first, depth), columns],
                preferred_element_type=F32,
            )
            total = part if total is None else total + part
        return total

    bcs[...] = project(bw, slice(None))
    for quad in range(quads):
        columns = slice(quad * 256, quad * 256 + 256)
        xs[:, columns] = project(xw, columns).astype(BF)
        zs[:, columns] = project(zw, columns).astype(BF)

    lane = lax.broadcasted_iota(jnp.int32, (span, 128), 1)
    row = lax.broadcasted_iota(jnp.int32, (span, 128), 0)
    low = lane < 64
    causal = row >= lane
    lane8 = lax.broadcasted_iota(jnp.int32, (heads, span), 1)
    head_mask = [((lane // 32) == k).astype(F32).astype(BF) for k in range(4)]
    head_masks = [jnp.concatenate([m, m], axis=1) for m in head_mask]

    for distance in range(4):
        place = me ^ distance
        first = pl.multiple_of(place * span, span)
        rows = pl.ds(first, span)
        count = count_ref[place]
        bc = bcs[rows, 0:128]
        turned = pltpu.roll(bc, 64, 1)
        bc_low = jnp.where(low, bc, 0.0).astype(BF)
        bc_high = jnp.where(low, 0.0, turned).astype(BF)
        c_low = jnp.where(low, turned, 0.0).astype(BF)
        c_high = jnp.where(low, 0.0, bc).astype(BF)
        scores = lax.dot_general(
            c_low, bc_low, (((1,), (1,)), ((), ())), preferred_element_type=F32
        )
        scores = jnp.where(causal, scores, 0.0)
        raw = jnp.transpose(bcs[rows, 128:256])[:heads] + bias[...]
        soft = jnp.maximum(raw, 0.0) + jnp.log1p(jnp.exp(-jnp.abs(raw)))
        step = jnp.where(lane8 < count, soft, 0.0)
        total = step * rate[...]
        shift = 1
        while shift < span:
            total = total + jnp.where(lane8 >= shift, pltpu.roll(total, shift, 1), 0.0)
            shift *= 2
        last = total[:, span - 1 : span]
        weights = jnp.exp(jnp.minimum(total - last, 0.0)) * step
        kept = jnp.exp(-last)
        cum = jnp.transpose(jnp.concatenate([total, jnp.zeros((128 - heads, span), F32)], axis=0))
        state = states[slot_ref[place]]
        carried = lax.dot_general(
            jnp.concatenate([c_low, c_high], axis=0),
            state,
            (((1,), (1,)), ((), ())),
            preferred_element_type=F32,
        )
        b_both = jnp.concatenate([bc_low, bc_high], axis=0)
        gated = []
        squares = None
        for quad in range(quads):
            columns = slice(quad * 256, quad * 256 + 256)
            x = xs[rows, columns]
            mixes = []
            blocks = []
            spread = None
            for k in range(4):
                head = quad * 4 + k
                level = jnp.broadcast_to(cum[:, head : head + 1], (span, 128))
                gap = jnp.minimum(total[head : head + 1, :] - level, 0.0)
                mixes.append((jnp.exp(gap) * step[head : head + 1, :] * scores).astype(BF))
                blocks.append(x * head_masks[k])
                spread = level if spread is None else jnp.where(lane >= 32 * k, level, spread)
            diagonal = jnp.dot(
                jnp.concatenate(mixes, axis=1),
                jnp.concatenate(blocks, axis=0),
                preferred_element_type=F32,
            )
            fade = jnp.exp(-spread)
            part = slice(quad * 128, quad * 128 + 128)
            before = jnp.concatenate(
                [carried[:span, part] * fade, carried[span:, part] * fade], axis=1
            )
            gate = zs[rows, columns].astype(F32)
            value = (diagonal + before) * (gate / (1.0 + jnp.exp(-gate)))
            gated.append(value)
            own = jnp.sum(value * value, axis=1, keepdims=True)
            squares = own if squares is None else squares + own
            weight_rows = jnp.concatenate(
                [
                    jnp.broadcast_to(weights[quad * 4 + k : quad * 4 + k + 1, :], (32, span))
                    for k in range(4)
                ],
                axis=0,
            )
            xf = x.astype(F32)
            even = (jnp.transpose(xf[:, :128]) * weight_rows).astype(BF)
            odd = (jnp.transpose(xf[:, 128:]) * weight_rows).astype(BF)
            added = jnp.dot(
                jnp.concatenate([even, odd], axis=1), b_both, preferred_element_type=F32
            )
            keep_rows = jnp.concatenate(
                [
                    jnp.broadcast_to(kept[quad * 4 + k : quad * 4 + k + 1, :], (32, 128))
                    for k in range(4)
                ],
                axis=0,
            )
            new_states[place, quad * 128 : quad * 128 + 128, :] = (
                keep_rows * state[quad * 128 : quad * 128 + 128].astype(F32) + added
            ).astype(BF)
        inverse = lax.rsqrt(squares * (1.0 / (heads * 64)) + 1e-05)
        inverse = jnp.where(row[:, :1] < count, inverse, 0.0)
        for quad in range(quads):
            columns = slice(quad * 256, quad * 256 + 256)
            normed_out[distance][:, columns] = (
                gated[quad] * inverse * gain[:, columns]
            ).astype(BF)


def layer_call(me, slots, counts, pieces, weights, small, states):
    rows, depth = pieces[0].shape
    heads = small[0].shape[0]
    width = weights[0].shape[1]
    span = rows // 4
    vmem = pl.BlockSpec(memory_space=pltpu.VMEM)
    smem = pl.BlockSpec(memory_space=pltpu.SMEM)
    return pl.pallas_call(
        functools.partial(layer_kernel, heads, span),
        out_shape=[jax.ShapeDtypeStruct((span, width), BF)] * 4
        + [jax.ShapeDtypeStruct((4,) + states.shape[1:], BF)],
        in_specs=[smem] * 3 + [vmem] * 11,
        out_specs=[vmem] * 5,
        scratch_shapes=[
            pltpu.VMEM((rows, width), BF),
            pltpu.VMEM((rows, width), BF),
            pltpu.VMEM((rows, weights[2].shape[1]), F32),
        ],
        compiler_params=pltpu.CompilerParams(vmem_limit_bytes=40 * 2**20),
        cost_estimate=pl.CostEstimate(
            flops=2 * rows * depth * 4 * 1280, bytes_accessed=9 * 2**20, transcendentals=0
        ),
        name="layer",
    )(me, slots, counts, *pieces, *weights, *small, states)


def out_kernel(chunks, *refs):
    weights = refs[chunks * 4 : chunks * 4 + 4]
    out = refs[-1]
    span = refs[0].shape[0]
    for chunk in range(chunks):
        total = None
        for distance in range(4):
            part = jnp.dot(
                refs[chunk * 4 + distance][...],
                weights[distance][...],
                preferred_element_type=F32,
            )
            total = part if total is None else total + part
        out[chunk * span : (chunk + 1) * span, :] = total.astype(BF)


def out_call(normed, weights):
    chunks = len(normed)
    span, depth = normed[0][0].shape
    columns = weights[0].shape[1]
    block = 512
    return pl.pallas_call(
        functools.partial(out_kernel, chunks),
        grid=(columns // block,),
        out_shape=jax.ShapeDtypeStruct((chunks * span, columns), BF),
        in_specs=[pl.BlockSpec((span, depth), lambda j: (0, 0))] * (chunks * 4)
        + [pl.BlockSpec((depth, block), lambda j: (0, j))] * 4,
        out_specs=pl.BlockSpec((chunks * span, block), lambda j: (0, j)),
        compiler_params=pltpu.CompilerParams(vmem_limit_bytes=32 * 2**20),
        cost_estimate=pl.CostEstimate(
            flops=2 * chunks * span * depth * 4 * columns,
            bytes_accessed=12 * 2**20,
            transcendentals=0,
        ),
        name="project_out",
    )(*[piece for chunk in normed for piece in chunk], *weights)


def body(
    tokens,
    x_weight,
    z_weight,
    bc_weight,
    dt_weight,
    dt_bias,
    decay_rate,
    norm_gain,
    out_weight,
    store_states,
    home_rows,
    event_counts,
):
    shard_count = lax.axis_size("dp")
    model_shards = lax.axis_size("mp")
    store_index = lax.axis_index("dp")
    me = lax.axis_index("mp")
    sessions_here, state_width = store_states.shape
    capacity = max(2, (sessions_here + shard_count - 1) // shard_count)
    slot_count = shard_count * capacity
    heads = dt_bias.shape[0]
    width = x_weight.shape[1]
    depth = tokens.shape[1]
    span = tokens.shape[0] // sessions_here
    chunks = sessions_here // model_shards

    def exchange(value, distance):
        pairs = [(j, j ^ distance) for j in range(model_shards)]
        return lax.ppermute(value, "mp", pairs)

    by_chunk = tokens.reshape(model_shards, chunks, span, depth)
    own = [by_chunk[:, c].reshape(model_shards * span, depth) for c in range(chunks)]
    across = [exchange(own[c], 2) for c in range(chunks)]
    sibling = [exchange(own[c], 1) for c in range(chunks)]
    far = [exchange(across[c], 1) for c in range(chunks)]

    positions = jnp.arange(sessions_here, dtype=jnp.int32)
    store_rows = store_index * sessions_here + positions
    everyone = jnp.arange(home_rows.shape[0], dtype=jnp.int32)
    owner = jnp.sum(
        (home_rows[None, :] == store_rows[:, None]).astype(jnp.int32) * everyone[None, :], axis=1
    )
    server = owner // sessions_here
    row_slot = server * capacity + rank_within(server, positions)
    outbound = pack_rows(store_states, row_slot, slot_count).reshape(
        shard_count, capacity, state_width // 128, 128
    )
    inbound = lax.all_to_all(outbound, "dp", split_axis=0, concat_axis=0, tiled=True).reshape(
        slot_count, state_width // 128, 128
    )
    wanted = lax.dynamic_slice_in_dim(home_rows, store_index * sessions_here, sessions_here)
    home_shard = wanted // sessions_here
    session_slot = home_shard * capacity + rank_within(home_shard, wanted % sessions_here)

    new_column = jnp.arange(width, dtype=jnp.int32)
    quad, parity, k, pair = (
        new_column // 256,
        (new_column // 128) % 2,
        (new_column // 32) % 4,
        new_column % 32,
    )
    old_column = (quad * 4 + k) * 64 + pair * 2 + parity
    order = (old_column[None, :] == jnp.arange(width, dtype=jnp.int32)[:, None]).astype(BF)
    xw = jnp.dot(x_weight, order, preferred_element_type=F32).astype(BF)
    zw = jnp.dot(z_weight, order, preferred_element_type=F32).astype(BF)
    ow = jnp.dot(order.T, out_weight, preferred_element_type=F32).astype(BF)
    bw = jnp.concatenate(
        [bc_weight, dt_weight, jnp.zeros((bc_weight.shape[0], 128 - heads), BF)], axis=1
    )
    gain = (
        norm_gain.reshape(heads // 4, 4, 32, 2).transpose(0, 3, 1, 2).reshape(1, width)
    )

    replicas = lax.axis_size("groups") * shard_count
    replica = lax.axis_index("groups") * shard_count + store_index
    share = width // replicas
    ow_part = exchange(lax.dynamic_slice_in_dim(ow, replica * share, share), 2)
    ow_across = lax.all_gather(ow_part, ("groups", "dp"), axis=0, tiled=True)
    ow_sibling = exchange(ow, 1)
    ow_far = exchange(ow_across, 1)

    small = (dt_bias.reshape(heads, 1), decay_rate.reshape(heads, 1), gain)
    slots = session_slot.reshape(model_shards, chunks)
    counts = event_counts.reshape(model_shards, chunks)
    mine = me.reshape(1).astype(jnp.int32)
    normed = []
    states = []
    for c in range(chunks):
        *parts, new_states = layer_call(
            mine,
            slots[:, c],
            counts[:, c],
            (own[c], sibling[c], across[c], far[c]),
            (xw, zw, bw),
            small,
            inbound,
        )
        normed.append([parts[0]] + [exchange(parts[d], d) for d in range(1, 4)])
        states.append(new_states)
    new_state = jnp.stack(states, axis=1).reshape(sessions_here, state_width // 128, 128)
    outgoing = pack_rows(new_state, session_slot, slot_count).reshape(
        shard_count, capacity, state_width // 128, 128
    )
    returned = lax.all_to_all(outgoing, "dp", split_axis=0, concat_axis=0, tiled=True).reshape(
        slot_count, state_width // 128, 128
    )
    new_store = jnp.take(returned, row_slot, axis=0).reshape(sessions_here, state_width)
    out_tokens = out_call(normed, (ow, ow_sibling, ow_across, ow_far))
    return (out_tokens, new_store)


def solution(mesh):
    return jax.shard_map(
        body,
        mesh=mesh,
        in_specs=(
            P(("groups", "dp"), "mp"),
            P(None, "mp"),
            P(None, "mp"),
            P(None, "mp"),
            P(None, "mp"),
            P("mp"),
            P("mp"),
            P("mp"),
            P("mp", None),
            P(("groups", "dp"), "mp"),
            P("groups"),
            P(("groups", "dp")),
        ),
        out_specs=(P(("groups", "dp", "mp"), None), P(("groups", "dp"), "mp")),
        check_vma=False,
    )
```

```python
import functools

import jax
import jax.numpy as jnp
import numpy as np
from jax import lax
from jax.experimental import pallas as pl
from jax.experimental.pallas import tpu as pltpu
from jax.sharding import PartitionSpec as P

BF = jnp.bfloat16
F32 = jnp.float32


def pick(values, index):
    chosen = index[..., None] == jnp.arange(values.shape[0], dtype=jnp.int32)
    return jnp.sum(jnp.where(chosen, values, 0), axis=-1, dtype=jnp.int32)


def count_before(same, order):
    earlier = order[None, :] < order[:, None]
    return jnp.sum((same & earlier).astype(jnp.int32), axis=1)


def split_sessions(home_rows, block, per_target):
    total = home_rows.shape[0]
    session = jnp.arange(total, dtype=jnp.int32)
    server = session // block
    shard = home_rows // block
    same_server = server[:, None] == server[None, :]
    same_pair = same_server & (shard[:, None] == shard[None, :])
    rank = count_before(same_pair, session)
    size = jnp.sum(same_pair.astype(jnp.int32), axis=1)
    single = (rank ^ 1) >= size
    both_single = same_server & single[:, None] & single[None, :]
    single_rank = count_before(both_single, session)
    partners = (same_pair & (rank[None, :] == (rank ^ 1)[:, None])) | (
        both_single & (single_rank[None, :] == (single_rank ^ 1)[:, None])
    )
    partner = jnp.sum(jnp.where(partners, session[None, :], 0), axis=1, dtype=jnp.int32)
    step = partner ^ 1
    lowest = session
    reach = 1
    while reach < block // 2:
        lowest = jnp.minimum(lowest, pick(lowest, step))
        step = pick(step, step)
        reach *= 2
    half = (lowest > pick(lowest, partner)).astype(jnp.int32)
    same_half = half[:, None] == half[None, :]
    target = session // per_target
    turn = count_before(same_half & (target[:, None] == target[None, :]), session)
    chunk = half * (per_target // 2) + turn
    place = count_before(same_half & same_pair, session)
    return server, shard, half, chunk, place


def layer_kernel(
    heads, span, meta, a0, a1, a2, a3, b0, b1, b2, b3, t2, t3, xw, zw, bw, bias, rate, gain, order,
    s0, s1, s2, s3, earlier, n0, n1, n2, n3, outgoing, xs, zs, bcs, fresh, sems,
):
    del earlier
    me = meta[12]
    states = (s0, s1, s2, s3)
    pieces = (
        jnp.concatenate([a0[...], a1[...], a2[...], a3[...]], axis=0),
        jnp.concatenate([b0[...], b1[...], b2[...], b3[...]], axis=0),
        t2[...],
        t3[...],
    )
    normed_out = (n0, n1, n2, n3)
    depth = t2.shape[1]
    quads = heads // 4

    def project(weight, columns):
        total = None
        for distance in range(4):
            first = pl.multiple_of((me ^ distance) * depth, depth)
            part = jnp.dot(
                pieces[distance],
                weight[pl.ds(first, depth), columns],
                preferred_element_type=F32,
            )
            total = part if total is None else total + part
        return total

    bcs[...] = project(bw, slice(None))
    for weight, rounded in ((xw, xs), (zw, zs)):
        natural = jnp.concatenate(
            [
                project(weight, slice(quad * 256, quad * 256 + 256)).astype(BF)
                for quad in range(quads)
            ],
            axis=1,
        )
        rounded[...] = jnp.dot(natural, order[...], preferred_element_type=F32).astype(BF)

    lane = lax.broadcasted_iota(jnp.int32, (span, 128), 1)
    row = lax.broadcasted_iota(jnp.int32, (span, 128), 0)
    low = lane < 64
    causal = row >= lane
    lane8 = lax.broadcasted_iota(jnp.int32, (heads, span), 1)
    head_mask = [((lane // 32) == k).astype(F32).astype(BF) for k in range(4)]
    head_masks = [jnp.concatenate([m, m], axis=1) for m in head_mask]

    sends = []
    for distance in range(4):
        place = me ^ distance
        first = pl.multiple_of(place * span, span)
        rows = pl.ds(first, span)
        count = meta[8 + place]
        bc = bcs[rows, 0:128]
        turned = pltpu.roll(bc, 64, 1)
        bc_low = jnp.where(low, bc, 0.0).astype(BF)
        bc_high = jnp.where(low, 0.0, turned).astype(BF)
        c_low = jnp.where(low, turned, 0.0).astype(BF)
        c_high = jnp.where(low, 0.0, bc).astype(BF)
        scores = lax.dot_general(
            c_low, bc_low, (((1,), (1,)), ((), ())), preferred_element_type=F32
        )
        scores = jnp.where(causal, scores, 0.0)
        raw = jnp.transpose(bcs[rows, 128:256])[:heads] + bias[...]
        soft = jnp.maximum(raw, 0.0) + jnp.log1p(jnp.exp(-jnp.abs(raw)))
        step = jnp.where(lane8 < count, soft, 0.0)
        total = step * rate[...]
        shift = 1
        while shift < span:
            total = total + jnp.where(lane8 >= shift, pltpu.roll(total, shift, 1), 0.0)
            shift *= 2
        last = total[:, span - 1 : span]
        weights = jnp.exp(jnp.minimum(total - last, 0.0)) * step
        kept = jnp.exp(-last)
        cum = jnp.transpose(jnp.concatenate([total, jnp.zeros((128 - heads, span), F32)], axis=0))
        state = states[distance][...]
        carried = lax.dot_general(
            jnp.concatenate([c_low, c_high], axis=0),
            state,
            (((1,), (1,)), ((), ())),
            preferred_element_type=F32,
        )
        b_both = jnp.concatenate([bc_low, bc_high], axis=0)
        gated = []
        squares = None
        for quad in range(quads):
            columns = slice(quad * 256, quad * 256 + 256)
            x = xs[rows, columns]
            mixes = []
            blocks = []
            spread = None
            for k in range(4):
                head = quad * 4 + k
                level = jnp.broadcast_to(cum[:, head : head + 1], (span, 128))
                gap = jnp.minimum(total[head : head + 1, :] - level, 0.0)
                mixes.append((jnp.exp(gap) * step[head : head + 1, :] * scores).astype(BF))
                blocks.append(x * head_masks[k])
                spread = level if spread is None else jnp.where(lane >= 32 * k, level, spread)
            diagonal = jnp.dot(
                jnp.concatenate(mixes, axis=1),
                jnp.concatenate(blocks, axis=0),
                preferred_element_type=F32,
            )
            fade = jnp.exp(-spread)
            part = slice(quad * 128, quad * 128 + 128)
            before = jnp.concatenate(
                [carried[:span, part] * fade, carried[span:, part] * fade], axis=1
            )
            gate = zs[rows, columns].astype(F32)
            value = (diagonal + before) * (gate / (1.0 + jnp.exp(-gate)))
            gated.append(value)
            own = jnp.sum(value * value, axis=1, keepdims=True)
            squares = own if squares is None else squares + own
            weight_rows = jnp.concatenate(
                [
                    jnp.broadcast_to(weights[quad * 4 + k : quad * 4 + k + 1, :], (32, span))
                    for k in range(4)
                ],
                axis=0,
            )
            xf = x.astype(F32)
            even = (jnp.transpose(xf[:, :128]) * weight_rows).astype(BF)
            odd = (jnp.transpose(xf[:, 128:]) * weight_rows).astype(BF)
            added = jnp.dot(
                jnp.concatenate([even, odd], axis=1), b_both, preferred_element_type=F32
            )
            keep_rows = jnp.concatenate(
                [
                    jnp.broadcast_to(kept[quad * 4 + k : quad * 4 + k + 1, :], (32, 128))
                    for k in range(4)
                ],
                axis=0,
            )
            fresh[distance, quad * 128 : quad * 128 + 128, :] = (
                keep_rows * state[quad * 128 : quad * 128 + 128].astype(F32) + added
            ).astype(BF)
        sends.append(
            pltpu.make_async_copy(
                fresh.at[distance], outgoing.at[meta[4 + place]], sems.at[distance]
            )
        )
        sends[-1].start()
        inverse = lax.rsqrt(squares * (1.0 / (heads * 64)) + 1e-05)
        inverse = jnp.where(row[:, :1] < count, inverse, 0.0)
        normed = jnp.concatenate(
            [
                (gated[quad] * inverse * gain[:, quad * 256 : quad * 256 + 256]).astype(BF)
                for quad in range(quads)
            ],
            axis=1,
        )
        normed_out[distance][...] = lax.dot_general(
            normed, order[...], (((1,), (1,)), ((), ())), preferred_element_type=F32
        ).astype(BF)
    for send in sends:
        send.wait()


def layer_call(meta, tokens, sibling, across, far, weights, small, inbound, earlier):
    rows, depth = across.shape
    heads = small[0].shape[0]
    width = weights[0].shape[1]
    span = rows // 4
    vmem = pl.BlockSpec(memory_space=pltpu.VMEM)

    def session_block(k):
        return pl.BlockSpec((None, span, depth), lambda i, meta: (meta[k], 0, 0))

    def state_block(distance):
        return pl.BlockSpec(
            (None,) + inbound.shape[1:], lambda i, meta: (meta[4 + (meta[12] ^ distance)], 0, 0)
        )

    sessions = [session_block(k) for k in range(4)]
    operands = [*[tokens] * 4, *[sibling] * 4, across, far, *weights, *small, *[inbound] * 4]
    aliases = {}
    if earlier is None:
        earlier = jnp.zeros((8, 128), BF)
    else:
        aliases = {len(operands) + 1: 4}
    return pl.pallas_call(
        functools.partial(layer_kernel, heads, span),
        out_shape=[jax.ShapeDtypeStruct((span, width), BF)] * 4
        + [jax.ShapeDtypeStruct(inbound.shape, BF)],
        grid_spec=pltpu.PrefetchScalarGridSpec(
            num_scalar_prefetch=1,
            grid=(1,),
            in_specs=sessions
            + sessions
            + [vmem] * 9
            + [state_block(k) for k in range(4)]
            + [pl.BlockSpec(memory_space=pl.ANY)],
            out_specs=[vmem] * 4 + [pl.BlockSpec(memory_space=pl.ANY)],
            scratch_shapes=[
                pltpu.VMEM((rows, width), BF),
                pltpu.VMEM((rows, width), BF),
                pltpu.VMEM((rows, weights[2].shape[1]), F32),
                pltpu.VMEM((4,) + inbound.shape[1:], BF),
                pltpu.SemaphoreType.DMA((4,)),
            ],
        ),
        input_output_aliases=aliases,
        compiler_params=pltpu.CompilerParams(vmem_limit_bytes=40 * 2**20),
        cost_estimate=pl.CostEstimate(
            flops=8 * 10**9, bytes_accessed=9 * 2**20, transcendentals=0
        ),
        name="layer",
    )(meta, *operands, earlier)


def out_kernel(chunks, at_ref, *refs):
    weights = refs[chunks * 4 : chunks * 4 + 4]
    out = refs[-1]
    span = refs[0].shape[0]
    for chunk in range(chunks):
        total = None
        for distance in range(4):
            part = jnp.dot(
                refs[chunk * 4 + distance][...],
                weights[distance][...],
                preferred_element_type=F32,
            )
            total = part if total is None else total + part
        out[pl.ds(pl.multiple_of(at_ref[chunk] * span, span), span), :] = total.astype(BF)


def out_call(at, normed, weights):
    chunks = len(normed)
    span, depth = normed[0][0].shape
    columns = weights[0].shape[1]
    block = 512
    return pl.pallas_call(
        functools.partial(out_kernel, chunks),
        grid=(columns // block,),
        out_shape=jax.ShapeDtypeStruct((chunks * span, columns), BF),
        in_specs=[pl.BlockSpec(memory_space=pltpu.SMEM)]
        + [pl.BlockSpec((span, depth), lambda j: (0, 0))] * (chunks * 4)
        + [pl.BlockSpec((depth, block), lambda j: (0, j))] * 4,
        out_specs=pl.BlockSpec((chunks * span, block), lambda j: (0, j)),
        compiler_params=pltpu.CompilerParams(vmem_limit_bytes=32 * 2**20),
        cost_estimate=pl.CostEstimate(
            flops=2 * chunks * span * depth * 4 * columns,
            bytes_accessed=12 * 2**20,
            transcendentals=0,
        ),
        name="project_out",
    )(at, *[piece for chunk in normed for piece in chunk], *weights)


def body(
    tokens,
    x_weight,
    z_weight,
    bc_weight,
    dt_weight,
    dt_bias,
    decay_rate,
    norm_gain,
    out_weight,
    store_states,
    home_rows,
    event_counts,
):
    shard_count = lax.axis_size("dp")
    model_shards = lax.axis_size("mp")
    shard_index = lax.axis_index("dp")
    me = lax.axis_index("mp")
    sessions_here, state_width = store_states.shape
    heads = dt_bias.shape[0]
    width = x_weight.shape[1]
    depth = tokens.shape[1]
    span = tokens.shape[0] // sessions_here
    chunks = sessions_here // model_shards
    capacity = max(2, (sessions_here + shard_count - 1) // shard_count)
    places = (capacity + 1) // 2
    slot_count = shard_count * places
    row_shape = (state_width // 128, 128)

    def exchange(value, distance):
        pairs = [(j, j ^ distance) for j in range(model_shards)]
        return lax.ppermute(value, "mp", pairs)

    def trade(value):
        return lax.all_to_all(
            value.reshape((shard_count, places) + row_shape),
            "dp",
            split_axis=0,
            concat_axis=0,
            tiled=True,
        ).reshape((slot_count,) + row_shape)

    replicas = lax.axis_size("groups") * shard_count
    replica = lax.axis_index("groups") * shard_count + shard_index
    share = width // replicas
    ow_part = exchange(lax.dynamic_slice_in_dim(out_weight, replica * share, share), 2)
    sibling = exchange(tokens, 1)

    server, shard, half, chunk, place = split_sessions(home_rows, sessions_here, chunks)
    local = jnp.arange(sessions_here, dtype=jnp.int32)
    mine = shard_index * sessions_here + local
    by_turn = (jnp.arange(chunks)[:, None, None] == pick(chunk, mine)) & (
        jnp.arange(model_shards)[None, :, None] == local // chunks
    )

    def arranged(values):
        return jnp.sum(jnp.where(by_turn, values, 0), axis=2, dtype=jnp.int32)

    turns = arranged(local)
    slots = arranged(pick(shard * places + place, mine))
    counts = arranged(event_counts)
    meta = jnp.concatenate(
        [turns, slots, counts, jnp.full((chunks, 4), me, jnp.int32)], axis=1
    )
    at = jnp.sum(
        jnp.where(jnp.arange(model_shards)[None, :] == me, turns - me * chunks, 0), axis=1
    )

    by_session = tokens.reshape(sessions_here, span, depth)
    own = [
        jnp.concatenate(
            [lax.dynamic_slice_in_dim(by_session, turns[c, j], 1) for j in range(model_shards)]
        ).reshape(model_shards * span, depth)
        for c in range(chunks)
    ]
    across = [exchange(own[c], 2) for c in range(chunks)]

    store_row = home_rows - shard_index * sessions_here
    here = shard == shard_index
    there = server * places + place
    wanted = jnp.arange(slot_count, dtype=jnp.int32)
    kept = store_states.reshape((sessions_here,) + row_shape)
    inbound = []
    for k in range(2):
        chosen = (wanted[:, None] == there[None, :]) & (here & (half == k))[None, :]
        source = jnp.sum(jnp.where(chosen, store_row[None, :], 0), axis=1)
        inbound.append(trade(jnp.take(kept, source, axis=0, mode="clip")))
    owned = here[None, :] & (store_row[None, :] == local[:, None])
    came_back = jnp.sum(jnp.where(owned, half * slot_count + there, 0), axis=1)

    new_column = np.arange(width)
    old_column = (
        (new_column // 256 * 4 + new_column // 32 % 4) * 64
        + new_column % 32 * 2
        + new_column // 128 % 2
    )
    order = jnp.asarray(old_column[None, :] == np.arange(width)[:, None], BF)
    bw = jnp.concatenate(
        [bc_weight, dt_weight, jnp.zeros((bc_weight.shape[0], 128 - heads), BF)], axis=1
    )
    gain = norm_gain.reshape(heads // 4, 4, 32, 2).transpose(0, 3, 1, 2).reshape(1, width)

    ow_across = lax.all_gather(ow_part, ("groups", "dp"), axis=0, tiled=True)
    ow_sibling = exchange(out_weight, 1)
    ow_far = exchange(ow_across, 1)

    small = (dt_bias.reshape(heads, 1), decay_rate.reshape(heads, 1), gain, order)
    normed = []
    returned = []
    earlier = None
    sibling = sibling.reshape(sessions_here, span, depth)
    for c in range(chunks):
        turn = meta[c]
        arrived = across[c]
        if c >= 2:
            arrived, _ = lax.optimization_barrier((arrived, normed[c - 2][0]))
            turn, _ = lax.optimization_barrier((turn, normed[c - 2]))
        if c >= 1:
            turn, _ = lax.optimization_barrier((turn, normed[c - 1][0]))
        far = exchange(arrived, 1)
        *parts, outgoing = layer_call(
            turn,
            by_session,
            sibling,
            arrived,
            far,
            (x_weight, z_weight, bw),
            small,
            inbound[c * 2 // chunks],
            earlier,
        )
        earlier = outgoing
        if (c + 1) % (chunks // 2) == 0:
            returned.append(trade(outgoing))
            earlier = None
        normed.append([parts[0]] + [exchange(parts[d], d) for d in range(1, 4)])
    new_store = jnp.take(jnp.concatenate(returned), came_back, axis=0, mode="clip").reshape(
        sessions_here, state_width
    )
    out_tokens = out_call(at, normed, (out_weight, ow_sibling, ow_across, ow_far))
    return (out_tokens, new_store)


def solution(mesh):
    return jax.shard_map(
        body,
        mesh=mesh,
        in_specs=(
            P(("groups", "dp"), "mp"),
            P(None, "mp"),
            P(None, "mp"),
            P(None, "mp"),
            P(None, "mp"),
            P("mp"),
            P("mp"),
            P("mp"),
            P("mp", None),
            P(("groups", "dp"), "mp"),
            P("groups"),
            P(("groups", "dp")),
        ),
        out_specs=(P(("groups", "dp", "mp"), None), P(("groups", "dp"), "mp")),
        check_vma=False,
    )
```

```python
import functools

import jax
import jax.numpy as jnp
import numpy as np
from jax import lax
from jax.experimental import pallas as pl
from jax.experimental.pallas import tpu as pltpu
from jax.sharding import PartitionSpec as P

BF = jnp.bfloat16
F32 = jnp.float32
ANY = pl.BlockSpec(memory_space=pl.ANY)
VMEM = pl.BlockSpec(memory_space=pltpu.VMEM)
SMEM = pl.BlockSpec(memory_space=pltpu.SMEM)
NT = (((1,), (1,)), ((), ()))


def pick(values, index):
    chosen = index[..., None] == jnp.arange(values.shape[0], dtype=jnp.int32)
    return jnp.sum(jnp.where(chosen, values, 0), axis=-1, dtype=jnp.int32)


def count_before(same, order):
    earlier = order[None, :] < order[:, None]
    return jnp.sum((same & earlier).astype(jnp.int32), axis=1)


def split_sessions(home_rows, block, per_target):
    total = home_rows.shape[0]
    session = jnp.arange(total, dtype=jnp.int32)
    server = session // block
    shard = home_rows // block
    same_server = server[:, None] == server[None, :]
    same_pair = same_server & (shard[:, None] == shard[None, :])
    rank = count_before(same_pair, session)
    size = jnp.sum(same_pair.astype(jnp.int32), axis=1)
    single = (rank ^ 1) >= size
    both_single = same_server & single[:, None] & single[None, :]
    single_rank = count_before(both_single, session)
    partners = (
        same_pair
        & ~single[:, None]
        & ~single[None, :]
        & (rank[None, :] == (rank ^ 1)[:, None])
    ) | (both_single & (single_rank[None, :] == (single_rank ^ 1)[:, None]))
    partner = jnp.sum(jnp.where(partners, session[None, :], 0), axis=1, dtype=jnp.int32)
    step = partner ^ 1
    lowest = session
    reach = 1
    while reach < block // 2:
        lowest = jnp.minimum(lowest, pick(lowest, step))
        step = pick(step, step)
        reach *= 2
    half = (lowest > pick(lowest, partner)).astype(jnp.int32)
    same_half = half[:, None] == half[None, :]
    target = session // per_target
    turn = count_before(same_half & (target[:, None] == target[None, :]), session)
    chunk = half * (per_target // 2) + turn
    place = count_before(same_half & same_pair, session)
    return server, shard, half, chunk, place


def copy_kernel(groups, index, source, *refs):
    outs, sems = refs[:-1], refs[-1]
    copies = []
    for k, out in enumerate(outs):
        for j in range(groups):
            n = k * groups + j
            copies.append(
                pltpu.make_async_copy(source.at[index[n]], out.at[j], sems.at[n])
            )
            copies[-1].start()
    for copy in copies:
        copy.wait()


def copy_rows(index, source, outs, name):
    groups = index.shape[0] // outs
    return pl.pallas_call(
        functools.partial(copy_kernel, groups),
        out_shape=[jax.ShapeDtypeStruct((groups,) + source.shape[1:], source.dtype)] * outs,
        in_specs=[SMEM, ANY],
        out_specs=[ANY] * outs,
        scratch_shapes=[pltpu.SemaphoreType.DMA((index.shape[0],))],
        compiler_params=pltpu.CompilerParams(vmem_limit_bytes=58 * 2**20),
        cost_estimate=pl.CostEstimate(
            flops=0, bytes_accessed=2 * source.size * 2, transcendentals=0
        ),
        name=name,
    )(index, source)


def layer_kernel(
    heads, span, aliased, meta, tokens, sibling, across, far, xw_any, zw_any, bw_any, bias, rate,
    gain, order, inbound, *refs,
):
    refs = refs[5 if aliased & 2 else (1 if aliased & 1 else 0):]
    n0, n1, n2, n3, outgoing = refs[:5]
    piece0, piece1, piece2, piece3, xw, zw, bw, state4, xs, zs, xt, fresh, sems, out_sems = refs[5:]
    normed_out = (n0, n1, n2, n3)
    pieces = (piece0, piece1, piece2, piece3)
    me = meta[12]
    depth = across.shape[1]
    quads = heads // 4
    copies = []

    def bring(source, target):
        copies.append(pltpu.make_async_copy(source, target, sems.at[len(copies)]))
        copies[-1].start()

    for d in range(4):
        rows = pl.ds(d * span, span)
        bring(tokens.at[meta[d]], piece0.at[rows])
        bring(sibling.at[meta[d]], piece1.at[rows])
    bring(across, piece2)
    for d in range(4):
        bring(far.at[pl.ds((d ^ 1) * span, span)], piece3.at[pl.ds(d * span, span)])
    bring(bw_any, bw)
    early = len(copies)
    bring(xw_any, xw)
    bring(zw_any, zw)
    for d in range(4):
        bring(inbound.at[meta[4 + d]], state4.at[d])

    def project(weight, columns):
        total = None
        for d in range(4):
            first = pl.multiple_of((me ^ d) * depth, depth)
            part = jnp.dot(
                pieces[d][...], weight[pl.ds(first, depth), columns], preferred_element_type=F32
            )
            total = part if total is None else total + part
        return total

    for copy in copies[:early]:
        copy.wait()
    bcs = project(bw, slice(None))

    lane = lax.broadcasted_iota(jnp.int32, (span, 128), 1)
    row = lax.broadcasted_iota(jnp.int32, (span, 128), 0)
    low = lane < 64
    causal = row >= lane
    lane8 = lax.broadcasted_iota(jnp.int32, (heads, span), 1)
    lane32 = lax.broadcasted_iota(jnp.int32, (heads * 4, span), 1)
    raw = jnp.concatenate(
        [jnp.transpose(bcs[d * span : (d + 1) * span, 128:256])[:heads] + bias[...] for d in range(4)],
        axis=0,
    )
    alive = jnp.concatenate([(lane8 < meta[8 + d]).astype(F32) for d in range(4)], axis=0)
    steps = (jnp.maximum(raw, 0.0) + jnp.log1p(jnp.exp(-jnp.abs(raw)))) * alive
    totals = steps * jnp.concatenate([rate[...]] * 4, axis=0)
    shift = 1
    while shift < span:
        totals = totals + jnp.where(lane32 >= shift, pltpu.roll(totals, shift, 1), 0.0)
        shift *= 2
    lasts = totals[:, span - 1 : span]
    weight_rows = jnp.exp(jnp.minimum(totals - lasts, 0.0)) * steps
    kept = jnp.exp(-lasts)
    cum = jnp.transpose(
        jnp.concatenate([totals, jnp.zeros((128 - heads * 4, span), F32)], axis=0)
    )

    copies[early].wait()
    for quad in range(quads):
        columns = slice(quad * 256, quad * 256 + 256)
        xs[:, columns] = project(xw, columns).astype(BF)
    copies[early + 1].wait()
    for quad in range(quads):
        columns = slice(quad * 256, quad * 256 + 256)
        zs[:, columns] = project(zw, columns).astype(BF)
    for copy in copies[early + 2 :]:
        copy.wait()

    wide = lax.broadcasted_iota(jnp.int32, (span, 256), 1) // 64
    head_masks = [(wide == k).astype(F32).astype(BF) for k in range(4)]
    sends = []
    for d in range(4):
        rows = slice(d * span, (d + 1) * span)
        count = meta[8 + d]
        bc = bcs[rows, 0:128]
        turned = pltpu.roll(bc, 64, 1)
        b_low = jnp.where(low, bc, 0.0).astype(BF)
        b_high = jnp.where(low, 0.0, turned).astype(BF)
        c_low = jnp.where(low, turned, 0.0).astype(BF)
        c_high = jnp.where(low, 0.0, bc).astype(BF)
        scores = lax.dot_general(c_low, b_low, NT, preferred_element_type=F32)
        scores = jnp.where(causal, scores, 0.0)
        state = state4[d]
        carried = lax.dot_general(
            jnp.concatenate([c_low, c_high], axis=0), state, NT, preferred_element_type=F32
        ).astype(BF)
        b_both = jnp.concatenate([b_low, b_high], axis=0)
        gated = []
        squares = None
        for quad in range(quads):
            columns = slice(quad * 256, quad * 256 + 256)
            part = slice(quad * 128, quad * 128 + 128)
            x = xs[rows, columns]
            mixes = []
            levels = []
            for k in range(4):
                head = d * heads + quad * 4 + k
                level = jnp.broadcast_to(cum[:, head : head + 1], (span, 128))
                gap = jnp.minimum(totals[head : head + 1, :] - level, 0.0)
                mixes.append((jnp.exp(gap) * steps[head : head + 1, :] * scores).astype(BF))
                levels.append(level)
            diagonal = jnp.dot(
                jnp.concatenate(mixes, axis=1),
                jnp.concatenate([x * head_masks[k] for k in range(4)], axis=0),
                preferred_element_type=F32,
            )
            before = jnp.dot(
                jnp.concatenate([carried[:span, part], carried[span:, part]], axis=1),
                order[...],
                preferred_element_type=F32,
            )
            fade = jnp.exp(
                -jnp.concatenate(
                    [jnp.where(low, levels[0], levels[1]), jnp.where(low, levels[2], levels[3])],
                    axis=1,
                )
            )
            gate = zs[rows, columns].astype(F32)
            value = (diagonal + before * fade) * (gate / (1.0 + jnp.exp(-gate)))
            gated.append(value)
            own = jnp.sum(value * value, axis=1, keepdims=True)
            squares = own if squares is None else squares + own
            flipped = jnp.transpose(x.astype(F32))
            first_head = d * heads + quad * 4
            xt[d, quad] = flipped * jnp.concatenate(
                [
                    jnp.broadcast_to(weight_rows[first_head + k : first_head + k + 1, :], (64, span))
                    for k in range(4)
                ],
                axis=0,
            )
            even = xt[d, quad, pl.ds(0, 128, stride=2), :].astype(BF)
            odd = xt[d, quad, pl.ds(1, 128, stride=2), :].astype(BF)
            added = jnp.dot(
                jnp.concatenate([even, odd], axis=1), b_both, preferred_element_type=F32
            )
            keep_rows = jnp.concatenate(
                [
                    jnp.broadcast_to(kept[first_head + k : first_head + k + 1, :], (32, 128))
                    for k in range(4)
                ],
                axis=0,
            )
            fresh[d, part, :] = (keep_rows * state[part].astype(F32) + added).astype(BF)
        sends.append(
            pltpu.make_async_copy(fresh.at[d], outgoing.at[meta[4 + d]], out_sems.at[d])
        )
        sends[-1].start()
        inverse = lax.rsqrt(squares * (1.0 / (heads * 64)) + 1e-05)
        inverse = jnp.where(row[:, :1] < count, inverse, 0.0)
        for quad in range(quads):
            columns = slice(quad * 256, quad * 256 + 256)
            normed_out[d][:, columns] = (gated[quad] * inverse * gain[:, columns]).astype(BF)
    for send in sends:
        send.wait()


def layer_call(meta, tokens, sibling, across, far, weights, small, inbound, turn, turns, earlier):
    rows, depth = across.shape
    heads = small[0].shape[0]
    width = weights[0].shape[1]
    span = rows // 4
    row_shape = inbound.shape[1:]
    operands = [tokens, sibling, across, far, *weights, *small, inbound]
    aliases = {}
    aliased = 0
    if earlier is not None:
        aliased = 1 if len(earlier) == 1 else 2
        first = 1 + len(operands)
        for k in range(len(earlier)):
            aliases[first + k] = k + 5 - len(earlier)
        operands += list(earlier)
    return pl.pallas_call(
        functools.partial(layer_kernel, heads, span, aliased),
        out_shape=[jax.ShapeDtypeStruct((turns * span, width), BF)] * 4
        + [jax.ShapeDtypeStruct(inbound.shape, BF)],
        grid_spec=pltpu.PrefetchScalarGridSpec(
            num_scalar_prefetch=1,
            grid=(1,),
            in_specs=[ANY] * 7 + [VMEM] * 4 + [ANY] * (len(operands) - 11),
            out_specs=[pl.BlockSpec((span, width), lambda i, meta: (turn, 0))] * 4 + [ANY],
            scratch_shapes=[
                *[pltpu.VMEM((rows, depth), BF)] * 4,
                *[pltpu.VMEM(weight.shape, BF) for weight in weights],
                pltpu.VMEM((4,) + row_shape, BF),
                pltpu.VMEM((rows, width), BF),
                pltpu.VMEM((rows, width), BF),
                pltpu.VMEM((4, heads // 4, 256, span), F32),
                pltpu.VMEM((4,) + row_shape, BF),
                pltpu.SemaphoreType.DMA((20,)),
                pltpu.SemaphoreType.DMA((4,)),
            ],
        ),
        input_output_aliases=aliases,
        compiler_params=pltpu.CompilerParams(vmem_limit_bytes=58 * 2**20),
        cost_estimate=pl.CostEstimate(
            flops=8 * 10**9, bytes_accessed=9 * 2**20, transcendentals=0
        ),
        name="layer",
    )(meta, *operands)


def out_kernel(where, span, at_ref, *refs):
    weights, out = refs[-5:-1], refs[-1]
    for chunk, (first, offset) in enumerate(where):
        total = None
        for d in range(4):
            piece = refs[first * 4 + d][offset * span : (offset + 1) * span, :]
            part = jnp.dot(piece, weights[d][...], preferred_element_type=F32)
            total = part if total is None else total + part
        out[at_ref[chunk]] = total.astype(BF)


def out_call(at, normed, weights, span):
    depth = normed[0].shape[1]
    columns = weights[0].shape[1]
    chunks = at.shape[0]
    block = 512
    where = [
        (k, offset)
        for k in range(len(normed) // 4)
        for offset in range(normed[k * 4].shape[0] // span)
    ]
    return pl.pallas_call(
        functools.partial(out_kernel, where, span),
        grid=(columns // block,),
        out_shape=jax.ShapeDtypeStruct((chunks, span, columns), BF),
        in_specs=[SMEM]
        + [pl.BlockSpec(piece.shape, lambda j: (0, 0)) for piece in normed]
        + [pl.BlockSpec((depth, block), lambda j: (0, j))] * 4,
        out_specs=pl.BlockSpec((chunks, span, block), lambda j: (0, 0, j)),
        compiler_params=pltpu.CompilerParams(vmem_limit_bytes=58 * 2**20),
        cost_estimate=pl.CostEstimate(
            flops=2 * chunks * span * depth * 4 * columns,
            bytes_accessed=12 * 2**20,
            transcendentals=0,
        ),
        name="project_out",
    )(at, *normed, *weights)


def gather_kernel(sessions, slots, index, first, second, out):
    lines = out.shape[1] // 128
    picked = []
    for r in range(sessions):
        slot = index[r]
        inside = jnp.minimum(slot, slots - 1)
        other = jnp.maximum(slot - slots, 0)
        scale = jnp.where(slot < slots, 1.0, 0.0)
        picked.append(
            jnp.where(scale > 0.5, first[inside].astype(F32), second[other].astype(F32))
        )
    block = jnp.stack(picked, axis=0)
    turned = jnp.swapaxes(block, 0, 1)
    for j in range(lines):
        out[:, j * 128 : (j + 1) * 128] = turned[j].astype(BF)


def gather_call(index, first, second):
    sessions = index.shape[0]
    slots, lines, lanes = first.shape
    block = 16
    return pl.pallas_call(
        functools.partial(gather_kernel, sessions, slots),
        grid=(lines // block,),
        out_shape=jax.ShapeDtypeStruct((sessions, lines * lanes), BF),
        in_specs=[SMEM] + [pl.BlockSpec((slots, block, lanes), lambda j: (0, j, 0))] * 2,
        out_specs=pl.BlockSpec((sessions, block * lanes), lambda j: (0, j)),
        compiler_params=pltpu.CompilerParams(vmem_limit_bytes=58 * 2**20),
        cost_estimate=pl.CostEstimate(
            flops=0, bytes_accessed=2 * 2**20, transcendentals=0
        ),
        name="gather_states",
    )(index, first, second)


def after(value, *others):
    return lax.optimization_barrier((value,) + others)[0]


def body(
    tokens,
    x_weight,
    z_weight,
    bc_weight,
    dt_weight,
    dt_bias,
    decay_rate,
    norm_gain,
    out_weight,
    store_states,
    home_rows,
    event_counts,
):
    shard_count = lax.axis_size("dp")
    model_shards = lax.axis_size("mp")
    shard_index = lax.axis_index("dp")
    me = lax.axis_index("mp")
    sessions_here, state_width = store_states.shape
    heads = dt_bias.shape[0]
    width = x_weight.shape[1]
    depth = tokens.shape[1]
    span = tokens.shape[0] // sessions_here
    chunks = sessions_here // model_shards
    capacity = max(2, (sessions_here + shard_count - 1) // shard_count)
    places = (capacity + 1) // 2
    slot_count = shard_count * places
    row_shape = (state_width // 128, 128)

    def exchange(value, distance):
        pairs = [(j, j ^ distance) for j in range(model_shards)]
        return lax.ppermute(value, "mp", pairs)

    def trade(value):
        return lax.all_to_all(
            value.reshape((shard_count, places) + row_shape),
            "dp",
            split_axis=0,
            concat_axis=0,
            tiled=True,
        ).reshape((slot_count,) + row_shape)

    replicas = lax.axis_size("groups") * shard_count
    replica = lax.axis_index("groups") * shard_count + shard_index
    share = width // replicas
    ow_part = exchange(lax.dynamic_slice_in_dim(out_weight, replica * share, share), 2)
    sibling = exchange(tokens, 1).reshape(sessions_here, span, depth)

    server, shard, half, chunk, place = split_sessions(home_rows, sessions_here, chunks)
    local = jnp.arange(sessions_here, dtype=jnp.int32)
    mine = shard_index * sessions_here + local
    my_chunk = pick(chunk, mine)
    my_slot = pick(shard * places + place, mine)
    relative = jnp.arange(model_shards, dtype=jnp.int32) ^ me
    turns_from = jnp.arange(chunks, dtype=jnp.int32)

    def arranged(values, targets):
        by_turn = (turns_from[:, None, None] == my_chunk) & (
            targets[None, :, None] == local // chunks
        )
        return jnp.sum(jnp.where(by_turn, values, 0), axis=2, dtype=jnp.int32)

    turns = arranged(local, relative)
    meta = jnp.concatenate(
        [
            turns,
            arranged(my_slot, relative),
            arranged(event_counts, relative),
            jnp.full((chunks, 4), me, jnp.int32),
        ],
        axis=1,
    )
    at = turns[:, 0] - me * chunks

    by_session = tokens.reshape(sessions_here, span, depth)
    outward = arranged(local, relative ^ 2)
    own = [
        piece.reshape(model_shards * span, depth)
        for piece in copy_rows(outward.reshape(-1), by_session, chunks, "pack_tokens")
    ]
    across = []
    for c in range(chunks):
        ready = own[c]
        if c >= 2:
            ready = after(ready, across[c - 2])
        elif c == 1:
            ready = after(ready, ow_part)
        across.append(exchange(ready, 2))

    store_row = home_rows - shard_index * sessions_here
    here = shard == shard_index
    there = server * places + place
    wanted = jnp.arange(2 * slot_count, dtype=jnp.int32)
    filed = half * slot_count + there
    chosen = (wanted[:, None] == filed[None, :]) & here[None, :]
    source = jnp.sum(jnp.where(chosen, store_row[None, :], 0), axis=1)
    kept = store_states.reshape((sessions_here,) + row_shape)
    inbound = [trade(part) for part in copy_rows(source, kept, 2, "pack_states")]
    owned = here[None, :] & (store_row[None, :] == local[:, None])
    came_back = jnp.sum(jnp.where(owned, filed, 0), axis=1)

    column = np.arange(256)
    natural = (column % 128 // 32) * 64 + column % 32 * 2 + column // 128
    order = jnp.asarray(natural[:, None] == column[None, :], BF)
    bw = jnp.concatenate(
        [bc_weight, dt_weight, jnp.zeros((bc_weight.shape[0], 128 - heads), BF)], axis=1
    )

    ow_across = lax.all_gather(ow_part, ("groups", "dp"), axis=0, tiled=True)
    ow_sibling = exchange(out_weight, 1)
    ow_far = exchange(ow_across, 1)

    small = (
        dt_bias.reshape(heads, 1),
        decay_rate.reshape(heads, 1),
        norm_gain.reshape(1, width),
        order,
    )
    weights = (x_weight, z_weight, bw)
    per_half = chunks // 2
    normed = []
    returned = []
    received = []
    earlier = None
    for c in range(chunks):
        number = c // per_half
        turn = meta[c]
        arrived = across[c]
        if c >= 1:
            turn = after(turn, normed[c - 1][0])
        if c >= 2:
            arrived = after(arrived, normed[c - 2][0])
        far = exchange(arrived, 1)
        merged = number == 0
        parts = layer_call(
            turn,
            by_session,
            sibling,
            arrived,
            far,
            weights,
            small,
            inbound[number],
            c % per_half if merged else 0,
            per_half if merged else 1,
            earlier,
        )
        normed.append(parts)
        last = (c + 1) % per_half == 0
        earlier = None if last else (parts if merged else parts[4:])
        if last:
            returned.append(trade(parts[4]))
        if last or not merged:
            received.append([parts[0]] + [exchange(parts[d], d) for d in range(1, 4)])
    new_store = gather_call(came_back, *returned)
    ow = (out_weight, ow_sibling, ow_across, ow_far)
    pieces = [piece for group in received for piece in group]
    out_tokens = out_call(at, pieces, ow, span).reshape(chunks * span, out_weight.shape[1])
    return (out_tokens, new_store)


def solution(mesh):
    return jax.shard_map(
        body,
        mesh=mesh,
        in_specs=(
            P(("groups", "dp"), "mp"),
            P(None, "mp"),
            P(None, "mp"),
            P(None, "mp"),
            P(None, "mp"),
            P("mp"),
            P("mp"),
            P("mp"),
            P("mp", None),
            P(("groups", "dp"), "mp"),
            P("groups"),
            P(("groups", "dp")),
        ),
        out_specs=(P(("groups", "dp", "mp"), None), P(("groups", "dp"), "mp")),
        check_vma=False,
    )
```

```python
import functools

import jax
import jax.numpy as jnp
import numpy as np
from jax import lax
from jax.experimental import pallas as pl
from jax.experimental.pallas import tpu as pltpu
from jax.sharding import PartitionSpec as P

BF = jnp.bfloat16
F32 = jnp.float32
ANY = pl.BlockSpec(memory_space=pl.ANY)
VMEM = pl.BlockSpec(memory_space=pltpu.VMEM)
SMEM = pl.BlockSpec(memory_space=pltpu.SMEM)
NT = (((1,), (1,)), ((), ()))


def pick(values, index):
    chosen = index[..., None] == jnp.arange(values.shape[0], dtype=jnp.int32)
    return jnp.sum(jnp.where(chosen, values, 0), axis=-1, dtype=jnp.int32)


def count_before(same, order):
    earlier = order[None, :] < order[:, None]
    return jnp.sum((same & earlier).astype(jnp.int32), axis=1)


def split_sessions(home_rows, block, per_target):
    total = home_rows.shape[0]
    session = jnp.arange(total, dtype=jnp.int32)
    server = session // block
    shard = home_rows // block
    same_server = server[:, None] == server[None, :]
    same_pair = same_server & (shard[:, None] == shard[None, :])
    rank = count_before(same_pair, session)
    size = jnp.sum(same_pair.astype(jnp.int32), axis=1)
    single = (rank ^ 1) >= size
    both_single = same_server & single[:, None] & single[None, :]
    single_rank = count_before(both_single, session)
    partners = (
        same_pair
        & ~single[:, None]
        & ~single[None, :]
        & (rank[None, :] == (rank ^ 1)[:, None])
    ) | (both_single & (single_rank[None, :] == (single_rank ^ 1)[:, None]))
    partner = jnp.sum(jnp.where(partners, session[None, :], 0), axis=1, dtype=jnp.int32)
    step = partner ^ 1
    lowest = session
    reach = 1
    while reach < block // 2:
        lowest = jnp.minimum(lowest, pick(lowest, step))
        step = pick(step, step)
        reach *= 2
    half = (lowest > pick(lowest, partner)).astype(jnp.int32)
    same_half = half[:, None] == half[None, :]
    target = session // per_target
    turn = count_before(same_half & (target[:, None] == target[None, :]), session)
    chunk = half * (per_target // 2) + turn
    place = count_before(same_half & same_pair, session)
    return server, shard, half, chunk, place


def pack_tokens_kernel(chunks, meta, source, *refs):
    outs, held, in_sems, out_sems = refs[:chunks], refs[chunks], refs[-2], refs[-1]
    groups = held.shape[0] // chunks
    coming, going = [], []
    for n in range(chunks * groups):
        first = n // groups * groups
        coming.append(
            pltpu.make_async_copy(
                source.at[meta[first + (n - first ^ 2)]], held.at[n], in_sems.at[n]
            )
        )
        coming[-1].start()
    for n in range(chunks * groups):
        coming[n].wait()
        going.append(
            pltpu.make_async_copy(held.at[n], outs[n // groups].at[n % groups], out_sems.at[n])
        )
        going[-1].start()
    for copy in going:
        copy.wait()


def pack_tokens(meta, source, chunks):
    blocks = source.shape[0]
    groups = blocks // chunks
    return pl.pallas_call(
        functools.partial(pack_tokens_kernel, chunks),
        out_shape=[jax.ShapeDtypeStruct((groups,) + source.shape[1:], source.dtype)] * chunks,
        in_specs=[SMEM, ANY],
        out_specs=[ANY] * chunks,
        scratch_shapes=[
            pltpu.VMEM(source.shape, source.dtype),
            pltpu.SemaphoreType.DMA((blocks,)),
            pltpu.SemaphoreType.DMA((blocks,)),
        ],
        compiler_params=pltpu.CompilerParams(vmem_limit_bytes=16 * 2**20),
        cost_estimate=pl.CostEstimate(
            flops=0, bytes_accessed=2 * source.size * 2, transcendentals=0
        ),
        name="pack_tokens",
    )(meta, source)


def pack_states(source, store, swap, slots):
    sessions, width = store.shape
    lines = width // 128

    def kernel(source, store, swap, first, second, held):
        for part in range(4):
            base = part * 16 * 128
            stacked = jnp.concatenate(
                [store[:, base + j * 128 : base + (j + 1) * 128] for j in range(16)], axis=0
            )
            turned = jnp.dot(swap[...], stacked, preferred_element_type=F32).astype(BF)
            for r in range(sessions):
                held[r, part * 16 : (part + 1) * 16, :] = turned[r * 16 : (r + 1) * 16]
        for n in range(slots):
            first[n] = held[source[n]]
            second[n] = held[source[slots + n]]

    return pl.pallas_call(
        kernel,
        grid=(lines // 64,),
        out_shape=[jax.ShapeDtypeStruct((slots, lines, 128), BF)] * 2,
        in_specs=[
            SMEM,
            pl.BlockSpec((sessions, 64 * 128), lambda j: (0, j)),
            pl.BlockSpec(swap.shape, lambda j: (0, 0)),
        ],
        out_specs=[pl.BlockSpec((slots, 64, 128), lambda j: (0, j, 0))] * 2,
        scratch_shapes=[pltpu.VMEM((sessions, 64, 128), BF)],
        compiler_params=pltpu.CompilerParams(vmem_limit_bytes=16 * 2**20),
        cost_estimate=pl.CostEstimate(
            flops=2 * 256 * 256 * width // 16, bytes_accessed=4 * 2**20, transcendentals=0
        ),
        name="pack_states",
    )(source, store, swap)


def layer_kernel(
    heads, span, chunk, aliased, meta, tokens, sibling, across, far, xw, zw, bw, bias, rate, gain,
    order, inbound, *refs,
):
    refs = refs[aliased:]
    n0, n1, n2, n3, outgoing, xs, zs, xt, fresh, out_sems = refs
    normed_out = (n0, n1, n2, n3)
    groups = meta.shape[0] // 4
    turn_at, slot_at, count_at = chunk * 4, groups + chunk * 4, 2 * groups + chunk * 4
    me = meta[3 * groups]
    depth = across.shape[1]
    quads = heads // 4
    pieces = (
        jnp.concatenate([tokens[meta[turn_at + d]] for d in range(4)], axis=0),
        jnp.concatenate([sibling[meta[turn_at + d]] for d in range(4)], axis=0),
        across[...],
        jnp.concatenate([far[(d ^ 1) * span : ((d ^ 1) + 1) * span] for d in range(4)], axis=0),
    )

    def project(weight, columns):
        total = None
        for d in range(4):
            first = pl.multiple_of((me ^ d) * depth, depth)
            part = jnp.dot(
                pieces[d], weight[pl.ds(first, depth), columns], preferred_element_type=F32
            )
            total = part if total is None else total + part
        return total

    bcs = project(bw, slice(None))

    lane = lax.broadcasted_iota(jnp.int32, (span, 128), 1)
    row = lax.broadcasted_iota(jnp.int32, (span, 128), 0)
    low = lane < 64
    causal = row >= lane
    lane8 = lax.broadcasted_iota(jnp.int32, (heads, span), 1)
    lane32 = lax.broadcasted_iota(jnp.int32, (heads * 4, span), 1)
    raw = jnp.concatenate(
        [jnp.transpose(bcs[d * span : (d + 1) * span, 128:256])[:heads] + bias[...] for d in range(4)],
        axis=0,
    )
    alive = jnp.concatenate([(lane8 < meta[count_at + d]).astype(F32) for d in range(4)], axis=0)
    steps = (jnp.maximum(raw, 0.0) + jnp.log1p(jnp.exp(-jnp.abs(raw)))) * alive
    totals = steps * jnp.concatenate([rate[...]] * 4, axis=0)
    shift = 1
    while shift < span:
        totals = totals + jnp.where(lane32 >= shift, pltpu.roll(totals, shift, 1), 0.0)
        shift *= 2
    lasts = totals[:, span - 1 : span]
    weight_rows = jnp.exp(jnp.minimum(totals - lasts, 0.0)) * steps
    kept = jnp.exp(-lasts)
    cum = jnp.transpose(
        jnp.concatenate([totals, jnp.zeros((128 - heads * 4, span), F32)], axis=0)
    )

    for quad in range(quads):
        columns = slice(quad * 256, quad * 256 + 256)
        xs[:, columns] = project(xw, columns).astype(BF)
    for quad in range(quads):
        columns = slice(quad * 256, quad * 256 + 256)
        zs[:, columns] = project(zw, columns).astype(BF)

    wide = lax.broadcasted_iota(jnp.int32, (span, 256), 1) // 64
    head_masks = [(wide == k).astype(F32).astype(BF) for k in range(4)]
    sends = []
    for d in range(4):
        rows = slice(d * span, (d + 1) * span)
        count = meta[count_at + d]
        bc = bcs[rows, 0:128]
        turned = pltpu.roll(bc, 64, 1)
        b_low = jnp.where(low, bc, 0.0).astype(BF)
        b_high = jnp.where(low, 0.0, turned).astype(BF)
        c_low = jnp.where(low, turned, 0.0).astype(BF)
        c_high = jnp.where(low, 0.0, bc).astype(BF)
        scores = lax.dot_general(c_low, b_low, NT, preferred_element_type=F32)
        scores = jnp.where(causal, scores, 0.0)
        state = inbound[meta[slot_at + d]]
        carried = lax.dot_general(
            jnp.concatenate([c_low, c_high], axis=0), state, NT, preferred_element_type=F32
        ).astype(BF)
        b_both = jnp.concatenate([b_low, b_high], axis=0)
        gated = []
        squares = None
        for quad in range(quads):
            columns = slice(quad * 256, quad * 256 + 256)
            part = slice(quad * 128, quad * 128 + 128)
            x = xs[rows, columns]
            mixes = []
            levels = []
            for k in range(4):
                head = d * heads + quad * 4 + k
                level = jnp.broadcast_to(cum[:, head : head + 1], (span, 128))
                gap = jnp.minimum(totals[head : head + 1, :] - level, 0.0)
                mixes.append((jnp.exp(gap) * steps[head : head + 1, :] * scores).astype(BF))
                levels.append(level)
            diagonal = jnp.dot(
                jnp.concatenate(mixes, axis=1),
                jnp.concatenate([x * head_masks[k] for k in range(4)], axis=0),
                preferred_element_type=F32,
            )
            before = jnp.dot(
                jnp.concatenate([carried[:span, part], carried[span:, part]], axis=1),
                order[...],
                preferred_element_type=F32,
            )
            fade = jnp.exp(
                -jnp.concatenate(
                    [jnp.where(low, levels[0], levels[1]), jnp.where(low, levels[2], levels[3])],
                    axis=1,
                )
            )
            gate = zs[rows, columns].astype(F32)
            value = (diagonal + before * fade) * (gate * (0.5 + 0.5 * jnp.tanh(0.5 * gate)))
            gated.append(value)
            own = jnp.sum(value * value, axis=1, keepdims=True)
            squares = own if squares is None else squares + own
            flipped = jnp.transpose(x.astype(F32))
            first_head = d * heads + quad * 4
            xt[d, quad] = flipped * jnp.concatenate(
                [
                    jnp.broadcast_to(weight_rows[first_head + k : first_head + k + 1, :], (64, span))
                    for k in range(4)
                ],
                axis=0,
            )
            even = xt[d, quad, pl.ds(0, 128, stride=2), :].astype(BF)
            odd = xt[d, quad, pl.ds(1, 128, stride=2), :].astype(BF)
            added = jnp.dot(
                jnp.concatenate([even, odd], axis=1), b_both, preferred_element_type=F32
            )
            keep_rows = jnp.concatenate(
                [
                    jnp.broadcast_to(kept[first_head + k : first_head + k + 1, :], (32, 128))
                    for k in range(4)
                ],
                axis=0,
            )
            fresh[d, part, :] = (keep_rows * state[part].astype(F32) + added).astype(BF)
        sends.append(
            pltpu.make_async_copy(fresh.at[d], outgoing.at[meta[slot_at + d]], out_sems.at[d])
        )
        sends[-1].start()
        inverse = lax.rsqrt(squares * (1.0 / (heads * 64)) + 1e-05)
        inverse = jnp.where(row[:, :1] < count, inverse, 0.0)
        for quad in range(quads):
            columns = slice(quad * 256, quad * 256 + 256)
            normed_out[d][:, columns] = (gated[quad] * inverse * gain[:, columns]).astype(BF)
    for send in sends:
        send.wait()


def layer_call(
    meta, chunk, tokens, sibling, across, far, weights, small, inbound, turn, turns, earlier
):
    rows, depth = across.shape
    heads = small[0].shape[0]
    width = weights[0].shape[1]
    span = rows // 4
    row_shape = inbound.shape[1:]
    operands = [meta, tokens, sibling, across, far, *weights, *small, inbound]
    known = len(operands) - 1
    aliases = {}
    if earlier is not None:
        for k in range(len(earlier)):
            aliases[len(operands) + k] = k + 5 - len(earlier)
        operands += list(earlier)
    extra = len(operands) - 1 - known
    return pl.pallas_call(
        functools.partial(layer_kernel, heads, span, chunk, extra),
        grid=(1,),
        out_shape=[jax.ShapeDtypeStruct((turns * span, width), BF)] * 4
        + [jax.ShapeDtypeStruct(inbound.shape, BF)],
        in_specs=[SMEM] + [VMEM] * known + [ANY] * extra,
        out_specs=[pl.BlockSpec((span, width), lambda i: (turn, 0))] * 4 + [ANY],
        scratch_shapes=[
            pltpu.VMEM((rows, width), BF),
            pltpu.VMEM((rows, width), BF),
            pltpu.VMEM((4, heads // 4, 256, span), F32),
            pltpu.VMEM((4,) + row_shape, BF),
            pltpu.SemaphoreType.DMA((4,)),
        ],
        input_output_aliases=aliases,
        compiler_params=pltpu.CompilerParams(vmem_limit_bytes=32 * 2**20),
        cost_estimate=pl.CostEstimate(
            flops=8 * 10**9, bytes_accessed=9 * 2**20, transcendentals=0
        ),
        name="layer",
    )(*operands)


def out_kernel(where, span, at_ref, *refs):
    weights, out = refs[-5:-1], refs[-1]
    for chunk, (first, offset) in enumerate(where):
        total = None
        for d in range(4):
            piece = refs[first * 4 + d][offset * span : (offset + 1) * span, :]
            part = jnp.dot(piece, weights[d][...], preferred_element_type=F32)
            total = part if total is None else total + part
        out[at_ref[chunk]] = total.astype(BF)


def out_call(at, normed, weights, span):
    depth = normed[0].shape[1]
    columns = weights[0].shape[1]
    chunks = at.shape[0]
    block = 512
    where = [
        (k, offset)
        for k in range(len(normed) // 4)
        for offset in range(normed[k * 4].shape[0] // span)
    ]
    return pl.pallas_call(
        functools.partial(out_kernel, where, span),
        grid=(columns // block,),
        out_shape=jax.ShapeDtypeStruct((chunks, span, columns), BF),
        in_specs=[SMEM]
        + [pl.BlockSpec(piece.shape, lambda j: (0, 0)) for piece in normed]
        + [pl.BlockSpec((depth, block), lambda j: (0, j))] * 4,
        out_specs=pl.BlockSpec((chunks, span, block), lambda j: (0, 0, j)),
        compiler_params=pltpu.CompilerParams(vmem_limit_bytes=32 * 2**20),
        cost_estimate=pl.CostEstimate(
            flops=2 * chunks * span * depth * 4 * columns,
            bytes_accessed=12 * 2**20,
            transcendentals=0,
        ),
        name="project_out",
    )(at, *normed, *weights)


def gather_kernel(sessions, slots, index, first, second, swap, out):
    for part in range(4):
        lines = slice(part * 16, (part + 1) * 16)
        stacked = jnp.concatenate(
            [
                jnp.where(
                    index[r] < slots,
                    first[jnp.minimum(index[r], slots - 1), lines, :],
                    second[jnp.maximum(index[r] - slots, 0), lines, :],
                )
                for r in range(sessions)
            ],
            axis=0,
        )
        turned = lax.dot_general(
            swap[...], stacked, (((0,), (0,)), ((), ())), preferred_element_type=F32
        ).astype(BF)
        for j in range(16):
            column = (part * 16 + j) * 128
            out[:, column : column + 128] = turned[j * sessions : (j + 1) * sessions]


def gather_states(index, first, second, swap):
    sessions = index.shape[0]
    slots, lines, lanes = first.shape
    return pl.pallas_call(
        functools.partial(gather_kernel, sessions, slots),
        grid=(lines // 64,),
        out_shape=jax.ShapeDtypeStruct((sessions, lines * lanes), BF),
        in_specs=[SMEM]
        + [pl.BlockSpec((slots, 64, lanes), lambda j: (0, j, 0))] * 2
        + [pl.BlockSpec(swap.shape, lambda j: (0, 0))],
        out_specs=pl.BlockSpec((sessions, 64 * lanes), lambda j: (0, j)),
        compiler_params=pltpu.CompilerParams(vmem_limit_bytes=16 * 2**20),
        cost_estimate=pl.CostEstimate(
            flops=0, bytes_accessed=2 * 2**20, transcendentals=0
        ),
        name="gather_states",
    )(index, first, second, swap)


def after(value, *others):
    return lax.optimization_barrier((value,) + others)[0]


def body(
    tokens,
    x_weight,
    z_weight,
    bc_weight,
    dt_weight,
    dt_bias,
    decay_rate,
    norm_gain,
    out_weight,
    store_states,
    home_rows,
    event_counts,
):
    shard_count = lax.axis_size("dp")
    model_shards = lax.axis_size("mp")
    shard_index = lax.axis_index("dp")
    me = lax.axis_index("mp")
    sessions_here, state_width = store_states.shape
    heads = dt_bias.shape[0]
    width = x_weight.shape[1]
    depth = tokens.shape[1]
    span = tokens.shape[0] // sessions_here
    chunks = sessions_here // model_shards
    capacity = max(2, (sessions_here + shard_count - 1) // shard_count)
    places = (capacity + 1) // 2
    slot_count = shard_count * places
    row_shape = (state_width // 128, 128)

    def exchange(value, distance):
        pairs = [(j, j ^ distance) for j in range(model_shards)]
        return lax.ppermute(value, "mp", pairs)

    def trade(value):
        return lax.all_to_all(
            value.reshape((shard_count, places) + row_shape),
            "dp",
            split_axis=0,
            concat_axis=0,
            tiled=True,
        ).reshape((slot_count,) + row_shape)

    replicas = lax.axis_size("groups") * shard_count
    replica = lax.axis_index("groups") * shard_count + shard_index
    share = width // replicas
    ow_part = exchange(lax.dynamic_slice_in_dim(out_weight, replica * share, share), 2)
    sibling = exchange(tokens, 1).reshape(sessions_here, span, depth)

    server, shard, half, chunk, place = split_sessions(home_rows, sessions_here, chunks)
    local = jnp.arange(sessions_here, dtype=jnp.int32)
    mine = shard_index * sessions_here + local
    my_chunk = pick(chunk, mine)
    my_slot = pick(shard * places + place, mine)
    entry = jnp.arange(sessions_here, dtype=jnp.int32)
    by_turn = (
        (entry // model_shards)[:, None] == my_chunk[None, :]
    ) & ((entry % model_shards ^ me)[:, None] == (local // chunks)[None, :])

    def arranged(values):
        return jnp.sum(jnp.where(by_turn, values[None, :], 0), axis=1, dtype=jnp.int32)

    turns = arranged(local)
    meta = jnp.concatenate(
        [
            turns,
            arranged(my_slot),
            arranged(event_counts),
            jnp.full((sessions_here,), me, jnp.int32),
        ]
    )

    by_session = tokens.reshape(sessions_here, span, depth)
    own = [
        piece.reshape(model_shards * span, depth)
        for piece in pack_tokens(meta, by_session, chunks)
    ]
    store_row = home_rows - shard_index * sessions_here
    here = shard == shard_index
    there = server * places + place
    wanted = jnp.arange(2 * slot_count, dtype=jnp.int32)
    filed = half * slot_count + there
    chosen = (wanted[:, None] == filed[None, :]) & here[None, :]
    source = jnp.sum(jnp.where(chosen, store_row[None, :], 0), axis=1)
    row = np.arange(sessions_here * 16)
    swap = jnp.asarray(
        (row % 16 * sessions_here + row // 16)[:, None] == row[None, :], BF
    )
    packed = pack_states(after(source, own[0]), store_states, swap, slot_count)
    inbound = [trade(part) for part in packed]
    owned = here[None, :] & (store_row[None, :] == local[:, None])
    came_back = jnp.sum(jnp.where(owned, filed, 0), axis=1)

    across = []
    for c in range(chunks):
        ready = own[c]
        if c >= 2:
            ready = after(ready, across[c - 2])
        elif c == 1:
            ready = after(ready, packed[0])
        across.append(exchange(ready, 2))

    column = np.arange(256)
    natural = (column % 128 // 32) * 64 + column % 32 * 2 + column // 128
    order = jnp.asarray(natural[:, None] == column[None, :], BF)
    bw = jnp.concatenate(
        [bc_weight, dt_weight, jnp.zeros((bc_weight.shape[0], 128 - heads), BF)], axis=1
    )

    ow_part = after(ow_part, own[0])
    ow_across = lax.all_gather(ow_part, ("groups", "dp"), axis=0, tiled=True)
    ow_sibling = exchange(out_weight, 1)
    ow_far = exchange(ow_across, 1)

    small = (
        dt_bias.reshape(heads, 1),
        decay_rate.reshape(heads, 1),
        norm_gain.reshape(1, width),
        order,
    )
    weights = (x_weight, z_weight, bw)
    per_half = chunks // 2
    normed = []
    returned = []
    received = []
    earlier = None
    for c in range(chunks):
        number = c // per_half
        turn = meta
        arrived = across[c]
        if c >= 1:
            turn = after(turn, normed[c - 1][0])
        if c == chunks - 1:
            turn = after(turn, *received[0], returned[0])
        if c >= 2:
            arrived = after(arrived, normed[c - 2][0])
        far = exchange(arrived, 1)
        merged = number == 0
        parts = layer_call(
            turn,
            c,
            by_session,
            sibling,
            arrived,
            far,
            weights,
            small,
            inbound[number],
            c % per_half if merged else 0,
            per_half if merged else 1,
            earlier,
        )
        normed.append(parts)
        last = (c + 1) % per_half == 0
        earlier = None if last else (parts if merged else parts[4:])
        if last:
            returned.append(trade(parts[4]))
        if last or not merged:
            received.append([parts[0]] + [exchange(parts[d], d) for d in range(1, 4)])
    new_store = gather_states(came_back, *returned, swap)
    ow = (out_weight, ow_sibling, ow_across, ow_far)
    pieces = [piece for group in received for piece in group]
    at = (turns - me * chunks).reshape(chunks, model_shards)[:, 0]
    out_tokens = out_call(at, pieces, ow, span).reshape(chunks * span, out_weight.shape[1])
    return (out_tokens, new_store)


def solution(mesh):
    return jax.shard_map(
        body,
        mesh=mesh,
        in_specs=(
            P(("groups", "dp"), "mp"),
            P(None, "mp"),
            P(None, "mp"),
            P(None, "mp"),
            P(None, "mp"),
            P("mp"),
            P("mp"),
            P("mp"),
            P("mp", None),
            P(("groups", "dp"), "mp"),
            P("groups"),
            P(("groups", "dp")),
        ),
        out_specs=(P(("groups", "dp", "mp"), None), P(("groups", "dp"), "mp")),
        check_vma=False,
    )
```

```python
import jax
import jax.numpy as jnp
import numpy as np
from jax import lax
from jax.experimental import pallas as pl
from jax.experimental.pallas import tpu as pltpu
from jax.sharding import PartitionSpec as P

BF = jnp.bfloat16
F32 = jnp.float32
ANY = pl.BlockSpec(memory_space=pl.ANY)
VMEM = pl.BlockSpec(memory_space=pltpu.VMEM)
SMEM = pl.BlockSpec(memory_space=pltpu.SMEM)
NT = (((1,), (1,)), ((), ()))


def rank_within(keys, order):
    earlier = (keys[None, :] == keys[:, None]) & (order[None, :] < order[:, None])
    return jnp.sum(earlier.astype(jnp.int32), axis=1)


def pack_states(source, store, swap, slots):
    sessions, width = store.shape
    lines = width // 128

    def kernel(source, store, swap, out, held):
        for part in range(4):
            base = part * 16 * 128
            stacked = jnp.concatenate(
                [store[:, base + j * 128 : base + (j + 1) * 128] for j in range(16)], axis=0
            )
            turned = jnp.dot(swap[...], stacked, preferred_element_type=F32).astype(BF)
            for r in range(sessions):
                held[r, part * 16 : (part + 1) * 16, :] = turned[r * 16 : (r + 1) * 16]
        for n in range(slots):
            out[n] = held[source[n]]

    return pl.pallas_call(
        kernel,
        grid=(lines // 64,),
        out_shape=jax.ShapeDtypeStruct((slots, lines, 128), BF),
        in_specs=[
            SMEM,
            pl.BlockSpec((sessions, 64 * 128), lambda j: (0, j)),
            pl.BlockSpec(swap.shape, lambda j: (0, 0)),
        ],
        out_specs=pl.BlockSpec((slots, 64, 128), lambda j: (0, j, 0)),
        scratch_shapes=[pltpu.VMEM((sessions, 64, 128), BF)],
        compiler_params=pltpu.CompilerParams(vmem_limit_bytes=16 * 2**20),
        cost_estimate=pl.CostEstimate(
            flops=2 * 256 * 256 * width // 16, bytes_accessed=4 * 2**20, transcendentals=0
        ),
        name="pack_states",
    )(source, store, swap)


def gather_states(index, returned, swap):
    sessions = index.shape[0]
    slots, lines, lanes = returned.shape

    def kernel(index, returned, swap, out):
        for part in range(4):
            rows = slice(part * 16, (part + 1) * 16)
            stacked = jnp.concatenate(
                [returned[index[r], rows, :] for r in range(sessions)], axis=0
            )
            turned = lax.dot_general(
                swap[...], stacked, (((0,), (0,)), ((), ())), preferred_element_type=F32
            ).astype(BF)
            for j in range(16):
                column = (part * 16 + j) * 128
                out[:, column : column + 128] = turned[j * sessions : (j + 1) * sessions]

    return pl.pallas_call(
        kernel,
        grid=(lines // 64,),
        out_shape=jax.ShapeDtypeStruct((sessions, lines * lanes), BF),
        in_specs=[
            SMEM,
            pl.BlockSpec((slots, 64, lanes), lambda j: (0, j, 0)),
            pl.BlockSpec(swap.shape, lambda j: (0, 0)),
        ],
        out_specs=pl.BlockSpec((sessions, 64 * lanes), lambda j: (0, j)),
        compiler_params=pltpu.CompilerParams(vmem_limit_bytes=16 * 2**20),
        cost_estimate=pl.CostEstimate(flops=0, bytes_accessed=2 * 2**20, transcendentals=0),
        name="gather_states",
    )(index, returned, swap)


def project(me, pieces, weight, columns):
    depth = pieces[0].shape[1]
    total = None
    for k in range(4):
        first = pl.multiple_of((me ^ k) * depth, depth)
        part = jnp.dot(
            pieces[k][...], weight[pl.ds(first, depth), columns], preferred_element_type=F32
        )
        total = part if total is None else total + part
    return total


def state_kernel(
    heads, span, pairs, half, meta, own, sibling, across, far, xw, bw, small, s0, s1, *refs
):
    xs, bc_out, steps_out, totals_out, outgoing, fresh, sems = refs[-7:]
    me = meta[0]
    step = pl.program_id(0)
    target = me ^ step
    pieces = (own, sibling, across, far)
    quads = heads // 4
    states = (s0, s1)
    bcs = project(me, pieces, bw, slice(None))
    for quad in range(quads):
        columns = slice(quad * 256, quad * 256 + 256)
        xs[:, columns] = project(me, pieces, xw, columns).astype(BF)
    bc_out[...] = bcs[:, :128].astype(BF)

    lane = lax.broadcasted_iota(jnp.int32, (span, 128), 1)
    low = lane < 64
    lane8 = lax.broadcasted_iota(jnp.int32, (heads, span), 1)
    lane_all = lax.broadcasted_iota(jnp.int32, (heads * pairs, span), 1)
    first_session = (target * 2 + half) * pairs
    raw = jnp.concatenate(
        [
            jnp.transpose(bcs[i * span : (i + 1) * span, 128:256])[:heads] + small[:, 0:1]
            for i in range(pairs)
        ],
        axis=0,
    )
    counts_at = 1 + meta.shape[0] // 2
    alive = jnp.concatenate(
        [(lane8 < meta[counts_at + first_session + i]).astype(F32) for i in range(pairs)], axis=0
    )
    steps = (jnp.maximum(raw, 0.0) + jnp.log1p(jnp.exp(-jnp.abs(raw)))) * alive
    totals = steps * jnp.concatenate([small[:, 1:2]] * pairs, axis=0)
    shift = 1
    while shift < span:
        totals = totals + jnp.where(lane_all >= shift, pltpu.roll(totals, shift, 1), 0.0)
        shift *= 2
    steps_out[...] = steps
    totals_out[...] = totals
    lasts = totals[:, span - 1 : span]
    weight_rows = jnp.exp(jnp.minimum(totals - lasts, 0.0)) * steps
    kept = jnp.exp(-lasts)

    for i in range(pairs):
        rows = slice(i * span, (i + 1) * span)
        bc = bcs[rows, 0:128]
        b_low = jnp.where(low, bc, 0.0).astype(BF)
        b_high = jnp.where(low, 0.0, pltpu.roll(bc, 64, 1)).astype(BF)
        b_both = jnp.concatenate([b_low, b_high], axis=0)
        for quad in range(quads):
            head = i * heads + quad * 4
            scale = jnp.concatenate(
                [
                    jnp.broadcast_to(weight_rows[head + k : head + k + 1, :], (32, span))
                    for k in range(4)
                ],
                axis=0,
            )
            x = xs[rows, quad * 256 : quad * 256 + 256].astype(F32)
            even = (jnp.transpose(x[:, :128]) * scale).astype(BF)
            odd = (jnp.transpose(x[:, 128:]) * scale).astype(BF)
            added = jnp.dot(
                jnp.concatenate([even, odd], axis=1), b_both, preferred_element_type=F32
            )
            keep = jnp.concatenate(
                [
                    jnp.broadcast_to(kept[head + k : head + k + 1, :], (32, 128))
                    for k in range(4)
                ],
                axis=0,
            )
            part = slice(quad * 128, quad * 128 + 128)
            fresh[step * pairs + i, part, :] = (
                keep * states[i][part, :].astype(F32) + added
            ).astype(BF)

    def sending(at, i):
        session = ((me ^ at) * 2 + half) * pairs + i
        number = at * pairs + i
        return pltpu.make_async_copy(
            fresh.at[number], outgoing.at[meta[1 + session]], sems.at[number]
        )

    for i in range(pairs):
        sending(step, i).start()

    @pl.when(step == 3)
    def _():
        for at in range(4):
            for i in range(pairs):
                sending(at, i).wait()


def scan_kernel(
    heads, span, pairs, half, meta, own, sibling, across, far, zw, gain, order, xs, bcs,
    steps_in, totals_in, s0, s1, n0, n1, n2, n3, zs,
):
    normed_out = (n0, n1, n2, n3)
    me = meta[0]
    step = pl.program_id(0)
    target = me ^ step
    pieces = (own, sibling, across, far)
    quads = heads // 4
    states = (s0, s1)
    for quad in range(quads):
        columns = slice(quad * 256, quad * 256 + 256)
        zs[:, columns] = project(me, pieces, zw, columns).astype(BF)

    lane = lax.broadcasted_iota(jnp.int32, (span, 128), 1)
    row = lax.broadcasted_iota(jnp.int32, (span, 128), 0)
    low = lane < 64
    causal = row >= lane
    head_masks = []
    for k in range(4):
        mask = (lane // 32 == k).astype(F32).astype(BF)
        head_masks.append(jnp.concatenate([mask, mask], axis=1))
    steps = steps_in[...]
    totals = totals_in[...]
    cum = jnp.transpose(
        jnp.concatenate([totals, jnp.zeros((128 - heads * pairs, span), F32)], axis=0)
    )
    counts_at = 1 + meta.shape[0] // 2
    for i in range(pairs):
        rows = slice(i * span, (i + 1) * span)
        count = meta[counts_at + (target * 2 + half) * pairs + i]
        bc = bcs[rows, :].astype(F32)
        turned = pltpu.roll(bc, 64, 1)
        b_low = jnp.where(low, bc, 0.0).astype(BF)
        c_low = jnp.where(low, turned, 0.0).astype(BF)
        c_high = jnp.where(low, 0.0, bc).astype(BF)
        scores = lax.dot_general(c_low, b_low, NT, preferred_element_type=F32)
        scores = jnp.where(causal, scores, 0.0)
        carried = lax.dot_general(
            jnp.concatenate([c_low, c_high], axis=0),
            states[i][...],
            NT,
            preferred_element_type=F32,
        )
        gated = []
        squares = None
        for quad in range(quads):
            columns = slice(quad * 256, quad * 256 + 256)
            part = slice(quad * 128, quad * 128 + 128)
            x = xs[rows, columns]
            mixes = []
            spread = None
            for k in range(4):
                head = i * heads + quad * 4 + k
                level = jnp.broadcast_to(cum[:, head : head + 1], (span, 128))
                gap = jnp.minimum(totals[head : head + 1, :] - level, 0.0)
                mixes.append((jnp.exp(gap) * steps[head : head + 1, :] * scores).astype(BF))
                spread = level if spread is None else jnp.where(lane >= 32 * k, level, spread)
            diagonal = jnp.dot(
                jnp.concatenate(mixes, axis=1),
                jnp.concatenate([x * head_masks[k] for k in range(4)], axis=0),
                preferred_element_type=F32,
            )
            fade = jnp.exp(-spread)
            before = jnp.concatenate(
                [carried[:span, part] * fade, carried[span:, part] * fade], axis=1
            )
            gate = zs[rows, columns].astype(F32)
            value = (diagonal + before) * (gate * (0.5 + 0.5 * jnp.tanh(0.5 * gate)))
            gated.append(value)
            own_squares = jnp.sum(value * value, axis=1, keepdims=True)
            squares = own_squares if squares is None else squares + own_squares
        inverse = lax.rsqrt(squares * (1.0 / (heads * 64)) + 1e-05)
        inverse = jnp.where(row[:, :1] < count, inverse, 0.0)
        for quad in range(quads):
            columns = slice(quad * 256, quad * 256 + 256)
            normed = (gated[quad] * inverse * gain[:, columns]).astype(BF)
            zs[rows, columns] = lax.dot_general(
                normed, order[...], NT, preferred_element_type=F32
            ).astype(BF)
    for d in range(4):

        @pl.when(step == d)
        def _():
            normed_out[d][...] = zs[...]


def whole(array):
    return pl.BlockSpec(array.shape, lambda i, meta: (0,) * array.ndim)


def token_specs(half, rows, depth):
    def near(i, meta):
        return (meta[0] ^ i, half, 0, 0)

    def arrived(i, meta):
        return (meta[0] ^ i, 0, 0)

    return [pl.BlockSpec((None, None, rows, depth), near)] * 2 + [
        pl.BlockSpec((None, rows, depth), arrived)
    ] * 2


def state_specs(inbound, pairs, half):
    def slot_of(n):
        return lambda i, meta: (meta[1 + ((meta[0] ^ i) * 2 + half) * pairs + n], 0, 0)

    return [pl.BlockSpec((None,) + inbound.shape[1:], slot_of(n)) for n in range(pairs)]


def by_step(shape, dtype=None):
    return pl.BlockSpec((None,) + tuple(shape), lambda i, meta: (i,) + (0,) * len(shape))


def state_call(half, meta, pieces, xw, bw, small, inbound, span, earlier):
    rows, depth = pieces[2].shape[1:]
    pairs = rows // span
    heads = small.shape[0]
    width = xw.shape[1]
    operands = [meta, *pieces, xw, bw, small] + [inbound] * pairs
    aliases = {}
    extra = []
    if earlier is not None:
        aliases = {len(operands): 4}
        operands.append(earlier)
        extra = [ANY]
    return pl.pallas_call(
        lambda *refs: state_kernel(heads, span, pairs, half, *refs),
        out_shape=[
            jax.ShapeDtypeStruct((4, rows, width), BF),
            jax.ShapeDtypeStruct((4, rows, 128), BF),
            jax.ShapeDtypeStruct((4, heads * pairs, span), F32),
            jax.ShapeDtypeStruct((4, heads * pairs, span), F32),
            jax.ShapeDtypeStruct(inbound.shape, BF),
        ],
        grid_spec=pltpu.PrefetchScalarGridSpec(
            num_scalar_prefetch=1,
            grid=(4,),
            in_specs=token_specs(half, rows, depth)
            + [whole(xw), whole(bw), whole(small)]
            + state_specs(inbound, pairs, half)
            + extra,
            out_specs=[
                by_step((rows, width)),
                by_step((rows, 128)),
                by_step((heads * pairs, span)),
                by_step((heads * pairs, span)),
                ANY,
            ],
            scratch_shapes=[
                pltpu.VMEM((4 * pairs,) + inbound.shape[1:], BF),
                pltpu.SemaphoreType.DMA((4 * pairs,)),
            ],
        ),
        input_output_aliases=aliases,
        compiler_params=pltpu.CompilerParams(vmem_limit_bytes=32 * 2**20),
        cost_estimate=pl.CostEstimate(
            flops=8 * 10**9, bytes_accessed=9 * 2**20, transcendentals=0
        ),
        name="states",
    )(*operands)


def scan_call(half, meta, pieces, zw, gain, order, mid, inbound, span):
    rows, depth = pieces[2].shape[1:]
    pairs = rows // span
    xs, bcs, steps, totals = mid
    heads = steps.shape[1] // pairs
    width = zw.shape[1]
    return pl.pallas_call(
        lambda *refs: scan_kernel(heads, span, pairs, half, *refs),
        out_shape=[jax.ShapeDtypeStruct((rows, width), BF)] * 4,
        grid_spec=pltpu.PrefetchScalarGridSpec(
            num_scalar_prefetch=1,
            grid=(4,),
            in_specs=token_specs(half, rows, depth)
            + [whole(zw), whole(gain), whole(order)]
            + [by_step(part.shape[1:]) for part in mid]
            + state_specs(inbound, pairs, half),
            out_specs=[pl.BlockSpec((rows, width), lambda i, meta: (0, 0))] * 4,
            scratch_shapes=[pltpu.VMEM((rows, width), BF)],
        ),
        compiler_params=pltpu.CompilerParams(vmem_limit_bytes=32 * 2**20),
        cost_estimate=pl.CostEstimate(
            flops=10 * 10**9, bytes_accessed=9 * 2**20, transcendentals=0
        ),
        name="scan",
    )(meta, *pieces, zw, gain, order, *mid, *[inbound] * pairs)


def out_call(half, halves, normed, weights, earlier):
    rows, depth = normed[0].shape
    columns = weights[0].shape[1]
    block = 512

    def kernel(*refs):
        out = refs[-1]
        total = None
        for d in range(4):
            part = jnp.dot(refs[d][...], refs[4 + d][...], preferred_element_type=F32)
            total = part if total is None else total + part
        out[...] = total.astype(BF)

    operands = [*normed, *weights]
    extra = []
    aliases = {}
    if earlier is not None:
        aliases = {len(operands): 0}
        operands.append(earlier)
        extra = [ANY]
    return pl.pallas_call(
        kernel,
        grid=(columns // block,),
        out_shape=jax.ShapeDtypeStruct((halves * rows, columns), BF),
        in_specs=[pl.BlockSpec((rows, depth), lambda j: (0, 0))] * 4
        + [pl.BlockSpec((depth, block), lambda j: (0, j))] * 4
        + extra,
        out_specs=pl.BlockSpec((rows, block), lambda j: (half, j)),
        input_output_aliases=aliases,
        compiler_params=pltpu.CompilerParams(vmem_limit_bytes=24 * 2**20),
        cost_estimate=pl.CostEstimate(
            flops=2 * rows * depth * 4 * columns, bytes_accessed=10 * 2**20, transcendentals=0
        ),
        name="project_out",
    )(*operands)


def after(value, *others):
    return lax.optimization_barrier((value,) + others)[0]


def body(
    tokens,
    x_weight,
    z_weight,
    bc_weight,
    dt_weight,
    dt_bias,
    decay_rate,
    norm_gain,
    out_weight,
    store_states,
    home_rows,
    event_counts,
):
    shard_count = lax.axis_size("dp")
    model_shards = lax.axis_size("mp")
    shard_index = lax.axis_index("dp")
    me = lax.axis_index("mp")
    sessions_here, state_width = store_states.shape
    heads = dt_bias.shape[0]
    width = x_weight.shape[1]
    depth = tokens.shape[1]
    span = tokens.shape[0] // sessions_here
    halves = 2
    rows = tokens.shape[0] // (model_shards * halves)
    capacity = max(2, (sessions_here + shard_count - 1) // shard_count)
    slot_count = shard_count * capacity
    row_shape = (state_width // 128, 128)

    def exchange(value, distance):
        pairs = [(j, j ^ distance) for j in range(model_shards)]
        return lax.ppermute(value, "mp", pairs)

    def trade(value):
        return lax.all_to_all(
            value.reshape((shard_count, capacity) + row_shape),
            "dp",
            split_axis=0,
            concat_axis=0,
            tiled=True,
        ).reshape((slot_count,) + row_shape)

    blocks = tokens.reshape(model_shards, halves, rows, depth)
    across = [exchange(blocks[:, h], 2) for h in range(halves)]
    sibling = exchange(tokens, 1).reshape(blocks.shape)
    replicas = lax.axis_size("groups") * shard_count
    replica = lax.axis_index("groups") * shard_count + shard_index
    share = width // replicas
    ow_part = exchange(lax.dynamic_slice_in_dim(out_weight, replica * share, share), 2)

    local = jnp.arange(sessions_here, dtype=jnp.int32)
    store_rows = shard_index * sessions_here + local
    everyone = jnp.arange(home_rows.shape[0], dtype=jnp.int32)
    owner = jnp.sum(
        jnp.where(home_rows[None, :] == store_rows[:, None], everyone[None, :], 0), axis=1
    )
    server = owner // sessions_here
    row_slot = server * capacity + rank_within(server, local)
    wanted_slots = jnp.arange(slot_count, dtype=jnp.int32)
    source = jnp.sum(
        jnp.where(row_slot[None, :] == wanted_slots[:, None], local[None, :], 0), axis=1
    )
    swap_row = np.arange(sessions_here * 16)
    swap = jnp.asarray(
        (swap_row % 16 * sessions_here + swap_row // 16)[:, None] == swap_row[None, :], BF
    )
    packed = pack_states(source, store_states, swap, slot_count)
    inbound = trade(packed)
    wanted = lax.dynamic_slice_in_dim(home_rows, shard_index * sessions_here, sessions_here)
    home_shard = wanted // sessions_here
    session_slot = home_shard * capacity + rank_within(home_shard, wanted % sessions_here)
    meta = jnp.concatenate([me.reshape(1).astype(jnp.int32), session_slot, event_counts])

    new_column = np.arange(width)
    old_column = (
        new_column // 256 * 256
        + new_column // 32 % 4 * 64
        + new_column % 32 * 2
        + new_column // 128 % 2
    )
    turn = jnp.asarray(old_column[None, :] == np.arange(width)[:, None], BF)
    xw = jnp.dot(x_weight, turn, preferred_element_type=F32).astype(BF)
    zw = jnp.dot(z_weight, turn, preferred_element_type=F32).astype(BF)
    order = turn[:256, :256]
    bw = jnp.concatenate(
        [bc_weight, dt_weight, jnp.zeros((bc_weight.shape[0], 128 - heads), BF)], axis=1
    )
    gain = norm_gain.reshape(heads // 4, 4, 32, 2).transpose(0, 3, 1, 2).reshape(1, width)
    small = jnp.stack([dt_bias, decay_rate], axis=1)

    ow_part = after(ow_part, packed)
    ow_across = lax.all_gather(ow_part, ("groups", "dp"), axis=0, tiled=True)
    ow_sibling = exchange(out_weight, 1)
    ow_far = exchange(ow_across, 1)

    outgoing = None
    received = []
    done = []
    for h in range(halves):
        arrived = across[h]
        turn_meta = meta
        if h:
            turn_meta = after(meta, done[-1])
            arrived = after(arrived, done[-1])
        pieces = (blocks, sibling, arrived, exchange(arrived, 1))
        *mid, outgoing = state_call(
            h, turn_meta, pieces, xw, bw, small, inbound, span, outgoing
        )
        parts = scan_call(h, turn_meta, pieces, zw, gain, order, mid, inbound, span)
        done.append(parts[0])
        received.append([parts[0]] + [exchange(parts[d], d) for d in range(1, 4)])
    returned = trade(outgoing)
    new_store = gather_states(row_slot, returned, swap)
    ow = (out_weight, ow_sibling, ow_across, ow_far)
    out_tokens = None
    for h in range(halves):
        normed = list(received[h])
        if h == 0:
            normed[0] = after(normed[0], done[-1])
        out_tokens = out_call(h, halves, normed, ow, out_tokens)
    return (out_tokens, new_store)


def solution(mesh):
    return jax.shard_map(
        body,
        mesh=mesh,
        in_specs=(
            P(("groups", "dp"), "mp"),
            P(None, "mp"),
            P(None, "mp"),
            P(None, "mp"),
            P(None, "mp"),
            P("mp"),
            P("mp"),
            P("mp"),
            P("mp", None),
            P(("groups", "dp"), "mp"),
            P("groups"),
            P(("groups", "dp")),
        ),
        out_specs=(P(("groups", "dp", "mp"), None), P(("groups", "dp"), "mp")),
        check_vma=False,
    )
```

```python
import jax
import jax.numpy as jnp
import numpy as np
from jax import lax
from jax.experimental import pallas as pl
from jax.experimental.pallas import tpu as pltpu
from jax.sharding import PartitionSpec as P

BF = jnp.bfloat16
F32 = jnp.float32
ANY = pl.BlockSpec(memory_space=pl.ANY)
VMEM = pl.BlockSpec(memory_space=pltpu.VMEM)
SMEM = pl.BlockSpec(memory_space=pltpu.SMEM)
NT = (((1,), (1,)), ((), ()))
VMEM_LIMIT = 58 * 2**20


def rank_within(keys, order):
    earlier = (keys[None, :] == keys[:, None]) & (order[None, :] < order[:, None])
    return jnp.sum(earlier.astype(jnp.int32), axis=1)


def pack_states(source, store, swap, slots):
    sessions, width = store.shape
    lines = width // 128

    def kernel(source, store, swap, out, held):
        for part in range(4):
            base = part * 16 * 128
            stacked = jnp.concatenate(
                [store[:, base + j * 128 : base + (j + 1) * 128] for j in range(16)], axis=0
            )
            turned = jnp.dot(swap[...], stacked, preferred_element_type=F32).astype(BF)
            for r in range(sessions):
                held[r, part * 16 : (part + 1) * 16, :] = turned[r * 16 : (r + 1) * 16]
        for n in range(slots):
            out[n] = held[source[n]]

    return pl.pallas_call(
        kernel,
        grid=(lines // 64,),
        out_shape=jax.ShapeDtypeStruct((slots, lines, 128), BF),
        in_specs=[
            SMEM,
            pl.BlockSpec((sessions, 64 * 128), lambda j: (0, j)),
            pl.BlockSpec(swap.shape, lambda j: (0, 0)),
        ],
        out_specs=pl.BlockSpec((slots, 64, 128), lambda j: (0, j, 0)),
        scratch_shapes=[pltpu.VMEM((sessions, 64, 128), BF)],
        compiler_params=pltpu.CompilerParams(vmem_limit_bytes=VMEM_LIMIT),
        cost_estimate=pl.CostEstimate(
            flops=1, bytes_accessed=1, transcendentals=0
        ),
        name="pack_states",
    )(source, store, swap)


def gather_states(index, returned, swap):
    sessions = index.shape[0]
    slots, lines, lanes = returned.shape

    def kernel(index, returned, swap, out):
        for part in range(4):
            rows = slice(part * 16, (part + 1) * 16)
            stacked = jnp.concatenate(
                [returned[index[r], rows, :] for r in range(sessions)], axis=0
            )
            turned = lax.dot_general(
                swap[...], stacked, (((0,), (0,)), ((), ())), preferred_element_type=F32
            ).astype(BF)
            for j in range(16):
                column = (part * 16 + j) * 128
                out[:, column : column + 128] = turned[j * sessions : (j + 1) * sessions]

    return pl.pallas_call(
        kernel,
        grid=(lines // 64,),
        out_shape=jax.ShapeDtypeStruct((sessions, lines * lanes), BF),
        in_specs=[
            SMEM,
            pl.BlockSpec((slots, 64, lanes), lambda j: (0, j, 0)),
            pl.BlockSpec(swap.shape, lambda j: (0, 0)),
        ],
        out_specs=pl.BlockSpec((sessions, 64 * lanes), lambda j: (0, j)),
        compiler_params=pltpu.CompilerParams(vmem_limit_bytes=VMEM_LIMIT),
        cost_estimate=pl.CostEstimate(flops=1, bytes_accessed=1, transcendentals=0),
        name="gather_states",
    )(index, returned, swap)


def project(me, pieces, weight, columns):
    depth = pieces[0].shape[1]
    total = None
    for k in range(4):
        first = pl.multiple_of((me ^ k) * depth, depth)
        part = jnp.dot(
            pieces[k][...], weight[pl.ds(first, depth), columns], preferred_element_type=F32
        )
        total = part if total is None else total + part
    return total


def state_kernel(
    heads, span, pairs, half, meta, own, sibling, across, far, bw, xw, zw, small, s0, s1, s2, s3,
    *refs
):
    xs, zs, bc_out, steps_out, totals_out, outgoing, fresh, sems = refs[-8:]
    me = meta[0]
    step = pl.program_id(0)
    side = (me // 2) ^ 1 ^ step
    count = 2 * pairs
    rows_all = count * span
    depth = across.shape[-1]
    pieces = [piece[...].reshape(rows_all, depth) for piece in (own, sibling, across, far)]
    quads = heads // 4
    states = (s0, s1, s2, s3)

    def session_of(at, n):
        return ((((me // 2) ^ 1 ^ at) * 2 + n // pairs) * 2 + half) * pairs + n % pairs

    bcs = project(me, pieces, bw, slice(None))
    for quad in range(quads):
        columns = slice(quad * 256, quad * 256 + 256)
        xs[:, columns] = project(me, pieces, xw, columns).astype(BF)
        zs[:, columns] = project(me, pieces, zw, columns).astype(BF)
    bc_out[...] = bcs[:, :128].astype(BF)

    lane = lax.broadcasted_iota(jnp.int32, (span, 128), 1)
    low = lane < 64
    lane8 = lax.broadcasted_iota(jnp.int32, (heads, span), 1)
    lane_all = lax.broadcasted_iota(jnp.int32, (heads * count, span), 1)
    raw = jnp.concatenate(
        [
            jnp.transpose(bcs[n * span : (n + 1) * span, 128:256])[:heads] + small[:, 0:1]
            for n in range(count)
        ],
        axis=0,
    )
    counts_at = 1 + meta.shape[0] // 2
    alive = jnp.concatenate(
        [(lane8 < meta[counts_at + session_of(step, n)]).astype(F32) for n in range(count)],
        axis=0,
    )
    steps = (jnp.maximum(raw, 0.0) + jnp.log1p(jnp.exp(-jnp.abs(raw)))) * alive
    totals = steps * jnp.concatenate([small[:, 1:2]] * count, axis=0)
    shift = 1
    while shift < span:
        totals = totals + jnp.where(lane_all >= shift, pltpu.roll(totals, shift, 1), 0.0)
        shift *= 2
    steps_out[...] = steps
    totals_out[...] = totals
    lasts = totals[:, span - 1 : span]
    weight_rows = jnp.exp(jnp.minimum(totals - lasts, 0.0)) * steps
    kept = jnp.exp(-lasts)

    for n in range(count):
        rows = slice(n * span, (n + 1) * span)
        bc = bcs[rows, 0:128]
        b_low = jnp.where(low, bc, 0.0).astype(BF)
        b_high = jnp.where(low, 0.0, pltpu.roll(bc, 64, 1)).astype(BF)
        b_both = jnp.concatenate([b_low, b_high], axis=0)
        for quad in range(quads):
            head = n * heads + quad * 4
            scale = jnp.concatenate(
                [
                    jnp.broadcast_to(weight_rows[head + k : head + k + 1, :], (32, span))
                    for k in range(4)
                ],
                axis=0,
            )
            x = xs[rows, quad * 256 : quad * 256 + 256].astype(F32)
            even = (jnp.transpose(x[:, :128]) * scale).astype(BF)
            odd = (jnp.transpose(x[:, 128:]) * scale).astype(BF)
            added = jnp.dot(
                jnp.concatenate([even, odd], axis=1), b_both, preferred_element_type=F32
            )
            keep = jnp.concatenate(
                [
                    jnp.broadcast_to(kept[head + k : head + k + 1, :], (32, 128))
                    for k in range(4)
                ],
                axis=0,
            )
            part = slice(quad * 128, quad * 128 + 128)
            fresh[step * count + n, part, :] = (
                keep * states[n][part, :].astype(F32) + added
            ).astype(BF)

    def sending(at, n):
        number = at * count + n
        return pltpu.make_async_copy(
            fresh.at[number], outgoing.at[meta[1 + session_of(at, n)]], sems.at[number]
        )

    for n in range(count):
        sending(step, n).start()

    @pl.when(step == 1)
    def _():
        for at in range(2):
            for n in range(count):
                sending(at, n).wait()


def scan_kernel(
    heads, span, pairs, half, side, meta, gain, order, xs, zs, bcs, steps_in, totals_in, s0, s1,
    na, nb, result,
):
    me = meta[0]
    step = pl.program_id(0)
    target = me ^ (2 * (1 - side) + step)
    quads = heads // 4
    states = (s0, s1)
    lane = lax.broadcasted_iota(jnp.int32, (span, 128), 1)
    row = lax.broadcasted_iota(jnp.int32, (span, 128), 0)
    low = lane < 64
    causal = row >= lane
    head_masks = []
    for k in range(4):
        mask = (lane // 32 == k).astype(F32).astype(BF)
        head_masks.append(jnp.concatenate([mask, mask], axis=1))
    steps = steps_in[...]
    totals = totals_in[...]
    cum = jnp.transpose(
        jnp.concatenate([totals, jnp.zeros((128 - heads * pairs, span), F32)], axis=0)
    )
    counts_at = 1 + meta.shape[0] // 2
    for i in range(pairs):
        rows = slice(i * span, (i + 1) * span)
        count = meta[counts_at + (target * 2 + half) * pairs + i]
        bc = bcs[rows, :].astype(F32)
        turned = pltpu.roll(bc, 64, 1)
        b_low = jnp.where(low, bc, 0.0).astype(BF)
        c_low = jnp.where(low, turned, 0.0).astype(BF)
        c_high = jnp.where(low, 0.0, bc).astype(BF)
        scores = lax.dot_general(c_low, b_low, NT, preferred_element_type=F32)
        scores = jnp.where(causal, scores, 0.0)
        carried = lax.dot_general(
            jnp.concatenate([c_low, c_high], axis=0),
            states[i][...],
            NT,
            preferred_element_type=F32,
        )
        gated = []
        squares = None
        for quad in range(quads):
            columns = slice(quad * 256, quad * 256 + 256)
            part = slice(quad * 128, quad * 128 + 128)
            x = xs[rows, columns]
            mixes = []
            spread = None
            for k in range(4):
                head = i * heads + quad * 4 + k
                level = jnp.broadcast_to(cum[:, head : head + 1], (span, 128))
                gap = jnp.minimum(totals[head : head + 1, :] - level, 0.0)
                mixes.append((jnp.exp(gap) * steps[head : head + 1, :] * scores).astype(BF))
                spread = level if spread is None else jnp.where(lane >= 32 * k, level, spread)
            diagonal = jnp.dot(
                jnp.concatenate(mixes, axis=1),
                jnp.concatenate([x * head_masks[k] for k in range(4)], axis=0),
                preferred_element_type=F32,
            )
            fade = jnp.exp(-spread)
            before = jnp.concatenate(
                [carried[:span, part] * fade, carried[span:, part] * fade], axis=1
            )
            gate = zs[rows, columns].astype(F32)
            value = (diagonal + before) * (gate * (0.5 + 0.5 * jnp.tanh(0.5 * gate)))
            gated.append(value)
            own_squares = jnp.sum(value * value, axis=1, keepdims=True)
            squares = own_squares if squares is None else squares + own_squares
        inverse = lax.rsqrt(squares * (1.0 / (heads * 64)) + 1e-05)
        inverse = jnp.where(row[:, :1] < count, inverse, 0.0)
        for quad in range(quads):
            columns = slice(quad * 256, quad * 256 + 256)
            normed = (gated[quad] * inverse * gain[:, columns]).astype(BF)
            result[rows, columns] = lax.dot_general(
                normed, order[...], NT, preferred_element_type=F32
            ).astype(BF)

    @pl.when(step == 0)
    def _():
        na[...] = result[...]

    @pl.when(step == 1)
    def _():
        nb[...] = result[...]


def whole(array):
    return pl.BlockSpec(array.shape, lambda i, meta: (0,) * array.ndim)


def state_call(half, meta, pieces, weights, small, inbound, span, earlier):
    rows, depth = pieces[2].shape[-2:]
    pairs = rows // span
    count = 2 * pairs
    heads = small.shape[0]
    width = weights[1].shape[1]

    def near(i, meta):
        return ((meta[0] // 2) ^ 1 ^ i, 0, half, 0, 0)

    def arrived(i, meta):
        return ((meta[0] // 2) ^ 1 ^ i, 0, 0, 0)

    def slot_of(n):
        def index(i, meta):
            target = ((meta[0] // 2) ^ 1 ^ i) * 2 + n // pairs
            return (meta[1 + (target * 2 + half) * pairs + n % pairs], 0, 0)

        return index

    def by_step(shape):
        return pl.BlockSpec((None,) + shape, lambda i, meta: (i, 0, 0))

    operands = [meta, *pieces, *weights, small] + [inbound] * count
    aliases = {}
    extra = []
    if earlier is not None:
        aliases = {len(operands): 5}
        operands.append(earlier)
        extra = [ANY]
    return pl.pallas_call(
        lambda *refs: state_kernel(heads, span, pairs, half, *refs),
        out_shape=[
            jax.ShapeDtypeStruct((2, count * span, width), BF),
            jax.ShapeDtypeStruct((2, count * span, width), BF),
            jax.ShapeDtypeStruct((2, count * span, 128), BF),
            jax.ShapeDtypeStruct((2, heads * count, span), F32),
            jax.ShapeDtypeStruct((2, heads * count, span), F32),
            jax.ShapeDtypeStruct(inbound.shape, BF),
        ],
        grid_spec=pltpu.PrefetchScalarGridSpec(
            num_scalar_prefetch=1,
            grid=(2,),
            in_specs=[pl.BlockSpec((None, 2, None, rows, depth), near)] * 2
            + [pl.BlockSpec((None, 2, rows, depth), arrived)] * 2
            + [whole(weight) for weight in weights]
            + [whole(small)]
            + [pl.BlockSpec((None,) + inbound.shape[1:], slot_of(n)) for n in range(count)]
            + extra,
            out_specs=[
                by_step((count * span, width)),
                by_step((count * span, width)),
                by_step((count * span, 128)),
                by_step((heads * count, span)),
                by_step((heads * count, span)),
                ANY,
            ],
            scratch_shapes=[
                pltpu.VMEM((2 * count,) + inbound.shape[1:], BF),
                pltpu.SemaphoreType.DMA((2 * count,)),
            ],
        ),
        input_output_aliases=aliases,
        compiler_params=pltpu.CompilerParams(vmem_limit_bytes=VMEM_LIMIT),
        cost_estimate=pl.CostEstimate(
            flops=1, bytes_accessed=1, transcendentals=0
        ),
        name="states",
    )(*operands)


def scan_call(half, side, meta, gain, order, mid, inbound, span, rows):
    pairs = rows // span
    heads = mid[-1].shape[1] // (2 * pairs)
    width = mid[0].shape[2]
    mid = [part.reshape(2, 2, part.shape[1] // 2, part.shape[2]) for part in mid]

    def block_of(part):
        return pl.BlockSpec(
            (None, None) + part.shape[2:], lambda i, meta: (side, i ^ (meta[0] % 2), 0, 0)
        )

    def slot_of(n):
        def index(i, meta):
            target = meta[0] ^ (2 * (1 - side) + i)
            return (meta[1 + (target * 2 + half) * pairs + n], 0, 0)

        return index

    return pl.pallas_call(
        lambda *refs: scan_kernel(heads, span, pairs, half, side, *refs),
        out_shape=[jax.ShapeDtypeStruct((rows, width), BF)] * 2,
        grid_spec=pltpu.PrefetchScalarGridSpec(
            num_scalar_prefetch=1,
            grid=(2,),
            in_specs=[whole(gain), whole(order)]
            + [block_of(part) for part in mid]
            + [pl.BlockSpec((None,) + inbound.shape[1:], slot_of(n)) for n in range(pairs)],
            out_specs=[pl.BlockSpec((rows, width), lambda i, meta: (0, 0))] * 2,
            scratch_shapes=[pltpu.VMEM((rows, width), BF)],
        ),
        compiler_params=pltpu.CompilerParams(vmem_limit_bytes=VMEM_LIMIT),
        cost_estimate=pl.CostEstimate(
            flops=1, bytes_accessed=1, transcendentals=0
        ),
        name="scan",
    )(meta, gain, order, *mid, *[inbound] * pairs)


def out_call(half, halves, normed, weights, earlier):
    rows, depth = normed[0].shape
    columns = weights[0].shape[1]
    block = 512

    def kernel(*refs):
        out = refs[-1]
        total = None
        for d in range(4):
            part = jnp.dot(refs[d][...], refs[4 + d][...], preferred_element_type=F32)
            total = part if total is None else total + part
        out[...] = total.astype(BF)

    operands = [*normed, *weights]
    extra = []
    aliases = {}
    if earlier is not None:
        aliases = {len(operands): 0}
        operands.append(earlier)
        extra = [ANY]
    return pl.pallas_call(
        kernel,
        grid=(columns // block,),
        out_shape=jax.ShapeDtypeStruct((halves * rows, columns), BF),
        in_specs=[pl.BlockSpec((rows, depth), lambda j: (0, 0))] * 4
        + [pl.BlockSpec((depth, block), lambda j: (0, j))] * 4
        + extra,
        out_specs=pl.BlockSpec((rows, block), lambda j: (half, j)),
        input_output_aliases=aliases,
        compiler_params=pltpu.CompilerParams(vmem_limit_bytes=VMEM_LIMIT),
        cost_estimate=pl.CostEstimate(
            flops=1, bytes_accessed=1, transcendentals=0
        ),
        name="project_out",
    )(*operands)


def after(value, *others):
    return lax.optimization_barrier((value,) + others)[0]


def body(
    tokens,
    x_weight,
    z_weight,
    bc_weight,
    dt_weight,
    dt_bias,
    decay_rate,
    norm_gain,
    out_weight,
    store_states,
    home_rows,
    event_counts,
):
    shard_count = lax.axis_size("dp")
    model_shards = lax.axis_size("mp")
    shard_index = lax.axis_index("dp")
    me = lax.axis_index("mp")
    sessions_here, state_width = store_states.shape
    heads = dt_bias.shape[0]
    width = x_weight.shape[1]
    depth = tokens.shape[1]
    span = tokens.shape[0] // sessions_here
    halves = 2
    rows = tokens.shape[0] // (model_shards * halves)
    capacity = max(2, (sessions_here + shard_count - 1) // shard_count)
    slot_count = shard_count * capacity
    row_shape = (state_width // 128, 128)

    def exchange(value, distance):
        pairs = [(j, j ^ distance) for j in range(model_shards)]
        return lax.ppermute(value, "mp", pairs)

    def trade(value):
        return lax.all_to_all(
            value.reshape((shard_count, capacity) + row_shape),
            "dp",
            split_axis=0,
            concat_axis=0,
            tiled=True,
        ).reshape((slot_count,) + row_shape)

    replicas = lax.axis_size("groups") * shard_count
    replica = lax.axis_index("groups") * shard_count + shard_index
    share = width // replicas
    ow_part = exchange(lax.dynamic_slice_in_dim(out_weight, replica * share, share), 2)
    blocks = tokens.reshape(model_shards // 2, 2, halves, rows, depth)
    sibling = exchange(tokens, 1).reshape(blocks.shape)

    local = jnp.arange(sessions_here, dtype=jnp.int32)
    store_rows = shard_index * sessions_here + local
    everyone = jnp.arange(home_rows.shape[0], dtype=jnp.int32)
    owner = jnp.sum(
        jnp.where(home_rows[None, :] == store_rows[:, None], everyone[None, :], 0), axis=1
    )
    server = owner // sessions_here
    row_slot = server * capacity + rank_within(server, local)
    wanted_slots = jnp.arange(slot_count, dtype=jnp.int32)
    source = jnp.sum(
        jnp.where(row_slot[None, :] == wanted_slots[:, None], local[None, :], 0), axis=1
    )
    swap_row = np.arange(sessions_here * 16)
    swap = jnp.asarray(
        (swap_row % 16 * sessions_here + swap_row // 16)[:, None] == swap_row[None, :], BF
    )
    packed = pack_states(source, store_states, swap, slot_count)
    inbound = trade(packed)
    first = after(blocks[:, :, 0], ow_part)
    across = [exchange(first, 2)]
    across.append(exchange(after(blocks[:, :, 1], across[0]), 2))
    wanted = lax.dynamic_slice_in_dim(home_rows, shard_index * sessions_here, sessions_here)
    home_shard = wanted // sessions_here
    session_slot = home_shard * capacity + rank_within(home_shard, wanted % sessions_here)
    meta = jnp.concatenate([me.reshape(1).astype(jnp.int32), session_slot, event_counts])

    new_column = np.arange(width)
    old_column = (
        new_column // 256 * 256
        + new_column // 32 % 4 * 64
        + new_column % 32 * 2
        + new_column // 128 % 2
    )
    turn = jnp.asarray(old_column[None, :] == np.arange(width)[:, None], BF)
    xw = jnp.dot(x_weight, turn, preferred_element_type=F32).astype(BF)
    zw = jnp.dot(z_weight, turn, preferred_element_type=F32).astype(BF)
    order = turn[:256, :256]
    bw = jnp.concatenate(
        [bc_weight, dt_weight, jnp.zeros((bc_weight.shape[0], 128 - heads), BF)], axis=1
    )
    gain = norm_gain.reshape(heads // 4, 4, 32, 2).transpose(0, 3, 1, 2).reshape(1, width)
    small = jnp.stack([dt_bias, decay_rate], axis=1)

    ow_across = lax.all_gather(ow_part, ("groups", "dp"), axis=0, tiled=True)
    ow_sibling = exchange(out_weight, 1)

    outgoing = None
    received = []
    done = []
    for h in range(halves):
        arrived = across[h]
        start = meta
        if h:
            start = after(meta, done[-1])
            arrived = after(arrived, mid[0])
        else:
            arrived = after(arrived, xw, zw, bw)
        pieces = (blocks, sibling, arrived, exchange(arrived, 1))
        *mid, outgoing = state_call(
            h, start, pieces, (bw, xw, zw), small, inbound, span, outgoing
        )
        far_part = scan_call(h, 0, start, gain, order, mid, inbound, span, rows)
        start = after(start, far_part[0])
        near_part = scan_call(h, 1, start, gain, order, mid, inbound, span, rows)
        done.append(near_part[0])
        received.append(
            [
                near_part[0],
                exchange(near_part[1], 1),
                exchange(far_part[0], 2),
                exchange(far_part[1], 3),
            ]
        )
    returned = trade(outgoing)
    ow_across = after(ow_across, done[-1])
    ow_far = exchange(ow_across, 1)
    new_store = gather_states(row_slot, returned, swap)
    ow = (out_weight, ow_sibling, ow_across, ow_far)
    out_tokens = None
    for h in range(halves):
        normed = list(received[h])
        if h == 0:
            normed[0] = after(normed[0], done[-1])
        out_tokens = out_call(h, halves, normed, ow, out_tokens)
    return (out_tokens, new_store)


def solution(mesh):
    return jax.shard_map(
        body,
        mesh=mesh,
        in_specs=(
            P(("groups", "dp"), "mp"),
            P(None, "mp"),
            P(None, "mp"),
            P(None, "mp"),
            P(None, "mp"),
            P("mp"),
            P("mp"),
            P("mp"),
            P("mp", None),
            P(("groups", "dp"), "mp"),
            P("groups"),
            P(("groups", "dp")),
        ),
        out_specs=(P(("groups", "dp", "mp"), None), P(("groups", "dp"), "mp")),
        check_vma=False,
    )
```

```python
import jax
import jax.numpy as jnp
import numpy as np
from jax import lax
from jax.experimental import pallas as pl
from jax.experimental.pallas import tpu as pltpu
from jax.sharding import PartitionSpec as P

BF = jnp.bfloat16
F32 = jnp.float32
ANY = pl.BlockSpec(memory_space=pl.ANY)
VMEM = pl.BlockSpec(memory_space=pltpu.VMEM)
SMEM = pl.BlockSpec(memory_space=pltpu.SMEM)
NT = (((1,), (1,)), ((), ()))
VMEM_LIMIT = 58 * 2**20


def rank_within(keys, order):
    earlier = (keys[None, :] == keys[:, None]) & (order[None, :] < order[:, None])
    return jnp.sum(earlier.astype(jnp.int32), axis=1)


def pack_states(source, store, swap, slots):
    sessions, width = store.shape
    lines = width // 128

    def kernel(source, store, swap, out, held):
        for part in range(4):
            base = part * 16 * 128
            stacked = jnp.concatenate(
                [store[:, base + j * 128 : base + (j + 1) * 128] for j in range(16)], axis=0
            )
            turned = jnp.dot(swap[...], stacked, preferred_element_type=F32).astype(BF)
            for r in range(sessions):
                held[r, part * 16 : (part + 1) * 16, :] = turned[r * 16 : (r + 1) * 16]
        for n in range(slots):
            out[n] = held[source[n]]

    return pl.pallas_call(
        kernel,
        grid=(lines // 64,),
        out_shape=jax.ShapeDtypeStruct((slots, lines, 128), BF),
        in_specs=[
            SMEM,
            pl.BlockSpec((sessions, 64 * 128), lambda j: (0, j)),
            pl.BlockSpec(swap.shape, lambda j: (0, 0)),
        ],
        out_specs=pl.BlockSpec((slots, 64, 128), lambda j: (0, j, 0)),
        scratch_shapes=[pltpu.VMEM((sessions, 64, 128), BF)],
        compiler_params=pltpu.CompilerParams(vmem_limit_bytes=VMEM_LIMIT),
        cost_estimate=pl.CostEstimate(
            flops=1, bytes_accessed=1, transcendentals=0
        ),
        name="pack_states",
    )(source, store, swap)


def gather_states(index, returned, swap):
    sessions = index.shape[0]
    slots, lines, lanes = returned.shape

    def kernel(index, returned, swap, out):
        for part in range(4):
            rows = slice(part * 16, (part + 1) * 16)
            stacked = jnp.concatenate(
                [returned[index[r], rows, :] for r in range(sessions)], axis=0
            )
            turned = lax.dot_general(
                swap[...], stacked, (((0,), (0,)), ((), ())), preferred_element_type=F32
            ).astype(BF)
            for j in range(16):
                column = (part * 16 + j) * 128
                out[:, column : column + 128] = turned[j * sessions : (j + 1) * sessions]

    return pl.pallas_call(
        kernel,
        grid=(lines // 64,),
        out_shape=jax.ShapeDtypeStruct((sessions, lines * lanes), BF),
        in_specs=[
            SMEM,
            pl.BlockSpec((slots, 64, lanes), lambda j: (0, j, 0)),
            pl.BlockSpec(swap.shape, lambda j: (0, 0)),
        ],
        out_specs=pl.BlockSpec((sessions, 64 * lanes), lambda j: (0, j)),
        compiler_params=pltpu.CompilerParams(vmem_limit_bytes=VMEM_LIMIT),
        cost_estimate=pl.CostEstimate(flops=1, bytes_accessed=1, transcendentals=0),
        name="gather_states",
    )(index, returned, swap)


def project(me, pieces, weight, columns):
    depth = pieces[0].shape[1]
    total = None
    for k in range(4):
        first = pl.multiple_of((me ^ k) * depth, depth)
        part = jnp.dot(
            pieces[k][...], weight[pl.ds(first, depth), columns], preferred_element_type=F32
        )
        total = part if total is None else total + part
    return total


def state_kernel(
    heads, span, pairs, half, meta, own, sibling, across, far, bw, xw, zw, small, s0, s1, s2, s3,
    *refs
):
    xs, zs, bc_out, steps_out, totals_out, outgoing, fresh, xw_held, zw_held, sems, in_sems = refs[-11:]
    me = meta[0]
    step = pl.program_id(0)
    side = (me // 2) ^ 1 ^ step
    count = 2 * pairs
    rows_all = count * span
    depth = across.shape[-1]
    pieces = [piece[...].reshape(rows_all, depth) for piece in (own, sibling, across, far)]
    quads = heads // 4
    states = (s0, s1, s2, s3)

    def session_of(at, n):
        return ((((me // 2) ^ 1 ^ at) * 2 + n // pairs) * 2 + half) * pairs + n % pairs

    x_copy = pltpu.make_async_copy(xw, xw_held, in_sems.at[0])
    z_copy = pltpu.make_async_copy(zw, zw_held, in_sems.at[1])

    @pl.when(step == 0)
    def _():
        x_copy.start()
        z_copy.start()

    bcs = project(me, pieces, bw, slice(None))
    bc_out[...] = bcs[:, :128].astype(BF)

    lane = lax.broadcasted_iota(jnp.int32, (span, 128), 1)
    low = lane < 64
    lane8 = lax.broadcasted_iota(jnp.int32, (heads, span), 1)
    lane_all = lax.broadcasted_iota(jnp.int32, (heads * count, span), 1)
    raw = jnp.concatenate(
        [
            jnp.transpose(bcs[n * span : (n + 1) * span, 128:256])[:heads] + small[:, 0:1]
            for n in range(count)
        ],
        axis=0,
    )
    counts_at = 1 + meta.shape[0] // 2
    alive = jnp.concatenate(
        [(lane8 < meta[counts_at + session_of(step, n)]).astype(F32) for n in range(count)],
        axis=0,
    )
    steps = (jnp.maximum(raw, 0.0) + jnp.log1p(jnp.exp(-jnp.abs(raw)))) * alive
    totals = steps * jnp.concatenate([small[:, 1:2]] * count, axis=0)
    shift = 1
    while shift < span:
        totals = totals + jnp.where(lane_all >= shift, pltpu.roll(totals, shift, 1), 0.0)
        shift *= 2
    steps_out[...] = steps
    totals_out[...] = totals
    lasts = totals[:, span - 1 : span]
    weight_rows = jnp.exp(jnp.minimum(totals - lasts, 0.0)) * steps
    kept = jnp.exp(-lasts)

    @pl.when(step == 0)
    def _():
        x_copy.wait()

    for quad in range(quads):
        columns = slice(quad * 256, quad * 256 + 256)
        xs[:, columns] = project(me, pieces, xw_held, columns).astype(BF)

    @pl.when(step == 0)
    def _():
        z_copy.wait()

    for quad in range(quads):
        columns = slice(quad * 256, quad * 256 + 256)
        zs[:, columns] = project(me, pieces, zw_held, columns).astype(BF)

    for n in range(count):
        rows = slice(n * span, (n + 1) * span)
        bc = bcs[rows, 0:128]
        b_low = jnp.where(low, bc, 0.0).astype(BF)
        b_high = jnp.where(low, 0.0, pltpu.roll(bc, 64, 1)).astype(BF)
        b_both = jnp.concatenate([b_low, b_high], axis=0)
        for quad in range(quads):
            head = n * heads + quad * 4
            scale = jnp.concatenate(
                [
                    jnp.broadcast_to(weight_rows[head + k : head + k + 1, :], (32, span))
                    for k in range(4)
                ],
                axis=0,
            )
            x = xs[rows, quad * 256 : quad * 256 + 256].astype(F32)
            even = (jnp.transpose(x[:, :128]) * scale).astype(BF)
            odd = (jnp.transpose(x[:, 128:]) * scale).astype(BF)
            added = jnp.dot(
                jnp.concatenate([even, odd], axis=1), b_both, preferred_element_type=F32
            )
            keep = jnp.concatenate(
                [
                    jnp.broadcast_to(kept[head + k : head + k + 1, :], (32, 128))
                    for k in range(4)
                ],
                axis=0,
            )
            part = slice(quad * 128, quad * 128 + 128)
            fresh[step * count + n, part, :] = (
                keep * states[n][part, :].astype(F32) + added
            ).astype(BF)

    def sending(at, n):
        number = at * count + n
        return pltpu.make_async_copy(
            fresh.at[number], outgoing.at[meta[1 + session_of(at, n)]], sems.at[number]
        )

    for n in range(count):
        sending(step, n).start()

    @pl.when(step == 1)
    def _():
        for at in range(2):
            for n in range(count):
                sending(at, n).wait()


def scan_kernel(
    heads, span, pairs, half, side, meta, gain, order, xs, zs, bcs, steps_in, totals_in, s0, s1,
    na, nb, result,
):
    me = meta[0]
    step = pl.program_id(0)
    target = me ^ (2 * (1 - side) + step)
    quads = heads // 4
    states = (s0, s1)
    lane = lax.broadcasted_iota(jnp.int32, (span, 128), 1)
    row = lax.broadcasted_iota(jnp.int32, (span, 128), 0)
    low = lane < 64
    causal = row >= lane
    head_masks = []
    for k in range(4):
        mask = (lane // 32 == k).astype(F32).astype(BF)
        head_masks.append(jnp.concatenate([mask, mask], axis=1))
    steps = steps_in[...]
    totals = totals_in[...]
    cum = jnp.transpose(
        jnp.concatenate([totals, jnp.zeros((128 - heads * pairs, span), F32)], axis=0)
    )
    counts_at = 1 + meta.shape[0] // 2
    for i in range(pairs):
        rows = slice(i * span, (i + 1) * span)
        count = meta[counts_at + (target * 2 + half) * pairs + i]
        bc = bcs[rows, :].astype(F32)
        turned = pltpu.roll(bc, 64, 1)
        b_low = jnp.where(low, bc, 0.0).astype(BF)
        c_low = jnp.where(low, turned, 0.0).astype(BF)
        c_high = jnp.where(low, 0.0, bc).astype(BF)
        scores = lax.dot_general(c_low, b_low, NT, preferred_element_type=F32)
        scores = jnp.where(causal, scores, 0.0)
        carried = lax.dot_general(
            jnp.concatenate([c_low, c_high], axis=0),
            states[i][...],
            NT,
            preferred_element_type=F32,
        )
        gated = []
        squares = None
        for quad in range(quads):
            columns = slice(quad * 256, quad * 256 + 256)
            part = slice(quad * 128, quad * 128 + 128)
            x = xs[rows, columns]
            mixes = []
            spread = None
            for k in range(4):
                head = i * heads + quad * 4 + k
                level = jnp.broadcast_to(cum[:, head : head + 1], (span, 128))
                gap = jnp.minimum(totals[head : head + 1, :] - level, 0.0)
                mixes.append((jnp.exp(gap) * steps[head : head + 1, :] * scores).astype(BF))
                spread = level if spread is None else jnp.where(lane >= 32 * k, level, spread)
            diagonal = jnp.dot(
                jnp.concatenate(mixes, axis=1),
                jnp.concatenate([x * head_masks[k] for k in range(4)], axis=0),
                preferred_element_type=F32,
            )
            fade = jnp.exp(-spread)
            before = jnp.concatenate(
                [carried[:span, part] * fade, carried[span:, part] * fade], axis=1
            )
            gate = zs[rows, columns].astype(F32)
            value = (diagonal + before) * (gate * (0.5 + 0.5 * jnp.tanh(0.5 * gate)))
            gated.append(value)
            own_squares = jnp.sum(value * value, axis=1, keepdims=True)
            squares = own_squares if squares is None else squares + own_squares
        inverse = lax.rsqrt(squares * (1.0 / (heads * 64)) + 1e-05)
        inverse = jnp.where(row[:, :1] < count, inverse, 0.0)
        for quad in range(quads):
            columns = slice(quad * 256, quad * 256 + 256)
            normed = (gated[quad] * inverse * gain[:, columns]).astype(BF)
            result[rows, columns] = lax.dot_general(
                normed, order[...], NT, preferred_element_type=F32
            ).astype(BF)

    @pl.when(step == 0)
    def _():
        na[...] = result[...]

    @pl.when(step == 1)
    def _():
        nb[...] = result[...]


def whole(array):
    return pl.BlockSpec(array.shape, lambda i, meta: (0,) * array.ndim)


def state_call(half, meta, pieces, weights, small, inbound, span, earlier):
    rows, depth = pieces[2].shape[-2:]
    pairs = rows // span
    count = 2 * pairs
    heads = small.shape[0]
    width = weights[1].shape[1]

    def near(i, meta):
        return ((meta[0] // 2) ^ 1 ^ i, 0, half, 0, 0)

    def arrived(i, meta):
        return ((meta[0] // 2) ^ 1 ^ i, 0, 0, 0)

    def slot_of(n):
        def index(i, meta):
            target = ((meta[0] // 2) ^ 1 ^ i) * 2 + n // pairs
            return (meta[1 + (target * 2 + half) * pairs + n % pairs], 0, 0)

        return index

    def by_step(shape):
        return pl.BlockSpec((None,) + shape, lambda i, meta: (i, 0, 0))

    operands = [meta, *pieces, *weights, small] + [inbound] * count
    aliases = {}
    extra = []
    if earlier is not None:
        aliases = {len(operands): 5}
        operands.append(earlier)
        extra = [ANY]
    return pl.pallas_call(
        lambda *refs: state_kernel(heads, span, pairs, half, *refs),
        out_shape=[
            jax.ShapeDtypeStruct((2, count * span, width), BF),
            jax.ShapeDtypeStruct((2, count * span, width), BF),
            jax.ShapeDtypeStruct((2, count * span, 128), BF),
            jax.ShapeDtypeStruct((2, heads * count, span), F32),
            jax.ShapeDtypeStruct((2, heads * count, span), F32),
            jax.ShapeDtypeStruct(inbound.shape, BF),
        ],
        grid_spec=pltpu.PrefetchScalarGridSpec(
            num_scalar_prefetch=1,
            grid=(2,),
            in_specs=[pl.BlockSpec((None, 2, None, rows, depth), near)] * 2
            + [pl.BlockSpec((None, 2, rows, depth), arrived)] * 2
            + [whole(weights[0]), ANY, ANY]
            + [whole(small)]
            + [pl.BlockSpec((None,) + inbound.shape[1:], slot_of(n)) for n in range(count)]
            + extra,
            out_specs=[
                by_step((count * span, width)),
                by_step((count * span, width)),
                by_step((count * span, 128)),
                by_step((heads * count, span)),
                by_step((heads * count, span)),
                ANY,
            ],
            scratch_shapes=[
                pltpu.VMEM((2 * count,) + inbound.shape[1:], BF),
                *[pltpu.VMEM(weight.shape, BF) for weight in weights[1:]],
                pltpu.SemaphoreType.DMA((2 * count,)),
                pltpu.SemaphoreType.DMA((2,)),
            ],
        ),
        input_output_aliases=aliases,
        compiler_params=pltpu.CompilerParams(vmem_limit_bytes=VMEM_LIMIT),
        cost_estimate=pl.CostEstimate(
            flops=4 * 10**9, bytes_accessed=1, transcendentals=0
        ),
        name="states",
    )(*operands)


def scan_call(half, side, meta, gain, order, mid, inbound, span, rows):
    pairs = rows // span
    heads = mid[-1].shape[1] // (2 * pairs)
    width = mid[0].shape[2]
    mid = [part.reshape(2, 2, part.shape[1] // 2, part.shape[2]) for part in mid]

    def block_of(part):
        return pl.BlockSpec(
            (None, None) + part.shape[2:], lambda i, meta: (side, i ^ (meta[0] % 2), 0, 0)
        )

    def slot_of(n):
        def index(i, meta):
            target = meta[0] ^ (2 * (1 - side) + i)
            return (meta[1 + (target * 2 + half) * pairs + n], 0, 0)

        return index

    return pl.pallas_call(
        lambda *refs: scan_kernel(heads, span, pairs, half, side, *refs),
        out_shape=[jax.ShapeDtypeStruct((rows, width), BF)] * 2,
        grid_spec=pltpu.PrefetchScalarGridSpec(
            num_scalar_prefetch=1,
            grid=(2,),
            in_specs=[whole(gain), whole(order)]
            + [block_of(part) for part in mid]
            + [pl.BlockSpec((None,) + inbound.shape[1:], slot_of(n)) for n in range(pairs)],
            out_specs=[pl.BlockSpec((rows, width), lambda i, meta: (0, 0))] * 2,
            scratch_shapes=[pltpu.VMEM((rows, width), BF)],
        ),
        compiler_params=pltpu.CompilerParams(vmem_limit_bytes=VMEM_LIMIT),
        cost_estimate=pl.CostEstimate(
            flops=2 * 10**9, bytes_accessed=1, transcendentals=0
        ),
        name="scan",
    )(meta, gain, order, *mid, *[inbound] * pairs)


def out_call(half, halves, normed, weights, earlier):
    rows, depth = normed[0].shape
    columns = weights[0].shape[1]
    block = 512

    def kernel(*refs):
        out = refs[-1]
        total = None
        for d in range(4):
            part = jnp.dot(refs[d][...], refs[4 + d][...], preferred_element_type=F32)
            total = part if total is None else total + part
        out[...] = total.astype(BF)

    operands = [*normed, *weights]
    extra = []
    aliases = {}
    if earlier is not None:
        aliases = {len(operands): 0}
        operands.append(earlier)
        extra = [ANY]
    return pl.pallas_call(
        kernel,
        grid=(columns // block,),
        out_shape=jax.ShapeDtypeStruct((halves * rows, columns), BF),
        in_specs=[pl.BlockSpec((rows, depth), lambda j: (0, 0))] * 4
        + [pl.BlockSpec((depth, block), lambda j: (0, j))] * 4
        + extra,
        out_specs=pl.BlockSpec((rows, block), lambda j: (half, j)),
        input_output_aliases=aliases,
        compiler_params=pltpu.CompilerParams(vmem_limit_bytes=VMEM_LIMIT),
        cost_estimate=pl.CostEstimate(
            flops=2 * 10**9, bytes_accessed=1, transcendentals=0
        ),
        name="project_out",
    )(*operands)


def after(value, *others):
    return lax.optimization_barrier((value,) + others)[0]


def body(
    tokens,
    x_weight,
    z_weight,
    bc_weight,
    dt_weight,
    dt_bias,
    decay_rate,
    norm_gain,
    out_weight,
    store_states,
    home_rows,
    event_counts,
):
    shard_count = lax.axis_size("dp")
    model_shards = lax.axis_size("mp")
    shard_index = lax.axis_index("dp")
    me = lax.axis_index("mp")
    sessions_here, state_width = store_states.shape
    heads = dt_bias.shape[0]
    width = x_weight.shape[1]
    depth = tokens.shape[1]
    span = tokens.shape[0] // sessions_here
    halves = 2
    rows = tokens.shape[0] // (model_shards * halves)
    capacity = max(2, (sessions_here + shard_count - 1) // shard_count)
    slot_count = shard_count * capacity
    row_shape = (state_width // 128, 128)

    def exchange(value, distance):
        pairs = [(j, j ^ distance) for j in range(model_shards)]
        return lax.ppermute(value, "mp", pairs)

    def trade(value):
        return lax.all_to_all(
            value.reshape((shard_count, capacity) + row_shape),
            "dp",
            split_axis=0,
            concat_axis=0,
            tiled=True,
        ).reshape((slot_count,) + row_shape)

    replicas = lax.axis_size("groups") * shard_count
    replica = lax.axis_index("groups") * shard_count + shard_index
    share = width // replicas
    ow_share = lax.dynamic_slice_in_dim(out_weight, replica * share, share)
    ow_part = exchange(ow_share, 2)
    blocks = tokens.reshape(model_shards // 2, 2, halves, rows, depth)
    sibling = exchange(tokens, 1).reshape(blocks.shape)

    local = jnp.arange(sessions_here, dtype=jnp.int32)
    store_rows = shard_index * sessions_here + local
    everyone = jnp.arange(home_rows.shape[0], dtype=jnp.int32)
    owner = jnp.sum(
        jnp.where(home_rows[None, :] == store_rows[:, None], everyone[None, :], 0), axis=1
    )
    server = owner // sessions_here
    row_slot = server * capacity + rank_within(server, local)
    wanted_slots = jnp.arange(slot_count, dtype=jnp.int32)
    source = jnp.sum(
        jnp.where(row_slot[None, :] == wanted_slots[:, None], local[None, :], 0), axis=1
    )
    swap_row = np.arange(sessions_here * 16)
    swap = jnp.asarray(
        (swap_row % 16 * sessions_here + swap_row // 16)[:, None] == swap_row[None, :], BF
    )
    first = after(blocks, ow_share)[:, :, 0]
    packed = pack_states(after(source, first), store_states, swap, slot_count)
    second = after(blocks, packed)[:, :, 1]
    across = [exchange(first, 2), exchange(second, 2)]
    inbound = trade(packed)
    wanted = lax.dynamic_slice_in_dim(home_rows, shard_index * sessions_here, sessions_here)
    home_shard = wanted // sessions_here
    session_slot = home_shard * capacity + rank_within(home_shard, wanted % sessions_here)
    meta = jnp.concatenate([me.reshape(1).astype(jnp.int32), session_slot, event_counts])

    new_column = np.arange(width)
    old_column = (
        new_column // 256 * 256
        + new_column // 32 % 4 * 64
        + new_column % 32 * 2
        + new_column // 128 % 2
    )
    turn = jnp.asarray(old_column[None, :] == np.arange(width)[:, None], BF)
    xw = jnp.dot(x_weight, turn, preferred_element_type=F32).astype(BF)
    zw = jnp.dot(z_weight, turn, preferred_element_type=F32).astype(BF)
    order = turn[:256, :256]
    bw = jnp.concatenate(
        [bc_weight, dt_weight, jnp.zeros((bc_weight.shape[0], 128 - heads), BF)], axis=1
    )
    gain = norm_gain.reshape(heads // 4, 4, 32, 2).transpose(0, 3, 1, 2).reshape(1, width)
    small = jnp.stack([dt_bias, decay_rate], axis=1)

    ow_part = after(ow_part, packed)
    ow_across = lax.all_gather(ow_part, ("groups", "dp"), axis=0, tiled=True)
    ow_sibling = exchange(out_weight, 1)

    outgoing = None
    received = []
    done = []
    for h in range(halves):
        arrived = across[h]
        start = meta
        if h:
            start = after(meta, done[-1], ow_sibling)
            arrived = after(arrived, mid[0])
        else:
            arrived = after(arrived, xw, zw, bw)
        pieces = (blocks, sibling, arrived, exchange(arrived, 1))
        *mid, outgoing = state_call(
            h, start, pieces, (bw, xw, zw), small, inbound, span, outgoing
        )
        far_part = scan_call(h, 0, start, gain, order, mid, inbound, span, rows)
        start = after(start, far_part[0])
        if h:
            start = after(start, *received[0])
        near_part = scan_call(h, 1, start, gain, order, mid, inbound, span, rows)
        done.append(near_part[0])
        received.append(
            [
                near_part[0],
                exchange(near_part[1], 1),
                exchange(far_part[0], 2),
                exchange(far_part[1], 3),
            ]
        )
    returned = trade(outgoing)
    ow_across = after(ow_across, done[-1])
    ow_far = exchange(ow_across, 1)
    new_store = gather_states(row_slot, returned, swap)
    ow = (out_weight, ow_sibling, ow_across, ow_far)
    out_tokens = None
    for h in range(halves):
        normed = list(received[h])
        if h == 0:
            normed[0] = after(normed[0], done[-1])
        out_tokens = out_call(h, halves, normed, ow, out_tokens)
    return (out_tokens, new_store)


def solution(mesh):
    return jax.shard_map(
        body,
        mesh=mesh,
        in_specs=(
            P(("groups", "dp"), "mp"),
            P(None, "mp"),
            P(None, "mp"),
            P(None, "mp"),
            P(None, "mp"),
            P("mp"),
            P("mp"),
            P("mp"),
            P("mp", None),
            P(("groups", "dp"), "mp"),
            P("groups"),
            P(("groups", "dp")),
        ),
        out_specs=(P(("groups", "dp", "mp"), None), P(("groups", "dp"), "mp")),
        check_vma=False,
    )
```

```python
import jax
import jax.numpy as jnp
import numpy as np
from jax import lax
from jax.experimental import pallas as pl
from jax.experimental.pallas import tpu as pltpu
from jax.sharding import PartitionSpec as P

BF = jnp.bfloat16
F32 = jnp.float32
ANY = pl.BlockSpec(memory_space=pl.ANY)
VMEM = pl.BlockSpec(memory_space=pltpu.VMEM)
SMEM = pl.BlockSpec(memory_space=pltpu.SMEM)
NT = (((1,), (1,)), ((), ()))
VMEM_LIMIT = 58 * 2**20


def rank_within(keys, order):
    earlier = (keys[None, :] == keys[:, None]) & (order[None, :] < order[:, None])
    return jnp.sum(earlier.astype(jnp.int32), axis=1)


def pack_states(source, store, swap, slots):
    sessions, width = store.shape
    lines = width // 128

    def kernel(source, store, swap, out, held):
        for part in range(4):
            base = part * 16 * 128
            stacked = jnp.concatenate(
                [store[:, base + j * 128 : base + (j + 1) * 128] for j in range(16)], axis=0
            )
            turned = jnp.dot(swap[...], stacked, preferred_element_type=F32).astype(BF)
            for r in range(sessions):
                held[r, part * 16 : (part + 1) * 16, :] = turned[r * 16 : (r + 1) * 16]
        for n in range(slots):
            out[n] = held[source[n]]

    return pl.pallas_call(
        kernel,
        grid=(lines // 64,),
        out_shape=jax.ShapeDtypeStruct((slots, lines, 128), BF),
        in_specs=[
            SMEM,
            pl.BlockSpec((sessions, 64 * 128), lambda j: (0, j)),
            pl.BlockSpec(swap.shape, lambda j: (0, 0)),
        ],
        out_specs=pl.BlockSpec((slots, 64, 128), lambda j: (0, j, 0)),
        scratch_shapes=[pltpu.VMEM((sessions, 64, 128), BF)],
        compiler_params=pltpu.CompilerParams(vmem_limit_bytes=VMEM_LIMIT),
        cost_estimate=pl.CostEstimate(
            flops=1, bytes_accessed=1, transcendentals=0
        ),
        name="pack_states",
    )(source, store, swap)


def gather_states(index, returned, swap):
    sessions = index.shape[0]
    slots, lines, lanes = returned.shape

    def kernel(index, returned, swap, out):
        for part in range(4):
            rows = slice(part * 16, (part + 1) * 16)
            stacked = jnp.concatenate(
                [returned[index[r], rows, :] for r in range(sessions)], axis=0
            )
            turned = lax.dot_general(
                swap[...], stacked, (((0,), (0,)), ((), ())), preferred_element_type=F32
            ).astype(BF)
            for j in range(16):
                column = (part * 16 + j) * 128
                out[:, column : column + 128] = turned[j * sessions : (j + 1) * sessions]

    return pl.pallas_call(
        kernel,
        grid=(lines // 64,),
        out_shape=jax.ShapeDtypeStruct((sessions, lines * lanes), BF),
        in_specs=[
            SMEM,
            pl.BlockSpec((slots, 64, lanes), lambda j: (0, j, 0)),
            pl.BlockSpec(swap.shape, lambda j: (0, 0)),
        ],
        out_specs=pl.BlockSpec((sessions, 64 * lanes), lambda j: (0, j)),
        compiler_params=pltpu.CompilerParams(vmem_limit_bytes=VMEM_LIMIT),
        cost_estimate=pl.CostEstimate(flops=1, bytes_accessed=1, transcendentals=0),
        name="gather_states",
    )(index, returned, swap)


def project(me, pieces, weight, columns):
    depth = pieces[0].shape[1]
    total = None
    for k in range(4):
        first = pl.multiple_of((me ^ k) * depth, depth)
        part = jnp.dot(
            pieces[k][...], weight[pl.ds(first, depth), columns], preferred_element_type=F32
        )
        total = part if total is None else total + part
    return total


def layer_kernel(
    heads, span, pairs, half, meta, own, sibling, across, far, bw, xw, zw, small, gain, order, s0,
    s1, s2, s3,
    *refs
):
    n0, n1, n2, n3, outgoing, xs, zs, fresh, sems = refs[-9:]
    normed_out = (n0, n1, n2, n3)
    me = meta[0]
    step = pl.program_id(0)
    count = 2 * pairs
    rows_all = count * span
    depth = across.shape[-1]
    pieces = [piece[...].reshape(rows_all, depth) for piece in (own, sibling, across, far)]
    quads = heads // 4
    states = (s0, s1, s2, s3)

    def session_of(at, n):
        return ((((me // 2) ^ 1 ^ at) * 2 + n // pairs) * 2 + half) * pairs + n % pairs

    bcs = project(me, pieces, bw, slice(None))
    for quad in range(quads):
        columns = slice(quad * 256, quad * 256 + 256)
        xs[:, columns] = project(me, pieces, xw, columns).astype(BF)
        zs[:, columns] = project(me, pieces, zw, columns).astype(BF)

    lane = lax.broadcasted_iota(jnp.int32, (span, 128), 1)
    low = lane < 64
    lane8 = lax.broadcasted_iota(jnp.int32, (heads, span), 1)
    lane_all = lax.broadcasted_iota(jnp.int32, (heads * count, span), 1)
    raw = jnp.concatenate(
        [
            jnp.transpose(bcs[n * span : (n + 1) * span, 128:256])[:heads] + small[:, 0:1]
            for n in range(count)
        ],
        axis=0,
    )
    counts_at = 1 + meta.shape[0] // 2
    alive = jnp.concatenate(
        [(lane8 < meta[counts_at + session_of(step, n)]).astype(F32) for n in range(count)],
        axis=0,
    )
    steps = (jnp.maximum(raw, 0.0) + jnp.log1p(jnp.exp(-jnp.abs(raw)))) * alive
    totals = steps * jnp.concatenate([small[:, 1:2]] * count, axis=0)
    shift = 1
    while shift < span:
        totals = totals + jnp.where(lane_all >= shift, pltpu.roll(totals, shift, 1), 0.0)
        shift *= 2
    lasts = totals[:, span - 1 : span]
    weight_rows = jnp.exp(jnp.minimum(totals - lasts, 0.0)) * steps
    kept = jnp.exp(-lasts)

    cum = jnp.transpose(
        jnp.concatenate([totals, jnp.zeros((128 - heads * count, span), F32)], axis=0)
    )
    row = lax.broadcasted_iota(jnp.int32, (span, 128), 0)
    causal = row >= lane
    head_masks = []
    for k in range(4):
        mask = (lane // 32 == k).astype(F32).astype(BF)
        head_masks.append(jnp.concatenate([mask, mask], axis=1))

    for n in range(count):
        rows = slice(n * span, (n + 1) * span)
        length = meta[counts_at + session_of(step, n)]
        bc = bcs[rows, 0:128]
        turned = pltpu.roll(bc, 64, 1)
        b_low = jnp.where(low, bc, 0.0).astype(BF)
        b_high = jnp.where(low, 0.0, turned).astype(BF)
        c_low = jnp.where(low, turned, 0.0).astype(BF)
        c_high = jnp.where(low, 0.0, bc).astype(BF)
        b_both = jnp.concatenate([b_low, b_high], axis=0)
        scores = lax.dot_general(c_low, b_low, NT, preferred_element_type=F32)
        scores = jnp.where(causal, scores, 0.0)
        carried = lax.dot_general(
            jnp.concatenate([c_low, c_high], axis=0),
            states[n][...],
            NT,
            preferred_element_type=F32,
        )
        gated = []
        squares = None
        for quad in range(quads):
            columns = slice(quad * 256, quad * 256 + 256)
            part = slice(quad * 128, quad * 128 + 128)
            first_head = n * heads + quad * 4
            x = xs[rows, columns]
            mixes = []
            spread = None
            for k in range(4):
                head = first_head + k
                level = jnp.broadcast_to(cum[:, head : head + 1], (span, 128))
                gap = jnp.minimum(totals[head : head + 1, :] - level, 0.0)
                mixes.append((jnp.exp(gap) * steps[head : head + 1, :] * scores).astype(BF))
                spread = level if spread is None else jnp.where(lane >= 32 * k, level, spread)
            diagonal = jnp.dot(
                jnp.concatenate(mixes, axis=1),
                jnp.concatenate([x * head_masks[k] for k in range(4)], axis=0),
                preferred_element_type=F32,
            )
            fade = jnp.exp(-spread)
            before = jnp.concatenate(
                [carried[:span, part] * fade, carried[span:, part] * fade], axis=1
            )
            gate = zs[rows, columns].astype(F32)
            value = (diagonal + before) * (gate * (0.5 + 0.5 * jnp.tanh(0.5 * gate)))
            gated.append(value)
            own_squares = jnp.sum(value * value, axis=1, keepdims=True)
            squares = own_squares if squares is None else squares + own_squares
            scale = jnp.concatenate(
                [
                    jnp.broadcast_to(
                        weight_rows[first_head + k : first_head + k + 1, :], (32, span)
                    )
                    for k in range(4)
                ],
                axis=0,
            )
            xf = x.astype(F32)
            even = (jnp.transpose(xf[:, :128]) * scale).astype(BF)
            odd = (jnp.transpose(xf[:, 128:]) * scale).astype(BF)
            added = jnp.dot(
                jnp.concatenate([even, odd], axis=1), b_both, preferred_element_type=F32
            )
            keep = jnp.concatenate(
                [
                    jnp.broadcast_to(kept[first_head + k : first_head + k + 1, :], (32, 128))
                    for k in range(4)
                ],
                axis=0,
            )
            fresh[step * count + n, part, :] = (
                keep * states[n][part, :].astype(F32) + added
            ).astype(BF)
        inverse = lax.rsqrt(squares * (1.0 / (heads * 64)) + 1e-05)
        inverse = jnp.where(row[:, :1] < length, inverse, 0.0)
        for quad in range(quads):
            columns = slice(quad * 256, quad * 256 + 256)
            normed = (gated[quad] * inverse * gain[:, columns]).astype(BF)
            zs[rows, columns] = lax.dot_general(
                normed, order[...], NT, preferred_element_type=F32
            ).astype(BF)

    def sending(at, n):
        number = at * count + n
        return pltpu.make_async_copy(
            fresh.at[number], outgoing.at[meta[1 + session_of(at, n)]], sems.at[number]
        )

    for n in range(count):
        sending(step, n).start()

    for at in range(2):

        @pl.when(step == at)
        def _():
            for near in range(2):
                first = pl.multiple_of((near ^ (me % 2)) * (pairs * span), pairs * span)
                normed_out[2 * (1 - at) + near][...] = zs[pl.ds(first, pairs * span), :]

    @pl.when(step == 1)
    def _():
        for at in range(2):
            for n in range(count):
                sending(at, n).wait()


def whole(array):
    return pl.BlockSpec(array.shape, lambda i, meta: (0,) * array.ndim)


def layer_call(half, meta, pieces, weights, smalls, inbound, span, earlier):
    rows, depth = pieces[2].shape[-2:]
    pairs = rows // span
    count = 2 * pairs
    heads = smalls[0].shape[0]
    width = weights[1].shape[1]

    def near(i, meta):
        return ((meta[0] // 2) ^ 1 ^ i, 0, half, 0, 0)

    def arrived(i, meta):
        return ((meta[0] // 2) ^ 1 ^ i, 0, 0, 0)

    def slot_of(n):
        def index(i, meta):
            target = ((meta[0] // 2) ^ 1 ^ i) * 2 + n // pairs
            return (meta[1 + (target * 2 + half) * pairs + n % pairs], 0, 0)

        return index

    operands = [meta, *pieces, *weights, *smalls] + [inbound] * count
    aliases = {}
    extra = []
    if earlier is not None:
        aliases = {len(operands): 4}
        operands.append(earlier)
        extra = [ANY]
    return pl.pallas_call(
        lambda *refs: layer_kernel(heads, span, pairs, half, *refs),
        out_shape=[jax.ShapeDtypeStruct((rows, width), BF)] * 4
        + [jax.ShapeDtypeStruct(inbound.shape, BF)],
        grid_spec=pltpu.PrefetchScalarGridSpec(
            num_scalar_prefetch=1,
            grid=(2,),
            in_specs=[pl.BlockSpec((None, 2, None, rows, depth), near)] * 2
            + [pl.BlockSpec((None, 2, rows, depth), arrived)] * 2
            + [whole(weight) for weight in weights]
            + [whole(small) for small in smalls]
            + [pl.BlockSpec((None,) + inbound.shape[1:], slot_of(n)) for n in range(count)]
            + extra,
            out_specs=[pl.BlockSpec((rows, width), lambda i, meta: (0, 0))] * 4 + [ANY],
            scratch_shapes=[
                pltpu.VMEM((count * span, width), BF),
                pltpu.VMEM((count * span, width), BF),
                pltpu.VMEM((2 * count,) + inbound.shape[1:], BF),
                pltpu.SemaphoreType.DMA((2 * count,)),
            ],
        ),
        input_output_aliases=aliases,
        compiler_params=pltpu.CompilerParams(vmem_limit_bytes=VMEM_LIMIT),
        cost_estimate=pl.CostEstimate(
            flops=6 * 10**9, bytes_accessed=1, transcendentals=0
        ),
        name="layer",
    )(*operands)


def out_call(half, halves, normed, weights, earlier):
    rows, depth = normed[0].shape
    columns = weights[0].shape[1]
    block = 512

    def kernel(*refs):
        out = refs[-1]
        total = None
        for d in range(4):
            part = jnp.dot(refs[d][...], refs[4 + d][...], preferred_element_type=F32)
            total = part if total is None else total + part
        out[...] = total.astype(BF)

    operands = [*normed, *weights]
    extra = []
    aliases = {}
    if earlier is not None:
        aliases = {len(operands): 0}
        operands.append(earlier)
        extra = [ANY]
    return pl.pallas_call(
        kernel,
        grid=(columns // block,),
        out_shape=jax.ShapeDtypeStruct((halves * rows, columns), BF),
        in_specs=[pl.BlockSpec((rows, depth), lambda j: (0, 0))] * 4
        + [pl.BlockSpec((depth, block), lambda j: (0, j))] * 4
        + extra,
        out_specs=pl.BlockSpec((rows, block), lambda j: (half, j)),
        input_output_aliases=aliases,
        compiler_params=pltpu.CompilerParams(vmem_limit_bytes=VMEM_LIMIT),
        cost_estimate=pl.CostEstimate(
            flops=2 * 10**9, bytes_accessed=1, transcendentals=0
        ),
        name="project_out",
    )(*operands)


def after(value, *others):
    return lax.optimization_barrier((value,) + others)[0]


def body(
    tokens,
    x_weight,
    z_weight,
    bc_weight,
    dt_weight,
    dt_bias,
    decay_rate,
    norm_gain,
    out_weight,
    store_states,
    home_rows,
    event_counts,
):
    shard_count = lax.axis_size("dp")
    model_shards = lax.axis_size("mp")
    shard_index = lax.axis_index("dp")
    me = lax.axis_index("mp")
    sessions_here, state_width = store_states.shape
    heads = dt_bias.shape[0]
    width = x_weight.shape[1]
    depth = tokens.shape[1]
    span = tokens.shape[0] // sessions_here
    halves = 2
    rows = tokens.shape[0] // (model_shards * halves)
    capacity = max(2, (sessions_here + shard_count - 1) // shard_count)
    slot_count = shard_count * capacity
    row_shape = (state_width // 128, 128)

    def exchange(value, distance):
        pairs = [(j, j ^ distance) for j in range(model_shards)]
        return lax.ppermute(value, "mp", pairs)

    def trade(value):
        return lax.all_to_all(
            value.reshape((shard_count, capacity) + row_shape),
            "dp",
            split_axis=0,
            concat_axis=0,
            tiled=True,
        ).reshape((slot_count,) + row_shape)

    replicas = lax.axis_size("groups") * shard_count
    replica = lax.axis_index("groups") * shard_count + shard_index
    share = width // replicas
    ow_share = lax.dynamic_slice_in_dim(out_weight, replica * share, share)
    ow_part = exchange(ow_share, 2)
    blocks = tokens.reshape(model_shards // 2, 2, halves, rows, depth)
    sibling = exchange(tokens, 1).reshape(blocks.shape)

    local = jnp.arange(sessions_here, dtype=jnp.int32)
    store_rows = shard_index * sessions_here + local
    everyone = jnp.arange(home_rows.shape[0], dtype=jnp.int32)
    owner = jnp.sum(
        jnp.where(home_rows[None, :] == store_rows[:, None], everyone[None, :], 0), axis=1
    )
    server = owner // sessions_here
    row_slot = server * capacity + rank_within(server, local)
    wanted_slots = jnp.arange(slot_count, dtype=jnp.int32)
    source = jnp.sum(
        jnp.where(row_slot[None, :] == wanted_slots[:, None], local[None, :], 0), axis=1
    )
    swap_row = np.arange(sessions_here * 16)
    swap = jnp.asarray(
        (swap_row % 16 * sessions_here + swap_row // 16)[:, None] == swap_row[None, :], BF
    )
    first = after(blocks, ow_share)[:, :, 0]
    packed = pack_states(after(source, first), store_states, swap, slot_count)
    second = after(blocks, packed)[:, :, 1]
    across = [exchange(first, 2), exchange(second, 2)]
    inbound = trade(packed)
    wanted = lax.dynamic_slice_in_dim(home_rows, shard_index * sessions_here, sessions_here)
    home_shard = wanted // sessions_here
    session_slot = home_shard * capacity + rank_within(home_shard, wanted % sessions_here)
    meta = jnp.concatenate([me.reshape(1).astype(jnp.int32), session_slot, event_counts])

    new_column = np.arange(width)
    old_column = (
        new_column // 256 * 256
        + new_column // 32 % 4 * 64
        + new_column % 32 * 2
        + new_column // 128 % 2
    )
    turn = jnp.asarray(old_column[None, :] == np.arange(width)[:, None], BF)
    xw = jnp.dot(x_weight, turn, preferred_element_type=F32).astype(BF)
    zw = jnp.dot(z_weight, turn, preferred_element_type=F32).astype(BF)
    order = turn[:256, :256]
    bw = jnp.concatenate(
        [bc_weight, dt_weight, jnp.zeros((bc_weight.shape[0], 128 - heads), BF)], axis=1
    )
    gain = norm_gain.reshape(heads // 4, 4, 32, 2).transpose(0, 3, 1, 2).reshape(1, width)
    small = jnp.stack([dt_bias, decay_rate], axis=1)

    ow_part = after(ow_part, inbound)
    ow_across = lax.all_gather(ow_part, ("groups", "dp"), axis=0, tiled=True)
    ow_sibling = exchange(out_weight, 1)

    outgoing = None
    received = []
    done = []
    for h in range(halves):
        arrived = across[h]
        start = meta
        if h:
            start = after(meta, done[-1], ow_sibling)
            arrived = after(arrived, done[-1])
        else:
            arrived = after(arrived, xw, zw, bw)
        pieces = (blocks, sibling, arrived, exchange(arrived, 1))
        *parts, outgoing = layer_call(
            h, start, pieces, (bw, xw, zw), (small, gain, order), inbound, span, outgoing
        )
        done.append(parts[0])
        received.append([parts[0]] + [exchange(parts[d], d) for d in range(1, 4)])
    returned = trade(outgoing)
    ow_across = after(ow_across, done[-1])
    ow_far = exchange(ow_across, 1)
    new_store = gather_states(row_slot, returned, swap)
    ow = (out_weight, ow_sibling, ow_across, ow_far)
    out_tokens = None
    for h in range(halves):
        normed = list(received[h])
        if h == 0:
            normed[0] = after(normed[0], done[-1])
        out_tokens = out_call(h, halves, normed, ow, out_tokens)
    return (out_tokens, new_store)


def solution(mesh):
    return jax.shard_map(
        body,
        mesh=mesh,
        in_specs=(
            P(("groups", "dp"), "mp"),
            P(None, "mp"),
            P(None, "mp"),
            P(None, "mp"),
            P(None, "mp"),
            P("mp"),
            P("mp"),
            P("mp"),
            P("mp", None),
            P(("groups", "dp"), "mp"),
            P("groups"),
            P(("groups", "dp")),
        ),
        out_specs=(P(("groups", "dp", "mp"), None), P(("groups", "dp"), "mp")),
        check_vma=False,
    )
```

```python
import jax
import jax.numpy as jnp
import numpy as np
from jax import lax
from jax.experimental import pallas as pl
from jax.experimental.pallas import tpu as pltpu
from jax.sharding import PartitionSpec as P

BF = jnp.bfloat16
F32 = jnp.float32
ANY = pl.BlockSpec(memory_space=pl.ANY)
VMEM = pl.BlockSpec(memory_space=pltpu.VMEM)
SMEM = pl.BlockSpec(memory_space=pltpu.SMEM)
NT = (((1,), (1,)), ((), ()))
VMEM_LIMIT = 58 * 2**20


def rank_within(keys, order):
    earlier = (keys[None, :] == keys[:, None]) & (order[None, :] < order[:, None])
    return jnp.sum(earlier.astype(jnp.int32), axis=1)


def pack_states(source, store, swap, slots):
    sessions, width = store.shape
    lines = width // 128

    def kernel(source, store, swap, out, held):
        for part in range(4):
            base = part * 16 * 128
            stacked = jnp.concatenate(
                [store[:, base + j * 128 : base + (j + 1) * 128] for j in range(16)], axis=0
            )
            turned = jnp.dot(swap[...], stacked, preferred_element_type=F32).astype(BF)
            for r in range(sessions):
                held[r, part * 16 : (part + 1) * 16, :] = turned[r * 16 : (r + 1) * 16]
        for n in range(slots):
            out[n] = held[source[n]]

    return pl.pallas_call(
        kernel,
        grid=(lines // 64,),
        out_shape=jax.ShapeDtypeStruct((slots, lines, 128), BF),
        in_specs=[
            SMEM,
            pl.BlockSpec((sessions, 64 * 128), lambda j: (0, j)),
            pl.BlockSpec(swap.shape, lambda j: (0, 0)),
        ],
        out_specs=pl.BlockSpec((slots, 64, 128), lambda j: (0, j, 0)),
        scratch_shapes=[pltpu.VMEM((sessions, 64, 128), BF)],
        compiler_params=pltpu.CompilerParams(vmem_limit_bytes=VMEM_LIMIT),
        cost_estimate=pl.CostEstimate(
            flops=1, bytes_accessed=1, transcendentals=0
        ),
        name="pack_states",
    )(source, store, swap)


def gather_states(index, returned, swap):
    sessions = index.shape[0]
    slots, lines, lanes = returned.shape

    def kernel(index, returned, swap, out):
        for part in range(4):
            rows = slice(part * 16, (part + 1) * 16)
            stacked = jnp.concatenate(
                [returned[index[r], rows, :] for r in range(sessions)], axis=0
            )
            turned = lax.dot_general(
                swap[...], stacked, (((0,), (0,)), ((), ())), preferred_element_type=F32
            ).astype(BF)
            for j in range(16):
                column = (part * 16 + j) * 128
                out[:, column : column + 128] = turned[j * sessions : (j + 1) * sessions]

    return pl.pallas_call(
        kernel,
        grid=(lines // 64,),
        out_shape=jax.ShapeDtypeStruct((sessions, lines * lanes), BF),
        in_specs=[
            SMEM,
            pl.BlockSpec((slots, 64, lanes), lambda j: (0, j, 0)),
            pl.BlockSpec(swap.shape, lambda j: (0, 0)),
        ],
        out_specs=pl.BlockSpec((sessions, 64 * lanes), lambda j: (0, j)),
        compiler_params=pltpu.CompilerParams(vmem_limit_bytes=VMEM_LIMIT),
        cost_estimate=pl.CostEstimate(flops=1, bytes_accessed=1, transcendentals=0),
        name="gather_states",
    )(index, returned, swap)


def project(me, pieces, weight, columns):
    depth = pieces[0].shape[1]
    total = None
    for k in range(4):
        first = pl.multiple_of((me ^ k) * depth, depth)
        part = jnp.dot(
            pieces[k][...], weight[pl.ds(first, depth), columns], preferred_element_type=F32
        )
        total = part if total is None else total + part
    return total


def layer_kernel(
    heads, span, pairs, half, meta, own, sibling, across, far, bw, xw, zw, small, gain, order, s0,
    s1, s2, s3,
    *refs
):
    n0, n1, n2, n3, outgoing, xs, zs, fresh, sems = refs[-9:]
    normed_out = (n0, n1, n2, n3)
    me = meta[0]
    step = pl.program_id(0)
    count = 2 * pairs
    rows_all = count * span
    depth = across.shape[-1]
    pieces = [piece[...].reshape(rows_all, depth) for piece in (own, sibling, across, far)]
    quads = heads // 4
    states = (s0, s1, s2, s3)

    def session_of(at, n):
        return ((((me // 2) ^ 1 ^ at) * 2 + n // pairs) * 2 + half) * pairs + n % pairs

    bcs = project(me, pieces, bw, slice(None))
    for quad in range(quads):
        columns = slice(quad * 256, quad * 256 + 256)
        xs[:, columns] = project(me, pieces, xw, columns).astype(BF)
        zs[:, columns] = project(me, pieces, zw, columns).astype(BF)

    lane = lax.broadcasted_iota(jnp.int32, (span, 128), 1)
    low = lane < 64
    lane8 = lax.broadcasted_iota(jnp.int32, (heads, span), 1)
    lane_all = lax.broadcasted_iota(jnp.int32, (heads * count, span), 1)
    raw = jnp.concatenate(
        [
            jnp.transpose(bcs[n * span : (n + 1) * span, 128:256])[:heads] + small[:, 0:1]
            for n in range(count)
        ],
        axis=0,
    )
    counts_at = 1 + meta.shape[0] // 2
    alive = jnp.concatenate(
        [(lane8 < meta[counts_at + session_of(step, n)]).astype(F32) for n in range(count)],
        axis=0,
    )
    steps = (jnp.maximum(raw, 0.0) + jnp.log1p(jnp.exp(-jnp.abs(raw)))) * alive
    totals = steps * jnp.concatenate([small[:, 1:2]] * count, axis=0)
    shift = 1
    while shift < span:
        totals = totals + jnp.where(lane_all >= shift, pltpu.roll(totals, shift, 1), 0.0)
        shift *= 2
    lasts = totals[:, span - 1 : span]
    weight_rows = jnp.exp(jnp.minimum(totals - lasts, 0.0)) * steps
    kept = jnp.exp(-lasts)

    cum = jnp.transpose(
        jnp.concatenate([totals, jnp.zeros((128 - heads * count, span), F32)], axis=0)
    )
    row = lax.broadcasted_iota(jnp.int32, (span, 128), 0)
    causal = row >= lane
    head_masks = []
    for k in range(4):
        mask = (lane // 32 == k).astype(F32).astype(BF)
        head_masks.append(jnp.concatenate([mask, mask], axis=1))

    for n in range(count):
        rows = slice(n * span, (n + 1) * span)
        length = meta[counts_at + session_of(step, n)]
        bc = bcs[rows, 0:128]
        turned = pltpu.roll(bc, 64, 1)
        b_low = jnp.where(low, bc, 0.0).astype(BF)
        b_high = jnp.where(low, 0.0, turned).astype(BF)
        c_low = jnp.where(low, turned, 0.0).astype(BF)
        c_high = jnp.where(low, 0.0, bc).astype(BF)
        b_both = jnp.concatenate([b_low, b_high], axis=0)
        scores = lax.dot_general(c_low, b_low, NT, preferred_element_type=F32)
        scores = jnp.where(causal, scores, 0.0)
        carried = lax.dot_general(
            jnp.concatenate([c_low, c_high], axis=0),
            states[n][...],
            NT,
            preferred_element_type=F32,
        )
        gated = []
        squares = None
        for quad in range(quads):
            columns = slice(quad * 256, quad * 256 + 256)
            part = slice(quad * 128, quad * 128 + 128)
            first_head = n * heads + quad * 4
            x = xs[rows, columns]
            mixes = []
            spread = None
            for k in range(4):
                head = first_head + k
                level = jnp.broadcast_to(cum[:, head : head + 1], (span, 128))
                gap = jnp.minimum(totals[head : head + 1, :] - level, 0.0)
                mixes.append((jnp.exp(gap) * steps[head : head + 1, :] * scores).astype(BF))
                spread = level if spread is None else jnp.where(lane >= 32 * k, level, spread)
            diagonal = jnp.dot(
                jnp.concatenate(mixes, axis=1),
                jnp.concatenate([x * head_masks[k] for k in range(4)], axis=0),
                preferred_element_type=F32,
            )
            fade = jnp.exp(-spread)
            before = jnp.concatenate(
                [carried[:span, part] * fade, carried[span:, part] * fade], axis=1
            )
            gate = zs[rows, columns].astype(F32)
            value = (diagonal + before) * (gate * (0.5 + 0.5 * jnp.tanh(0.5 * gate)))
            gated.append(value)
            own_squares = jnp.sum(value * value, axis=1, keepdims=True)
            squares = own_squares if squares is None else squares + own_squares
            scale = jnp.concatenate(
                [
                    jnp.broadcast_to(
                        weight_rows[first_head + k : first_head + k + 1, :], (32, span)
                    )
                    for k in range(4)
                ],
                axis=0,
            )
            xf = x.astype(F32)
            even = (jnp.transpose(xf[:, :128]) * scale).astype(BF)
            odd = (jnp.transpose(xf[:, 128:]) * scale).astype(BF)
            added = jnp.dot(
                jnp.concatenate([even, odd], axis=1), b_both, preferred_element_type=F32
            )
            keep = jnp.concatenate(
                [
                    jnp.broadcast_to(kept[first_head + k : first_head + k + 1, :], (32, 128))
                    for k in range(4)
                ],
                axis=0,
            )
            fresh[step * count + n, part, :] = (
                keep * states[n][part, :].astype(F32) + added
            ).astype(BF)
        inverse = lax.rsqrt(squares * (1.0 / (heads * 64)) + 1e-05)
        inverse = jnp.where(row[:, :1] < length, inverse, 0.0)
        for quad in range(quads):
            columns = slice(quad * 256, quad * 256 + 256)
            normed = (gated[quad] * inverse * gain[:, columns]).astype(BF)
            zs[rows, columns] = lax.dot_general(
                normed, order[...], NT, preferred_element_type=F32
            ).astype(BF)

    def sending(at, n):
        number = at * count + n
        return pltpu.make_async_copy(
            fresh.at[number], outgoing.at[meta[1 + session_of(at, n)]], sems.at[number]
        )

    for n in range(count):
        sending(step, n).start()

    for at in range(2):

        @pl.when(step == at)
        def _():
            for near in range(2):
                first = pl.multiple_of((near ^ (me % 2)) * (pairs * span), pairs * span)
                normed_out[2 * (1 - at) + near][...] = zs[pl.ds(first, pairs * span), :]

    @pl.when(step == 1)
    def _():
        for at in range(2):
            for n in range(count):
                sending(at, n).wait()


def whole(array):
    return pl.BlockSpec(array.shape, lambda i, meta: (0,) * array.ndim)


def layer_call(half, meta, pieces, weights, smalls, inbound, span, earlier):
    rows, depth = pieces[2].shape[-2:]
    pairs = rows // span
    count = 2 * pairs
    heads = smalls[0].shape[0]
    width = weights[1].shape[1]

    def near(i, meta):
        return ((meta[0] // 2) ^ 1 ^ i, 0, half, 0, 0)

    def arrived(i, meta):
        return ((meta[0] // 2) ^ 1 ^ i, 0, 0, 0)

    def slot_of(n):
        def index(i, meta):
            target = ((meta[0] // 2) ^ 1 ^ i) * 2 + n // pairs
            return (meta[1 + (target * 2 + half) * pairs + n % pairs], 0, 0)

        return index

    operands = [meta, *pieces, *weights, *smalls] + [inbound] * count
    aliases = {}
    extra = []
    if earlier is not None:
        aliases = {len(operands): 4}
        operands.append(earlier)
        extra = [ANY]
    return pl.pallas_call(
        lambda *refs: layer_kernel(heads, span, pairs, half, *refs),
        out_shape=[jax.ShapeDtypeStruct((rows, width), BF)] * 4
        + [jax.ShapeDtypeStruct(inbound.shape, BF)],
        grid_spec=pltpu.PrefetchScalarGridSpec(
            num_scalar_prefetch=1,
            grid=(2,),
            in_specs=[pl.BlockSpec((None, 2, None, rows, depth), near)] * 2
            + [pl.BlockSpec((None, 2, rows, depth), arrived)] * 2
            + [whole(weight) for weight in weights]
            + [whole(small) for small in smalls]
            + [pl.BlockSpec((None,) + inbound.shape[1:], slot_of(n)) for n in range(count)]
            + extra,
            out_specs=[pl.BlockSpec((rows, width), lambda i, meta: (0, 0))] * 4 + [ANY],
            scratch_shapes=[
                pltpu.VMEM((count * span, width), BF),
                pltpu.VMEM((count * span, width), BF),
                pltpu.VMEM((2 * count,) + inbound.shape[1:], BF),
                pltpu.SemaphoreType.DMA((2 * count,)),
            ],
        ),
        input_output_aliases=aliases,
        compiler_params=pltpu.CompilerParams(vmem_limit_bytes=VMEM_LIMIT),
        cost_estimate=pl.CostEstimate(
            flops=1, bytes_accessed=1, transcendentals=0
        ),
        name="layer",
    )(*operands)


def out_call(half, halves, normed, weights, earlier):
    rows, depth = normed[0].shape
    columns = weights[0].shape[1]
    block = 512

    def kernel(*refs):
        out = refs[-1]
        total = None
        for d in range(4):
            part = jnp.dot(refs[d][...], refs[4 + d][...], preferred_element_type=F32)
            total = part if total is None else total + part
        out[...] = total.astype(BF)

    operands = [*normed, *weights]
    extra = []
    aliases = {}
    if earlier is not None:
        aliases = {len(operands): 0}
        operands.append(earlier)
        extra = [ANY]
    return pl.pallas_call(
        kernel,
        grid=(columns // block,),
        out_shape=jax.ShapeDtypeStruct((halves * rows, columns), BF),
        in_specs=[pl.BlockSpec((rows, depth), lambda j: (0, 0))] * 4
        + [pl.BlockSpec((depth, block), lambda j: (0, j))] * 4
        + extra,
        out_specs=pl.BlockSpec((rows, block), lambda j: (half, j)),
        input_output_aliases=aliases,
        compiler_params=pltpu.CompilerParams(vmem_limit_bytes=VMEM_LIMIT),
        cost_estimate=pl.CostEstimate(
            flops=1, bytes_accessed=1, transcendentals=0
        ),
        name="project_out",
    )(*operands)


def after(value, *others):
    return lax.optimization_barrier((value,) + others)[0]


def body(
    tokens,
    x_weight,
    z_weight,
    bc_weight,
    dt_weight,
    dt_bias,
    decay_rate,
    norm_gain,
    out_weight,
    store_states,
    home_rows,
    event_counts,
):
    shard_count = lax.axis_size("dp")
    model_shards = lax.axis_size("mp")
    shard_index = lax.axis_index("dp")
    me = lax.axis_index("mp")
    sessions_here, state_width = store_states.shape
    heads = dt_bias.shape[0]
    width = x_weight.shape[1]
    depth = tokens.shape[1]
    span = tokens.shape[0] // sessions_here
    halves = 2
    rows = tokens.shape[0] // (model_shards * halves)
    capacity = max(2, (sessions_here + shard_count - 1) // shard_count)
    slot_count = shard_count * capacity
    row_shape = (state_width // 128, 128)

    def exchange(value, distance):
        pairs = [(j, j ^ distance) for j in range(model_shards)]
        return lax.ppermute(value, "mp", pairs)

    def trade(value):
        return lax.all_to_all(
            value.reshape((shard_count, capacity) + row_shape),
            "dp",
            split_axis=0,
            concat_axis=0,
            tiled=True,
        ).reshape((slot_count,) + row_shape)

    replicas = lax.axis_size("groups") * shard_count
    replica = lax.axis_index("groups") * shard_count + shard_index
    share = width // replicas
    ow_share = lax.dynamic_slice_in_dim(out_weight, replica * share, share)
    ow_part = exchange(ow_share, 2)
    blocks = tokens.reshape(model_shards // 2, 2, halves, rows, depth)
    sibling = exchange(tokens, 1).reshape(blocks.shape)

    local = jnp.arange(sessions_here, dtype=jnp.int32)
    store_rows = shard_index * sessions_here + local
    everyone = jnp.arange(home_rows.shape[0], dtype=jnp.int32)
    owner = jnp.sum(
        jnp.where(home_rows[None, :] == store_rows[:, None], everyone[None, :], 0), axis=1
    )
    server = owner // sessions_here
    row_slot = server * capacity + rank_within(server, local)
    wanted_slots = jnp.arange(slot_count, dtype=jnp.int32)
    source = jnp.sum(
        jnp.where(row_slot[None, :] == wanted_slots[:, None], local[None, :], 0), axis=1
    )
    swap_row = np.arange(sessions_here * 16)
    swap = jnp.asarray(
        (swap_row % 16 * sessions_here + swap_row // 16)[:, None] == swap_row[None, :], BF
    )
    first = after(blocks, ow_share)[:, :, 0]
    packed = pack_states(after(source, first), store_states, swap, slot_count)
    second = after(blocks, packed)[:, :, 1]
    across = [exchange(first, 2), exchange(second, 2)]
    inbound = trade(packed)
    wanted = lax.dynamic_slice_in_dim(home_rows, shard_index * sessions_here, sessions_here)
    home_shard = wanted // sessions_here
    session_slot = home_shard * capacity + rank_within(home_shard, wanted % sessions_here)
    meta = jnp.concatenate([me.reshape(1).astype(jnp.int32), session_slot, event_counts])

    new_column = np.arange(width)
    old_column = (
        new_column // 256 * 256
        + new_column // 32 % 4 * 64
        + new_column % 32 * 2
        + new_column // 128 % 2
    )
    turn = jnp.asarray(old_column[None, :] == np.arange(width)[:, None], BF)
    x_weight, z_weight, bc_weight, across[0], ow_part = lax.optimization_barrier(
        (x_weight, z_weight, bc_weight, across[0], ow_part)
    )
    xw = jnp.dot(x_weight, turn, preferred_element_type=F32).astype(BF)
    zw = jnp.dot(z_weight, turn, preferred_element_type=F32).astype(BF)
    order = turn[:256, :256]
    bw = jnp.concatenate(
        [bc_weight, dt_weight, jnp.zeros((bc_weight.shape[0], 128 - heads), BF)], axis=1
    )
    gain = norm_gain.reshape(heads // 4, 4, 32, 2).transpose(0, 3, 1, 2).reshape(1, width)
    small = jnp.stack([dt_bias, decay_rate], axis=1)

    ow_part = after(ow_part, inbound)
    ow_across = lax.all_gather(ow_part, ("groups", "dp"), axis=0, tiled=True)
    ow_sibling = exchange(out_weight, 1)

    outgoing = None
    received = []
    done = []
    for h in range(halves):
        arrived = across[h]
        start = meta
        if h:
            start = after(meta, done[-1], ow_sibling)
            arrived = after(arrived, done[-1])
        pieces = (blocks, sibling, arrived, exchange(arrived, 1))
        *parts, outgoing = layer_call(
            h, start, pieces, (bw, xw, zw), (small, gain, order), inbound, span, outgoing
        )
        done.append(parts[0])
        received.append([parts[0]] + [exchange(parts[d], d) for d in range(1, 4)])
    returned = trade(outgoing)
    ow_across = after(ow_across, done[-1])
    ow_far = exchange(ow_across, 1)
    ow = (out_weight, ow_sibling, ow_across, ow_far)
    out_tokens = None
    for h in range(halves):
        normed = list(received[h])
        if h == 0:
            normed[0] = after(normed[0], done[-1])
        out_tokens = out_call(h, halves, normed, ow, out_tokens)
    returned, out_tokens = lax.optimization_barrier((returned, out_tokens))
    new_store = gather_states(row_slot, returned, swap)
    return (out_tokens, new_store)


def solution(mesh):
    return jax.shard_map(
        body,
        mesh=mesh,
        in_specs=(
            P(("groups", "dp"), "mp"),
            P(None, "mp"),
            P(None, "mp"),
            P(None, "mp"),
            P(None, "mp"),
            P("mp"),
            P("mp"),
            P("mp"),
            P("mp", None),
            P(("groups", "dp"), "mp"),
            P("groups"),
            P(("groups", "dp")),
        ),
        out_specs=(P(("groups", "dp", "mp"), None), P(("groups", "dp"), "mp")),
        check_vma=False,
    )
```

```python
import jax
import jax.numpy as jnp
import numpy as np
from jax import lax
from jax.experimental import pallas as pl
from jax.experimental.pallas import tpu as pltpu
from jax.sharding import PartitionSpec as P

BF = jnp.bfloat16
F32 = jnp.float32
ANY = pl.BlockSpec(memory_space=pl.ANY)
VMEM = pl.BlockSpec(memory_space=pltpu.VMEM)
SMEM = pl.BlockSpec(memory_space=pltpu.SMEM)
NT = (((1,), (1,)), ((), ()))
VMEM_LIMIT = 58 * 2**20


def rank_within(keys, order):
    earlier = (keys[None, :] == keys[:, None]) & (order[None, :] < order[:, None])
    return jnp.sum(earlier.astype(jnp.int32), axis=1)


def pack_states(source, store, swap, slots):
    sessions, width = store.shape
    lines = width // 128

    def kernel(source, store, swap, out, held):
        for part in range(4):
            base = part * 16 * 128
            stacked = jnp.concatenate(
                [store[:, base + j * 128 : base + (j + 1) * 128] for j in range(16)], axis=0
            )
            turned = jnp.dot(swap[...], stacked, preferred_element_type=F32).astype(BF)
            for r in range(sessions):
                held[r, part * 16 : (part + 1) * 16, :] = turned[r * 16 : (r + 1) * 16]
        for n in range(slots):
            out[n] = held[source[n]]

    return pl.pallas_call(
        kernel,
        grid=(lines // 64,),
        out_shape=jax.ShapeDtypeStruct((slots, lines, 128), BF),
        in_specs=[
            SMEM,
            pl.BlockSpec((sessions, 64 * 128), lambda j: (0, j)),
            pl.BlockSpec(swap.shape, lambda j: (0, 0)),
        ],
        out_specs=pl.BlockSpec((slots, 64, 128), lambda j: (0, j, 0)),
        scratch_shapes=[pltpu.VMEM((sessions, 64, 128), BF)],
        compiler_params=pltpu.CompilerParams(vmem_limit_bytes=VMEM_LIMIT),
        cost_estimate=pl.CostEstimate(
            flops=1, bytes_accessed=1, transcendentals=0
        ),
        name="pack_states",
    )(source, store, swap)


def gather_states(index, returned, swap):
    sessions = index.shape[0]
    slots, lines, lanes = returned.shape

    def kernel(index, returned, swap, out):
        for part in range(4):
            rows = slice(part * 16, (part + 1) * 16)
            stacked = jnp.concatenate(
                [returned[index[r], rows, :] for r in range(sessions)], axis=0
            )
            turned = lax.dot_general(
                swap[...], stacked, (((0,), (0,)), ((), ())), preferred_element_type=F32
            ).astype(BF)
            for j in range(16):
                column = (part * 16 + j) * 128
                out[:, column : column + 128] = turned[j * sessions : (j + 1) * sessions]

    return pl.pallas_call(
        kernel,
        grid=(lines // 64,),
        out_shape=jax.ShapeDtypeStruct((sessions, lines * lanes), BF),
        in_specs=[
            SMEM,
            pl.BlockSpec((slots, 64, lanes), lambda j: (0, j, 0)),
            pl.BlockSpec(swap.shape, lambda j: (0, 0)),
        ],
        out_specs=pl.BlockSpec((sessions, 64 * lanes), lambda j: (0, j)),
        compiler_params=pltpu.CompilerParams(vmem_limit_bytes=VMEM_LIMIT),
        cost_estimate=pl.CostEstimate(flops=1, bytes_accessed=1, transcendentals=0),
        name="gather_states",
    )(index, returned, swap)


def project(me, pieces, weight, columns):
    depth = pieces[0].shape[1]
    total = None
    for k in range(4):
        first = pl.multiple_of((me ^ k) * depth, depth)
        part = jnp.dot(
            pieces[k][...], weight[pl.ds(first, depth), columns], preferred_element_type=F32
        )
        total = part if total is None else total + part
    return total


def layer_kernel(
    heads, span, pairs, half, meta, own, sibling, across, far, bw, xw, zw, small, gain, order, s0,
    s1, s2, s3,
    *refs
):
    n0, n1, n2, n3, outgoing, xs, zs, fresh, sems = refs[-9:]
    normed_out = (n0, n1, n2, n3)
    me = meta[0]
    step = pl.program_id(0)
    count = 2 * pairs
    rows_all = count * span
    depth = across.shape[-1]
    pieces = [piece[...].reshape(rows_all, depth) for piece in (own, sibling, across, far)]
    quads = heads // 4
    states = (s0, s1, s2, s3)

    def session_of(at, n):
        return ((((me // 2) ^ 1 ^ at) * 2 + n // pairs) * 2 + half) * pairs + n % pairs

    bcs = project(me, pieces, bw, slice(None))
    for quad in range(quads):
        columns = slice(quad * 256, quad * 256 + 256)
        xs[:, columns] = project(me, pieces, xw, columns).astype(BF)
        zs[:, columns] = project(me, pieces, zw, columns).astype(BF)

    lane = lax.broadcasted_iota(jnp.int32, (span, 128), 1)
    low = lane < 64
    lane8 = lax.broadcasted_iota(jnp.int32, (heads, span), 1)
    lane_all = lax.broadcasted_iota(jnp.int32, (heads * count, span), 1)
    raw = jnp.concatenate(
        [
            jnp.transpose(bcs[n * span : (n + 1) * span, 128:256])[:heads] + small[:, 0:1]
            for n in range(count)
        ],
        axis=0,
    )
    counts_at = 1 + meta.shape[0] // 2
    alive = jnp.concatenate(
        [(lane8 < meta[counts_at + session_of(step, n)]).astype(F32) for n in range(count)],
        axis=0,
    )
    steps = (jnp.maximum(raw, 0.0) + jnp.log1p(jnp.exp(-jnp.abs(raw)))) * alive
    totals = steps * jnp.concatenate([small[:, 1:2]] * count, axis=0)
    shift = 1
    while shift < span:
        totals = totals + jnp.where(lane_all >= shift, pltpu.roll(totals, shift, 1), 0.0)
        shift *= 2
    lasts = totals[:, span - 1 : span]
    weight_rows = jnp.exp(jnp.minimum(totals - lasts, 0.0)) * steps
    kept = jnp.exp(-lasts)

    cum = jnp.transpose(
        jnp.concatenate([totals, jnp.zeros((128 - heads * count, span), F32)], axis=0)
    )
    row = lax.broadcasted_iota(jnp.int32, (span, 128), 0)
    causal = row >= lane
    head_masks = []
    for k in range(4):
        mask = (lane // 32 == k).astype(F32).astype(BF)
        head_masks.append(jnp.concatenate([mask, mask], axis=1))

    for n in range(count):
        rows = slice(n * span, (n + 1) * span)
        length = meta[counts_at + session_of(step, n)]
        bc = bcs[rows, 0:128]
        turned = pltpu.roll(bc, 64, 1)
        b_low = jnp.where(low, bc, 0.0).astype(BF)
        b_high = jnp.where(low, 0.0, turned).astype(BF)
        c_low = jnp.where(low, turned, 0.0).astype(BF)
        c_high = jnp.where(low, 0.0, bc).astype(BF)
        b_both = jnp.concatenate([b_low, b_high], axis=0)
        scores = lax.dot_general(c_low, b_low, NT, preferred_element_type=F32)
        scores = jnp.where(causal, scores, 0.0)
        carried = lax.dot_general(
            jnp.concatenate([c_low, c_high], axis=0),
            states[n][...],
            NT,
            preferred_element_type=F32,
        )
        gated = []
        squares = None
        for quad in range(quads):
            columns = slice(quad * 256, quad * 256 + 256)
            part = slice(quad * 128, quad * 128 + 128)
            first_head = n * heads + quad * 4
            x = xs[rows, columns]
            mixes = []
            spread = None
            for k in range(4):
                head = first_head + k
                level = jnp.broadcast_to(cum[:, head : head + 1], (span, 128))
                gap = jnp.minimum(totals[head : head + 1, :] - level, 0.0)
                mixes.append((jnp.exp(gap) * steps[head : head + 1, :] * scores).astype(BF))
                spread = level if spread is None else jnp.where(lane >= 32 * k, level, spread)
            diagonal = jnp.dot(
                jnp.concatenate(mixes, axis=1),
                jnp.concatenate([x * head_masks[k] for k in range(4)], axis=0),
                preferred_element_type=F32,
            )
            fade = jnp.exp(-spread)
            before = jnp.concatenate(
                [carried[:span, part] * fade, carried[span:, part] * fade], axis=1
            )
            gate = zs[rows, columns].astype(F32)
            value = (diagonal + before) * (gate * (0.5 + 0.5 * jnp.tanh(0.5 * gate)))
            gated.append(value)
            own_squares = jnp.sum(value * value, axis=1, keepdims=True)
            squares = own_squares if squares is None else squares + own_squares
            scale = jnp.concatenate(
                [
                    jnp.broadcast_to(
                        weight_rows[first_head + k : first_head + k + 1, :], (32, span)
                    )
                    for k in range(4)
                ],
                axis=0,
            )
            xf = x.astype(F32)
            even = (jnp.transpose(xf[:, :128]) * scale).astype(BF)
            odd = (jnp.transpose(xf[:, 128:]) * scale).astype(BF)
            added = jnp.dot(
                jnp.concatenate([even, odd], axis=1), b_both, preferred_element_type=F32
            )
            keep = jnp.concatenate(
                [
                    jnp.broadcast_to(kept[first_head + k : first_head + k + 1, :], (32, 128))
                    for k in range(4)
                ],
                axis=0,
            )
            fresh[step * count + n, part, :] = (
                keep * states[n][part, :].astype(F32) + added
            ).astype(BF)
        inverse = lax.rsqrt(squares * (1.0 / (heads * 64)) + 1e-05)
        inverse = jnp.where(row[:, :1] < length, inverse, 0.0)
        for quad in range(quads):
            columns = slice(quad * 256, quad * 256 + 256)
            normed = (gated[quad] * inverse * gain[:, columns]).astype(BF)
            zs[rows, columns] = lax.dot_general(
                normed, order[...], NT, preferred_element_type=F32
            ).astype(BF)

    def sending(at, n):
        number = at * count + n
        return pltpu.make_async_copy(
            fresh.at[number], outgoing.at[meta[1 + session_of(at, n)]], sems.at[number]
        )

    for n in range(count):
        sending(step, n).start()

    for at in range(2):

        @pl.when(step == at)
        def _():
            for near in range(2):
                first = pl.multiple_of((near ^ (me % 2)) * (pairs * span), pairs * span)
                normed_out[2 * (1 - at) + near][...] = zs[pl.ds(first, pairs * span), :]

    @pl.when(step == 1)
    def _():
        for at in range(2):
            for n in range(count):
                sending(at, n).wait()


def whole(array):
    return pl.BlockSpec(array.shape, lambda i, meta: (0,) * array.ndim)


def layer_call(half, meta, pieces, weights, smalls, inbound, span, earlier):
    rows, depth = pieces[2].shape[-2:]
    pairs = rows // span
    count = 2 * pairs
    heads = smalls[0].shape[0]
    width = weights[1].shape[1]

    def near(i, meta):
        return ((meta[0] // 2) ^ 1 ^ i, 0, half, 0, 0)

    def arrived(i, meta):
        return ((meta[0] // 2) ^ 1 ^ i, 0, 0, 0)

    def slot_of(n):
        def index(i, meta):
            target = ((meta[0] // 2) ^ 1 ^ i) * 2 + n // pairs
            return (meta[1 + (target * 2 + half) * pairs + n % pairs], 0, 0)

        return index

    operands = [meta, *pieces, *weights, *smalls] + [inbound] * count
    aliases = {}
    extra = []
    if earlier is not None:
        aliases = {len(operands): 4}
        operands.append(earlier)
        extra = [ANY]
    return pl.pallas_call(
        lambda *refs: layer_kernel(heads, span, pairs, half, *refs),
        out_shape=[jax.ShapeDtypeStruct((rows, width), BF)] * 4
        + [jax.ShapeDtypeStruct(inbound.shape, BF)],
        grid_spec=pltpu.PrefetchScalarGridSpec(
            num_scalar_prefetch=1,
            grid=(2,),
            in_specs=[pl.BlockSpec((None, 2, None, rows, depth), near)] * 2
            + [pl.BlockSpec((None, 2, rows, depth), arrived)] * 2
            + [whole(weight) for weight in weights]
            + [whole(small) for small in smalls]
            + [pl.BlockSpec((None,) + inbound.shape[1:], slot_of(n)) for n in range(count)]
            + extra,
            out_specs=[pl.BlockSpec((rows, width), lambda i, meta: (0, 0))] * 4 + [ANY],
            scratch_shapes=[
                pltpu.VMEM((count * span, width), BF),
                pltpu.VMEM((count * span, width), BF),
                pltpu.VMEM((2 * count,) + inbound.shape[1:], BF),
                pltpu.SemaphoreType.DMA((2 * count,)),
            ],
        ),
        input_output_aliases=aliases,
        compiler_params=pltpu.CompilerParams(vmem_limit_bytes=VMEM_LIMIT),
        cost_estimate=pl.CostEstimate(
            flops=1, bytes_accessed=1, transcendentals=0
        ),
        name="layer",
    )(*operands)


def out_call(half, halves, normed, weights, earlier):
    rows, depth = normed[0].shape
    columns = weights[0].shape[1]
    block = 512

    def kernel(*refs):
        out = refs[-1]
        total = None
        for d in range(4):
            part = jnp.dot(refs[d][...], refs[4 + d][...], preferred_element_type=F32)
            total = part if total is None else total + part
        out[...] = total.astype(BF)

    operands = [*normed, *weights]
    extra = []
    aliases = {}
    if earlier is not None:
        aliases = {len(operands): 0}
        operands.append(earlier)
        extra = [ANY]
    return pl.pallas_call(
        kernel,
        grid=(columns // block,),
        out_shape=jax.ShapeDtypeStruct((halves * rows, columns), BF),
        in_specs=[pl.BlockSpec((rows, depth), lambda j: (0, 0))] * 4
        + [pl.BlockSpec((depth, block), lambda j: (0, j))] * 4
        + extra,
        out_specs=pl.BlockSpec((rows, block), lambda j: (half, j)),
        input_output_aliases=aliases,
        compiler_params=pltpu.CompilerParams(vmem_limit_bytes=VMEM_LIMIT),
        cost_estimate=pl.CostEstimate(
            flops=1, bytes_accessed=1, transcendentals=0
        ),
        name="project_out",
    )(*operands)


def after(value, *others):
    return lax.optimization_barrier((value,) + others)[0]


def body(
    tokens,
    x_weight,
    z_weight,
    bc_weight,
    dt_weight,
    dt_bias,
    decay_rate,
    norm_gain,
    out_weight,
    store_states,
    home_rows,
    event_counts,
):
    shard_count = lax.axis_size("dp")
    model_shards = lax.axis_size("mp")
    shard_index = lax.axis_index("dp")
    me = lax.axis_index("mp")
    sessions_here, state_width = store_states.shape
    heads = dt_bias.shape[0]
    width = x_weight.shape[1]
    depth = tokens.shape[1]
    span = tokens.shape[0] // sessions_here
    halves = 2
    rows = tokens.shape[0] // (model_shards * halves)
    capacity = max(2, (sessions_here + shard_count - 1) // shard_count)
    slot_count = shard_count * capacity
    row_shape = (state_width // 128, 128)

    def exchange(value, distance):
        pairs = [(j, j ^ distance) for j in range(model_shards)]
        return lax.ppermute(value, "mp", pairs)

    def trade(value):
        return lax.all_to_all(
            value.reshape((shard_count, capacity) + row_shape),
            "dp",
            split_axis=0,
            concat_axis=0,
            tiled=True,
        ).reshape((slot_count,) + row_shape)

    replicas = lax.axis_size("groups") * shard_count
    replica = lax.axis_index("groups") * shard_count + shard_index
    share = width // replicas
    ow_share = lax.dynamic_slice_in_dim(out_weight, replica * share, share)
    ow_part = exchange(ow_share, 2)
    blocks = tokens.reshape(model_shards // 2, 2, halves, rows, depth)
    sibling = exchange(tokens, 1).reshape(blocks.shape)

    local = jnp.arange(sessions_here, dtype=jnp.int32)
    store_rows = shard_index * sessions_here + local
    everyone = jnp.arange(home_rows.shape[0], dtype=jnp.int32)
    owner = jnp.sum(
        jnp.where(home_rows[None, :] == store_rows[:, None], everyone[None, :], 0), axis=1
    )
    server = owner // sessions_here
    row_slot = server * capacity + rank_within(server, local)
    wanted_slots = jnp.arange(slot_count, dtype=jnp.int32)
    source = jnp.sum(
        jnp.where(row_slot[None, :] == wanted_slots[:, None], local[None, :], 0), axis=1
    )
    swap_row = np.arange(sessions_here * 16)
    swap = jnp.asarray(
        (swap_row % 16 * sessions_here + swap_row // 16)[:, None] == swap_row[None, :], BF
    )
    halved = after(blocks, ow_share)
    first, second = halved[:, :, 0], halved[:, :, 1]
    packed = pack_states(after(source, first, second), store_states, swap, slot_count)
    across = [exchange(first, 2), exchange(second, 2)]
    packed, ow_part = lax.optimization_barrier((packed, ow_part))
    inbound = trade(packed)
    wanted = lax.dynamic_slice_in_dim(home_rows, shard_index * sessions_here, sessions_here)
    home_shard = wanted // sessions_here
    session_slot = home_shard * capacity + rank_within(home_shard, wanted % sessions_here)
    meta = jnp.concatenate([me.reshape(1).astype(jnp.int32), session_slot, event_counts])

    new_column = np.arange(width)
    old_column = (
        new_column // 256 * 256
        + new_column // 32 % 4 * 64
        + new_column % 32 * 2
        + new_column // 128 % 2
    )
    turn = jnp.asarray(old_column[None, :] == np.arange(width)[:, None], BF)
    x_weight, z_weight, bc_weight, packed = lax.optimization_barrier(
        (x_weight, z_weight, bc_weight, packed)
    )
    xw = jnp.dot(x_weight, turn, preferred_element_type=F32).astype(BF)
    zw = jnp.dot(z_weight, turn, preferred_element_type=F32).astype(BF)
    order = turn[:256, :256]
    bw = jnp.concatenate(
        [bc_weight, dt_weight, jnp.zeros((bc_weight.shape[0], 128 - heads), BF)], axis=1
    )
    gain = norm_gain.reshape(heads // 4, 4, 32, 2).transpose(0, 3, 1, 2).reshape(1, width)
    small = jnp.stack([dt_bias, decay_rate], axis=1)

    across[0], xw, zw, bw = lax.optimization_barrier((across[0], xw, zw, bw))
    ow_part, across[0] = lax.optimization_barrier((ow_part, across[0]))
    ow_across = lax.all_gather(ow_part, ("groups", "dp"), axis=0, tiled=True)
    ow_sibling = exchange(out_weight, 1)

    outgoing = None
    received = []
    done = []
    for h in range(halves):
        arrived = across[h]
        start = meta
        if h:
            start = after(meta, done[-1], ow_sibling)
            arrived = after(arrived, done[-1])
        pieces = (blocks, sibling, arrived, exchange(arrived, 1))
        *parts, outgoing = layer_call(
            h, start, pieces, (bw, xw, zw), (small, gain, order), inbound, span, outgoing
        )
        done.append(parts[0])
        received.append([parts[0]] + [exchange(parts[d], d) for d in range(1, 4)])
    returned = trade(outgoing)
    ow_across = after(ow_across, done[-1])
    ow_far = exchange(ow_across, 1)
    ow = (out_weight, ow_sibling, ow_across, ow_far)
    out_tokens = None
    for h in range(halves):
        normed = list(received[h])
        if h == 0:
            normed[0] = after(normed[0], done[-1])
        out_tokens = out_call(h, halves, normed, ow, out_tokens)
    returned, out_tokens = lax.optimization_barrier((returned, out_tokens))
    new_store = gather_states(row_slot, returned, swap)
    return (out_tokens, new_store)


def solution(mesh):
    return jax.shard_map(
        body,
        mesh=mesh,
        in_specs=(
            P(("groups", "dp"), "mp"),
            P(None, "mp"),
            P(None, "mp"),
            P(None, "mp"),
            P(None, "mp"),
            P("mp"),
            P("mp"),
            P("mp"),
            P("mp", None),
            P(("groups", "dp"), "mp"),
            P("groups"),
            P(("groups", "dp")),
        ),
        out_specs=(P(("groups", "dp", "mp"), None), P(("groups", "dp"), "mp")),
        check_vma=False,
    )
```

```python
import jax
import jax.numpy as jnp
import numpy as np
from jax import lax
from jax.experimental import pallas as pl
from jax.experimental.pallas import tpu as pltpu
from jax.sharding import PartitionSpec as P

BF = jnp.bfloat16
F32 = jnp.float32
ANY = pl.BlockSpec(memory_space=pl.ANY)
VMEM = pl.BlockSpec(memory_space=pltpu.VMEM)
SMEM = pl.BlockSpec(memory_space=pltpu.SMEM)
NT = (((1,), (1,)), ((), ()))
VMEM_LIMIT = 58 * 2**20


def rank_within(keys, order):
    earlier = (keys[None, :] == keys[:, None]) & (order[None, :] < order[:, None])
    return jnp.sum(earlier.astype(jnp.int32), axis=1)


def pack_states(source, store, swap, slots):
    sessions, width = store.shape
    lines = width // 128

    def kernel(source, store, swap, out, held):
        for part in range(4):
            base = part * 16 * 128
            stacked = jnp.concatenate(
                [store[:, base + j * 128 : base + (j + 1) * 128] for j in range(16)], axis=0
            )
            turned = jnp.dot(swap[...], stacked, preferred_element_type=F32).astype(BF)
            for r in range(sessions):
                held[r, part * 16 : (part + 1) * 16, :] = turned[r * 16 : (r + 1) * 16]
        for n in range(slots):
            out[n] = held[source[n]]

    return pl.pallas_call(
        kernel,
        grid=(lines // 64,),
        out_shape=jax.ShapeDtypeStruct((slots, lines, 128), BF),
        in_specs=[
            SMEM,
            pl.BlockSpec((sessions, 64 * 128), lambda j: (0, j)),
            pl.BlockSpec(swap.shape, lambda j: (0, 0)),
        ],
        out_specs=pl.BlockSpec((slots, 64, 128), lambda j: (0, j, 0)),
        scratch_shapes=[pltpu.VMEM((sessions, 64, 128), BF)],
        compiler_params=pltpu.CompilerParams(vmem_limit_bytes=VMEM_LIMIT),
        cost_estimate=pl.CostEstimate(
            flops=1, bytes_accessed=1, transcendentals=0
        ),
        name="pack_states",
    )(source, store, swap)


def gather_states(index, returned, swap):
    sessions = index.shape[0]
    slots, lines, lanes = returned.shape

    def kernel(index, returned, swap, out):
        for part in range(4):
            rows = slice(part * 16, (part + 1) * 16)
            stacked = jnp.concatenate(
                [returned[index[r], rows, :] for r in range(sessions)], axis=0
            )
            turned = lax.dot_general(
                swap[...], stacked, (((0,), (0,)), ((), ())), preferred_element_type=F32
            ).astype(BF)
            for j in range(16):
                column = (part * 16 + j) * 128
                out[:, column : column + 128] = turned[j * sessions : (j + 1) * sessions]

    return pl.pallas_call(
        kernel,
        grid=(lines // 64,),
        out_shape=jax.ShapeDtypeStruct((sessions, lines * lanes), BF),
        in_specs=[
            SMEM,
            pl.BlockSpec((slots, 64, lanes), lambda j: (0, j, 0)),
            pl.BlockSpec(swap.shape, lambda j: (0, 0)),
        ],
        out_specs=pl.BlockSpec((sessions, 64 * lanes), lambda j: (0, j)),
        compiler_params=pltpu.CompilerParams(vmem_limit_bytes=VMEM_LIMIT),
        cost_estimate=pl.CostEstimate(flops=1, bytes_accessed=1, transcendentals=0),
        name="gather_states",
    )(index, returned, swap)


def project(me, pieces, weight, columns):
    depth = pieces[0].shape[1]
    total = None
    for k in range(4):
        first = pl.multiple_of((me ^ k) * depth, depth)
        part = jnp.dot(
            pieces[k][...], weight[pl.ds(first, depth), columns], preferred_element_type=F32
        )
        total = part if total is None else total + part
    return total


def layer_kernel(
    heads, span, pairs, half, meta, own, sibling, across, far, bw, xw, zw, small, gain, order, s0,
    s1, s2, s3,
    *refs
):
    n0, n1, n2, n3, outgoing, xs, zs, fresh, sems = refs[-9:]
    normed_out = (n0, n1, n2, n3)
    me = meta[0]
    step = pl.program_id(0)
    count = 2 * pairs
    rows_all = count * span
    depth = across.shape[-1]
    pieces = [piece[...].reshape(rows_all, depth) for piece in (own, sibling, across, far)]
    quads = heads // 4
    states = (s0, s1, s2, s3)

    def session_of(at, n):
        return ((((me // 2) ^ 1 ^ at) * 2 + n // pairs) * 2 + half) * pairs + n % pairs

    bcs = project(me, pieces, bw, slice(None))
    for quad in range(quads):
        columns = slice(quad * 256, quad * 256 + 256)
        xs[:, columns] = project(me, pieces, xw, columns).astype(BF)
        zs[:, columns] = project(me, pieces, zw, columns).astype(BF)

    lane = lax.broadcasted_iota(jnp.int32, (span, 128), 1)
    low = lane < 64
    lane8 = lax.broadcasted_iota(jnp.int32, (heads, span), 1)
    lane_all = lax.broadcasted_iota(jnp.int32, (heads * count, span), 1)
    raw = jnp.concatenate(
        [
            jnp.transpose(bcs[n * span : (n + 1) * span, 128:256])[:heads] + small[:, 0:1]
            for n in range(count)
        ],
        axis=0,
    )
    counts_at = 1 + meta.shape[0] // 2
    alive = jnp.concatenate(
        [(lane8 < meta[counts_at + session_of(step, n)]).astype(F32) for n in range(count)],
        axis=0,
    )
    steps = (jnp.maximum(raw, 0.0) + jnp.log1p(jnp.exp(-jnp.abs(raw)))) * alive
    totals = steps * jnp.concatenate([small[:, 1:2]] * count, axis=0)
    shift = 1
    while shift < span:
        totals = totals + jnp.where(lane_all >= shift, pltpu.roll(totals, shift, 1), 0.0)
        shift *= 2
    lasts = totals[:, span - 1 : span]
    weight_rows = jnp.exp(jnp.minimum(totals - lasts, 0.0)) * steps
    kept = jnp.exp(-lasts)

    cum = jnp.transpose(
        jnp.concatenate([totals, jnp.zeros((128 - heads * count, span), F32)], axis=0)
    )
    row = lax.broadcasted_iota(jnp.int32, (span, 128), 0)
    causal = row >= lane
    head_masks = []
    for k in range(4):
        mask = (lane // 32 == k).astype(F32).astype(BF)
        head_masks.append(jnp.concatenate([mask, mask], axis=1))

    for n in range(count):
        rows = slice(n * span, (n + 1) * span)
        length = meta[counts_at + session_of(step, n)]
        bc = bcs[rows, 0:128]
        turned = pltpu.roll(bc, 64, 1)
        b_low = jnp.where(low, bc, 0.0).astype(BF)
        b_high = jnp.where(low, 0.0, turned).astype(BF)
        c_low = jnp.where(low, turned, 0.0).astype(BF)
        c_high = jnp.where(low, 0.0, bc).astype(BF)
        b_both = jnp.concatenate([b_low, b_high], axis=0)
        scores = lax.dot_general(c_low, b_low, NT, preferred_element_type=F32)
        scores = jnp.where(causal, scores, 0.0)
        carried = lax.dot_general(
            jnp.concatenate([c_low, c_high], axis=0),
            states[n][...],
            NT,
            preferred_element_type=F32,
        )
        gated = []
        squares = None
        for quad in range(quads):
            columns = slice(quad * 256, quad * 256 + 256)
            part = slice(quad * 128, quad * 128 + 128)
            first_head = n * heads + quad * 4
            x = xs[rows, columns]
            mixes = []
            spread = None
            for k in range(4):
                head = first_head + k
                level = jnp.broadcast_to(cum[:, head : head + 1], (span, 128))
                gap = jnp.minimum(totals[head : head + 1, :] - level, 0.0)
                mixes.append((jnp.exp(gap) * steps[head : head + 1, :] * scores).astype(BF))
                spread = level if spread is None else jnp.where(lane >= 32 * k, level, spread)
            diagonal = jnp.dot(
                jnp.concatenate(mixes, axis=1),
                jnp.concatenate([x * head_masks[k] for k in range(4)], axis=0),
                preferred_element_type=F32,
            )
            fade = jnp.exp(-spread)
            before = jnp.concatenate(
                [carried[:span, part] * fade, carried[span:, part] * fade], axis=1
            )
            gate = zs[rows, columns].astype(F32)
            value = (diagonal + before) * (gate * (0.5 + 0.5 * jnp.tanh(0.5 * gate)))
            gated.append(value)
            own_squares = jnp.sum(value * value, axis=1, keepdims=True)
            squares = own_squares if squares is None else squares + own_squares
            scale = jnp.concatenate(
                [
                    jnp.broadcast_to(
                        weight_rows[first_head + k : first_head + k + 1, :], (32, span)
                    )
                    for k in range(4)
                ],
                axis=0,
            )
            xf = x.astype(F32)
            even = (jnp.transpose(xf[:, :128]) * scale).astype(BF)
            odd = (jnp.transpose(xf[:, 128:]) * scale).astype(BF)
            added = jnp.dot(
                jnp.concatenate([even, odd], axis=1), b_both, preferred_element_type=F32
            )
            keep = jnp.concatenate(
                [
                    jnp.broadcast_to(kept[first_head + k : first_head + k + 1, :], (32, 128))
                    for k in range(4)
                ],
                axis=0,
            )
            fresh[step * count + n, part, :] = (
                keep * states[n][part, :].astype(F32) + added
            ).astype(BF)
        inverse = lax.rsqrt(squares * (1.0 / (heads * 64)) + 1e-05)
        inverse = jnp.where(row[:, :1] < length, inverse, 0.0)
        for quad in range(quads):
            columns = slice(quad * 256, quad * 256 + 256)
            normed = (gated[quad] * inverse * gain[:, columns]).astype(BF)
            zs[rows, columns] = lax.dot_general(
                normed, order[...], NT, preferred_element_type=F32
            ).astype(BF)

    def sending(at, n):
        number = at * count + n
        return pltpu.make_async_copy(
            fresh.at[number], outgoing.at[meta[1 + session_of(at, n)]], sems.at[number]
        )

    for n in range(count):
        sending(step, n).start()

    for at in range(2):

        @pl.when(step == at)
        def _():
            for near in range(2):
                first = pl.multiple_of((near ^ (me % 2)) * (pairs * span), pairs * span)
                normed_out[2 * (1 - at) + near][...] = zs[pl.ds(first, pairs * span), :]

    @pl.when(step == 1)
    def _():
        for at in range(2):
            for n in range(count):
                sending(at, n).wait()


def whole(array):
    return pl.BlockSpec(array.shape, lambda i, meta: (0,) * array.ndim)


def layer_call(half, meta, pieces, weights, smalls, inbound, span, earlier):
    rows, depth = pieces[2].shape[-2:]
    pairs = rows // span
    count = 2 * pairs
    heads = smalls[0].shape[0]
    width = weights[1].shape[1]

    def near(i, meta):
        return ((meta[0] // 2) ^ 1 ^ i, 0, half, 0, 0)

    def arrived(i, meta):
        return ((meta[0] // 2) ^ 1 ^ i, 0, 0, 0)

    def slot_of(n):
        def index(i, meta):
            target = ((meta[0] // 2) ^ 1 ^ i) * 2 + n // pairs
            return (meta[1 + (target * 2 + half) * pairs + n % pairs], 0, 0)

        return index

    operands = [meta, *pieces, *weights, *smalls] + [inbound] * count
    aliases = {}
    extra = []
    if earlier is not None:
        aliases = {len(operands): 4}
        operands.append(earlier)
        extra = [ANY]
    return pl.pallas_call(
        lambda *refs: layer_kernel(heads, span, pairs, half, *refs),
        out_shape=[jax.ShapeDtypeStruct((rows, width), BF)] * 4
        + [jax.ShapeDtypeStruct(inbound.shape, BF)],
        grid_spec=pltpu.PrefetchScalarGridSpec(
            num_scalar_prefetch=1,
            grid=(2,),
            in_specs=[pl.BlockSpec((None, 2, None, rows, depth), near)] * 2
            + [pl.BlockSpec((None, 2, rows, depth), arrived)] * 2
            + [whole(weight) for weight in weights]
            + [whole(small) for small in smalls]
            + [pl.BlockSpec((None,) + inbound.shape[1:], slot_of(n)) for n in range(count)]
            + extra,
            out_specs=[pl.BlockSpec((rows, width), lambda i, meta: (0, 0))] * 4 + [ANY],
            scratch_shapes=[
                pltpu.VMEM((count * span, width), BF),
                pltpu.VMEM((count * span, width), BF),
                pltpu.VMEM((2 * count,) + inbound.shape[1:], BF),
                pltpu.SemaphoreType.DMA((2 * count,)),
            ],
        ),
        input_output_aliases=aliases,
        compiler_params=pltpu.CompilerParams(vmem_limit_bytes=VMEM_LIMIT),
        cost_estimate=pl.CostEstimate(
            flops=1, bytes_accessed=1, transcendentals=0
        ),
        name="layer",
    )(*operands)


def out_call(half, halves, normed, weights, earlier):
    rows, depth = normed[0].shape
    columns = weights[0].shape[1]
    block = 512

    def kernel(*refs):
        out = refs[-1]
        total = None
        for d in range(4):
            part = jnp.dot(refs[d][...], refs[4 + d][...], preferred_element_type=F32)
            total = part if total is None else total + part
        out[...] = total.astype(BF)

    operands = [*normed, *weights]
    extra = []
    aliases = {}
    if earlier is not None:
        aliases = {len(operands): 0}
        operands.append(earlier)
        extra = [ANY]
    return pl.pallas_call(
        kernel,
        grid=(columns // block,),
        out_shape=jax.ShapeDtypeStruct((halves * rows, columns), BF),
        in_specs=[pl.BlockSpec((rows, depth), lambda j: (0, 0))] * 4
        + [pl.BlockSpec((depth, block), lambda j: (0, j))] * 4
        + extra,
        out_specs=pl.BlockSpec((rows, block), lambda j: (half, j)),
        input_output_aliases=aliases,
        compiler_params=pltpu.CompilerParams(vmem_limit_bytes=VMEM_LIMIT),
        cost_estimate=pl.CostEstimate(
            flops=1, bytes_accessed=1, transcendentals=0
        ),
        name="project_out",
    )(*operands)


def after(value, *others):
    return lax.optimization_barrier((value,) + others)[0]


def body(
    tokens,
    x_weight,
    z_weight,
    bc_weight,
    dt_weight,
    dt_bias,
    decay_rate,
    norm_gain,
    out_weight,
    store_states,
    home_rows,
    event_counts,
):
    shard_count = lax.axis_size("dp")
    model_shards = lax.axis_size("mp")
    shard_index = lax.axis_index("dp")
    me = lax.axis_index("mp")
    sessions_here, state_width = store_states.shape
    heads = dt_bias.shape[0]
    width = x_weight.shape[1]
    depth = tokens.shape[1]
    span = tokens.shape[0] // sessions_here
    halves = 2
    rows = tokens.shape[0] // (model_shards * halves)
    capacity = max(2, (sessions_here + shard_count - 1) // shard_count)
    slot_count = shard_count * capacity
    row_shape = (state_width // 128, 128)

    def exchange(value, distance):
        pairs = [(j, j ^ distance) for j in range(model_shards)]
        return lax.ppermute(value, "mp", pairs)

    def trade(value):
        return lax.all_to_all(
            value.reshape((shard_count, capacity) + row_shape),
            "dp",
            split_axis=0,
            concat_axis=0,
            tiled=True,
        ).reshape((slot_count,) + row_shape)

    replicas = lax.axis_size("groups") * shard_count
    replica = lax.axis_index("groups") * shard_count + shard_index
    share = width // replicas
    ow_share = lax.dynamic_slice_in_dim(out_weight, replica * share, share)
    ow_part = exchange(ow_share, 2)
    blocks = tokens.reshape(model_shards // 2, 2, halves, rows, depth)
    sibling = exchange(tokens, 1).reshape(blocks.shape)

    local = jnp.arange(sessions_here, dtype=jnp.int32)
    store_rows = shard_index * sessions_here + local
    everyone = jnp.arange(home_rows.shape[0], dtype=jnp.int32)
    owner = jnp.sum(
        jnp.where(home_rows[None, :] == store_rows[:, None], everyone[None, :], 0), axis=1
    )
    server = owner // sessions_here
    row_slot = server * capacity + rank_within(server, local)
    wanted_slots = jnp.arange(slot_count, dtype=jnp.int32)
    source = jnp.sum(
        jnp.where(row_slot[None, :] == wanted_slots[:, None], local[None, :], 0), axis=1
    )
    swap_row = np.arange(sessions_here * 16)
    swap = jnp.asarray(
        (swap_row % 16 * sessions_here + swap_row // 16)[:, None] == swap_row[None, :], BF
    )
    halved = after(blocks, ow_share)
    first, second = halved[:, :, 0], halved[:, :, 1]
    packed = pack_states(after(source, first, second), store_states, swap, slot_count)
    across = [exchange(first, 2), exchange(second, 2)]
    packed, ow_part = lax.optimization_barrier((packed, ow_part))
    inbound = trade(packed)
    wanted = lax.dynamic_slice_in_dim(home_rows, shard_index * sessions_here, sessions_here)
    home_shard = wanted // sessions_here
    session_slot = home_shard * capacity + rank_within(home_shard, wanted % sessions_here)
    meta = jnp.concatenate([me.reshape(1).astype(jnp.int32), session_slot, event_counts])

    new_column = np.arange(width)
    old_column = (
        new_column // 256 * 256
        + new_column // 32 % 4 * 64
        + new_column % 32 * 2
        + new_column // 128 % 2
    )
    turn = jnp.asarray(old_column[None, :] == np.arange(width)[:, None], BF)
    bc_weight, inbound = lax.optimization_barrier((bc_weight, inbound))
    x_weight, z_weight, packed = lax.optimization_barrier((x_weight, z_weight, packed))
    xw = jnp.dot(x_weight, turn, preferred_element_type=F32).astype(BF)
    zw = jnp.dot(z_weight, turn, preferred_element_type=F32).astype(BF)
    order = turn[:256, :256]
    bw = jnp.concatenate(
        [bc_weight, dt_weight, jnp.zeros((bc_weight.shape[0], 128 - heads), BF)], axis=1
    )
    gain = norm_gain.reshape(heads // 4, 4, 32, 2).transpose(0, 3, 1, 2).reshape(1, width)
    small = jnp.stack([dt_bias, decay_rate], axis=1)

    across[0], xw, zw, bw, inbound, ow_part = lax.optimization_barrier(
        (across[0], xw, zw, bw, inbound, ow_part)
    )
    ow_across = lax.all_gather(ow_part, ("groups", "dp"), axis=0, tiled=True)
    ow_sibling = exchange(out_weight, 1)

    outgoing = None
    received = []
    done = []
    for h in range(halves):
        arrived = across[h]
        start = meta
        if h:
            start = after(meta, done[-1], ow_sibling)
            arrived = after(arrived, done[-1])
        pieces = (blocks, sibling, arrived, exchange(arrived, 1))
        *parts, outgoing = layer_call(
            h, start, pieces, (bw, xw, zw), (small, gain, order), inbound, span, outgoing
        )
        done.append(parts[0])
        received.append([parts[0]] + [exchange(parts[d], d) for d in range(1, 4)])
    returned = trade(outgoing)
    ow_across = after(ow_across, done[-1])
    ow_far = exchange(ow_across, 1)
    ow = (out_weight, ow_sibling, ow_across, ow_far)
    out_tokens = None
    for h in range(halves):
        normed = list(received[h])
        if h == 0:
            normed[0] = after(normed[0], done[-1])
        out_tokens = out_call(h, halves, normed, ow, out_tokens)
    returned, out_tokens = lax.optimization_barrier((returned, out_tokens))
    new_store = gather_states(row_slot, returned, swap)
    return (out_tokens, new_store)


def solution(mesh):
    return jax.shard_map(
        body,
        mesh=mesh,
        in_specs=(
            P(("groups", "dp"), "mp"),
            P(None, "mp"),
            P(None, "mp"),
            P(None, "mp"),
            P(None, "mp"),
            P("mp"),
            P("mp"),
            P("mp"),
            P("mp", None),
            P(("groups", "dp"), "mp"),
            P("groups"),
            P(("groups", "dp")),
        ),
        out_specs=(P(("groups", "dp", "mp"), None), P(("groups", "dp"), "mp")),
        check_vma=False,
    )
```
